128 devices in a mesh: lat: 16 (over z, x_hi, core), lon: 8 (over y, x_lo).
Axes of the slice: x: 4 (x_hi: 2, x_lo: 2; x = x_hi * 2 + x_lo), y: 4, z: 4, core: 2. Of those that a mesh axis runs over, the one named last changes fastest.
Arguments:
- buffer: bfloat16 [147456, 512], P(('lat', 'lon')), may hold values from -25 to 25
- fetch_owner: int32 [16, 8, 2304, 1], P('lat', 'lon'), may hold values from 0 to 15; in each aligned block of 2304 rows (0 to 2303, 2304 to 4607, ..., all dimensions but the last counted through in order) at most 288 rows name the same one
- fetch_slot: int32 [16, 8, 2304], P('lat', 'lon'), may hold values from 0 to 1151
- norm_gain: float32 [512], replicated, may hold values from 0.1 to 1.9
- qkv_weight: bfloat16 [512, 1536], replicated, may hold values from -8 to 8
- out_weight: bfloat16 [512, 512], replicated, may hold values from -0.25 to 0.25
- out_grad: bfloat16 [192, 384, 4, 512], P('lat', 'lon'), may hold values from -6 to 6
Outputs:
- block_out: bfloat16 [192, 384, 4, 512], P('lat', 'lon')
- grad_states: bfloat16 [192, 384, 4, 512], P('lat', 'lon')
- grad_qkv: float32 [512, 1536], P(('lat', 'lon'))
- grad_outw: float32 [512, 512], P(('lat', 'lon'))
The draws below stay inside these ranges and needn't reach their ends.
Inputs may be any that keep to these rules, and one draw needn't show every extreme that they name: `fetch_owner`: in the 2304 rows of one device at most 288 name the same owner band, and some owner band is named by exactly 288.
All inputs are finite; a program needn't handle non-finite values.
Results may differ from the reference program's by a relative error of at most 0.0091.
Values may be sent and summed in bfloat16 or wider, within the bound.
No kernel may reach another device: no remote copies, remote signals or barrier semaphores. Data moves between devices by JAX's collectives and lax.ppermute only.
A program may use at most 192 MiB of HBM per device.

```python
import math
import jax
import jax.numpy as jnp
import numpy as np
from jax import lax

D = 512
HEADS = 8
LEV = 4
WLAT = 6
WLON = 12
WLEV = 2
LAT_DEV = 12
LON_DEV = 48
BUF_DEV = 1152
SLAT = 3
SLON = 6
TOK_DEV = 2304
CAP = 288
NLAT = 192
NLON = 384
BUF_ROWS = 147456
N_LAT = 16
N_LON = 8


def draw_buffer(key, part):
    key = jax.random.fold_in(key, 11)
    key_base, key_rows, key_cols = jax.random.split(key, 3)
    base = jax.random.truncated_normal(key_base, -4.0, 4.0, (BUF_ROWS, D))
    row_scale = jnp.exp(jax.random.uniform(key_rows, (BUF_ROWS, 1), minval=math.log(0.4), maxval=math.log(2.5)))
    col_scale = jnp.exp(jax.random.uniform(key_cols, (1, D), minval=math.log(0.4), maxval=math.log(2.5)))
    return (base * row_scale * col_scale).astype(jnp.bfloat16)


def draw_qkv_weight(key, part):
    key = jax.random.fold_in(key, 23)
    values = jax.random.truncated_normal(key, -3.0, 3.0, (D, 3 * D)) * D ** (-0.5)
    return values.astype(jnp.bfloat16)


def set_ends(values, rng, low, high):
    dims = values.shape
    spot = [jax.random.randint(jax.random.fold_in(rng, axis), (), 0, dims[axis]) for axis in range(len(dims))]
    values = values.at[tuple(spot)].set(low)
    longest = dims.index(max(dims))
    spot[longest] = (spot[longest] + 1) % dims[longest]
    return values.at[tuple(spot)].set(high)


def levels(own_key, extent, cuts, low, largest):
    level, own = 1.0, jax.random.fold_in(own_key, 6)
    for position, shards_of in cuts:
        draws = jnp.exp(jax.random.uniform(jax.random.fold_in(own, position), (shards_of,), jnp.float32, low / len(cuts), largest / len(cuts)))
        level = level * jnp.repeat(draws, extent[position] // shards_of).reshape([-1 if axis == position else 1 for axis in range(len(extent))])
    return level


def deal_out(own_key, own, number, rows, number_of, top, most, skew):
    sequence = jax.random.permutation(own_key, number_of)
    crowded, usual = load_shares(number_of, rows * top, most, skew, True), load_shares(number_of, rows * top, most, skew, False)
    places = jnp.arange(number_of)

    def named(lengths, turn):
        used = int((lengths > 0).sum())
        fixed = max(1, used // 4)
        passed = fixed + (places - fixed + turn * (used - fixed)) % max(1, number_of - fixed)
        return jnp.zeros((number_of,), jnp.int32).at[sequence[jnp.where(places < fixed, places, passed)]].set(jnp.asarray(lengths, jnp.int32))

    lengths = jnp.where(number % 4 == 0, named(crowded, number // 4), named(usual, number - number // 4 - 1))
    mixed = jax.random.permutation(jax.random.fold_in(own, 3), number_of)
    giver, sink = mixed[0:number_of // 2 * 2:2], mixed[1:number_of // 2 * 2:2]
    margin = jnp.minimum(lengths[giver] - 1, most - lengths[sink]) // 2
    margin = jnp.where((giver == sequence[0]) | (sink == sequence[0]) | (lengths[sink] == 0), 0, jnp.maximum(margin, 0))
    passed = jax.random.randint(jax.random.fold_in(own, 4), (number_of // 2,), 0, 1 << 20) % (margin + 1)
    lengths = lengths.at[giver].add(-passed).at[sink].add(passed)
    members = jnp.searchsorted(jnp.cumsum(lengths), jnp.arange(rows * top), side="right").astype(jnp.int32)
    listing = members.reshape(top, rows).T
    listing = listing[jax.random.permutation(jax.random.fold_in(own, 1), rows)]
    turn = jax.random.randint(jax.random.fold_in(own, 2), (rows, 1), 0, top)
    return jnp.take_along_axis(listing, (jnp.arange(top)[None, :] + turn) % top, axis=1)


def load_shares(number_of, total, limit, slope, full):
    loads = [(1 << 20) // math.isqrt(grade ** slope) + 1 for grade in range(1, number_of + 1)]
    largest = limit if full else min(limit, max(-(-total // number_of), total * loads[0] // sum(loads)))
    least = 1 if total - largest >= number_of - 1 else 0
    counts, surplus = [largest] + [least] * (number_of - 1), total - largest - least * (number_of - 1)
    while surplus > 0:
        movable = [i for i in range(1, number_of) if counts[i] < largest] or [i for i in range(1, number_of) if counts[i] < limit]
        mass, left = sum([loads[i] for i in movable]), surplus
        for i in movable:
            more = min(limit - counts[i], max(1, left * loads[i] // mass), surplus)
            counts[i] = counts[i] + more
            surplus = surplus - more
    return np.array(counts)


def normal_values(own_key, dims, scale, limit, shards=(), held_as=jnp.bfloat16):
    array = scale * jax.random.normal(own_key, dims, jnp.float32)
    if shards:
        array = array * levels(own_key, dims, shards, -0.22, 0.18)
    return jnp.clip(array, -limit, limit).astype(held_as)


def setup_inputs(seed: int = 0) -> dict:
    streams_of = jax.random.split(jax.random.key(seed), 8)
    buffer = draw_buffer(jax.random.fold_in(streams_of[7], 71), 0)
    fetch_owner_keys = jax.random.split(jax.random.fold_in(streams_of[1], 1), N_LAT * N_LON * TOK_DEV // TOK_DEV)
    fetch_owner_turns = jax.random.permutation(jax.random.fold_in(streams_of[1], 3), N_LAT * N_LON * TOK_DEV // TOK_DEV)
    fetch_owner = jax.vmap(lambda own, number: deal_out(jax.random.fold_in(streams_of[1], 2), own, number, TOK_DEV, N_LAT, 1, CAP, 2))(fetch_owner_keys, fetch_owner_turns).reshape((N_LAT, N_LON, TOK_DEV, 1))
    fetch_slot = set_ends(jax.random.randint(streams_of[2], (N_LAT, N_LON, TOK_DEV), 0, BUF_DEV), jax.random.fold_in(streams_of[2], 1), 0, BUF_DEV - 1).astype(jnp.int32)
    norm_gain = jnp.clip(1.0 + 0.18 * jax.random.normal(streams_of[3], (D,), jnp.float32), 0.1, 1.9)
    qkv_weight = draw_qkv_weight(jax.random.fold_in(streams_of[7], 71), 0)
    out_weight = normal_values(streams_of[5], (D, D), D ** -0.5, 0.25)
    out_grad = normal_values(streams_of[6], (NLAT, NLON, LEV, D), 1.0, 6.0, ((0, 16), (1, 8)))
    return {"buffer": buffer, "fetch_owner": fetch_owner, "fetch_slot": fetch_slot, "norm_gain": norm_gain, "qkv_weight": qkv_weight, "out_weight": out_weight, "out_grad": out_grad}


EPSILON = 1e-05

def mixed_product(form, left, right):
    return jnp.einsum(form, left.astype(jnp.float32), right.astype(jnp.float32))

def to_windows(field_grid):
    lat_size, lon_size, lev_size = field_grid.shape[:3]
    trailing = field_grid.shape[3:]
    shaped = field_grid.reshape((lat_size // WLAT, WLAT, lon_size // WLON, WLON, lev_size // WLEV, WLEV) + trailing)
    ordering = (0, 2, 4, 1, 3, 5) + tuple(range(6, 6 + len(trailing)))
    return shaped.transpose(ordering).reshape((lat_size // WLAT, lon_size // WLON * (lev_size // WLEV), WLAT * WLON * WLEV) + trailing)

def from_windows(windows, lat_size, lon_size, lev_size):
    trailing = windows.shape[3:]
    shaped = windows.reshape((lat_size // WLAT, lon_size // WLON, lev_size // WLEV, WLAT, WLON, WLEV) + trailing)
    ordering = (0, 3, 1, 4, 2, 5) + tuple(range(6, 6 + len(trailing)))
    return shaped.transpose(ordering).reshape((lat_size, lon_size, lev_size) + trailing)

def window_pass(states_win, cotan_win, group_win, norm_gain, qkv_weight, out_weight):
    win_count, win_size, features = states_win.shape
    head_size = features // HEADS
    score_scale = head_size ** (-0.5)
    inputs = states_win.astype(jnp.float32)
    centred = inputs - lax.optimization_barrier(jnp.mean(inputs, -1, keepdims=True))
    inverse = lax.rsqrt(lax.optimization_barrier(jnp.mean(centred * centred, -1, keepdims=True)) + EPSILON)
    normed = centred * inverse
    hidden = (normed * norm_gain).astype(jnp.bfloat16)
    flat_hidden = hidden.reshape(win_count * win_size, features)
    packed = jnp.dot(flat_hidden, qkv_weight, preferred_element_type=jnp.float32).astype(jnp.bfloat16)
    packed = packed.reshape(win_count, win_size, 3, HEADS, head_size)
    queries = packed[:, :, 0]
    key_part = packed[:, :, 1]
    value_part = packed[:, :, 2]
    scores = mixed_product('nqhe,nkhe->nhqk', queries, key_part) * score_scale
    same_group = (group_win[:, :, None] == group_win[:, None, :])[:, None]
    scores = jnp.where(same_group, scores, -jnp.inf)
    shifted = jnp.exp(scores - lax.optimization_barrier(jnp.max(scores, -1, keepdims=True)))
    attention = shifted / lax.optimization_barrier(jnp.sum(shifted, -1, keepdims=True))
    attention_low = attention.astype(jnp.bfloat16)
    attended = mixed_product('nhqk,nkhe->nqhe', attention_low, value_part).astype(jnp.bfloat16)
    attended = attended.reshape(win_count * win_size, features)
    projected = jnp.dot(attended, out_weight, preferred_element_type=jnp.float32)
    result = (inputs.reshape(win_count * win_size, features) + projected).astype(jnp.bfloat16)
    cotan_flat = cotan_win.reshape(win_count * win_size, features)
    grad_attended = jnp.dot(cotan_flat, out_weight.T, preferred_element_type=jnp.float32).astype(jnp.bfloat16)
    grad_attended = grad_attended.reshape(win_count, win_size, HEADS, head_size)
    grad_probs = mixed_product('nqhe,nkhe->nhqk', grad_attended, value_part)
    grad_values = mixed_product('nhqk,nqhe->nkhe', attention_low, grad_attended).astype(jnp.bfloat16)
    grad_scores = attention * (grad_probs - lax.optimization_barrier(jnp.sum(attention * grad_probs, -1, keepdims=True))) * score_scale
    grad_scores = grad_scores.astype(jnp.bfloat16)
    grad_queries = mixed_product('nhqk,nkhe->nqhe', grad_scores, key_part).astype(jnp.bfloat16)
    grad_keys = mixed_product('nhqk,nqhe->nkhe', grad_scores, queries).astype(jnp.bfloat16)
    grad_packed = jnp.stack([grad_queries, grad_keys, grad_values], 2).reshape(win_count * win_size, 3 * features)
    grad_hidden = jnp.dot(grad_packed, qkv_weight.T, preferred_element_type=jnp.float32)
    grad_hidden = grad_hidden.reshape(win_count, win_size, features) * norm_gain
    grad_norm = inverse * (grad_hidden - lax.optimization_barrier(jnp.mean(grad_hidden, -1, keepdims=True)) - normed * lax.optimization_barrier(jnp.mean(grad_hidden * normed, -1, keepdims=True)))
    grad_rolled = (cotan_win.astype(jnp.float32) + grad_norm).astype(jnp.bfloat16)
    return (result.reshape(win_count, win_size, features), grad_rolled, flat_hidden, grad_packed, attended, cotan_flat)

def reference(buffer, fetch_owner, fetch_slot, norm_gain, qkv_weight, out_weight, out_grad):
    sector = jnp.arange(N_LON, dtype=jnp.int32)[None, :, None]
    row_ids = (fetch_owner[..., 0] * N_LON + sector) * BUF_DEV + fetch_slot
    fetched = jnp.take(buffer, row_ids.reshape(-1), axis=0)
    fetched = fetched.reshape(N_LAT, N_LON, LAT_DEV, LON_DEV, LEV, D)
    states = fetched.transpose(0, 2, 1, 3, 4, 5).reshape(NLAT, NLON, LEV, D)
    rolled = jnp.roll(states, (-SLAT, -SLON), axis=(0, 1))
    cotangent = jnp.roll(out_grad, (-SLAT, -SLON), axis=(0, 1))
    latitude = jnp.arange(NLAT, dtype=jnp.int32)
    group_ids = jnp.broadcast_to((latitude >= NLAT - SLAT).astype(jnp.int32)[:, None, None], (NLAT, NLON, LEV))

    def scan_step(grad_total, pieces):
        result, grad_rolled, flat_hidden, grad_packed, attended, cotan_flat = window_pass(pieces[0], pieces[1], pieces[2], norm_gain, qkv_weight, out_weight)
        term = jnp.concatenate([jnp.dot(flat_hidden.T, grad_packed, preferred_element_type=jnp.float32), jnp.dot(attended.T, cotan_flat, preferred_element_type=jnp.float32)], 1)
        return (grad_total + term, (result, grad_rolled))
    grad_total, (results, grads_win) = lax.scan(scan_step, jnp.zeros((D, 4 * D), jnp.float32), (to_windows(rolled), to_windows(cotangent), to_windows(group_ids)))
    block_out = jnp.roll(from_windows(results, NLAT, NLON, LEV), (SLAT, SLON), axis=(0, 1))
    grad_states = jnp.roll(from_windows(grads_win, NLAT, NLON, LEV), (SLAT, SLON), axis=(0, 1))
    return (block_out, grad_states, grad_total[:, :3 * D], grad_total[:, 3 * D:])
```

```python
import functools
import jax
import jax.numpy as jnp
import numpy as np
from jax import lax
from jax.experimental import pallas as pl
from jax.experimental.pallas import tpu as pltpu
from jax.sharding import PartitionSpec as P

NN = (((1,), (0,)), ((), ()))
NT = (((1,), (1,)), ((), ()))
TN = (((0,), (0,)), ((), ()))
F32 = jnp.float32
BF16 = jnp.bfloat16
I32 = jnp.int32
D = 512
BANDS, SECTORS = 16, 8
DEVICES = BANDS * SECTORS
LAT, LON, LEV = 12, 48, 4
TOKENS = LAT * LON * LEV
STRIP = LON * LEV
ROWS = 1152
CAP = 288
WIN = 144
HALF = 72
SMALL = 80
BLOCK = 2 * WIN
SCALE = 0.125
LOG2E = 1.4426950408889634
BOTH = ("lat", "lon")

UP, SIDE, CORNER = 3 * WIN + SMALL, WIN + SMALL, SMALL
INNER, EDGE = 6 * WIN, 4 * WIN + SMALL


def split_matrix(places, rows):
    matrix = np.zeros((rows, places * 4), np.float32)
    for place in range(places):
        for level in range(4):
            matrix[(level // 2) * places * 2 + place * 2 + level % 2, place * 4 + level] = 1
    return matrix


SPLIT = split_matrix(36, WIN)
SPLIT_SMALL = split_matrix(18, SMALL)


def corner_matrix():
    matrix = np.zeros((BLOCK, 4 * SMALL), np.float32)
    for r in range(2):
        for part in range(4):
            for at in range(36):
                matrix[r * WIN + part * 36 + at, part * SMALL + r * 36 + at] = 1
    return matrix


CORNER_JOIN = corner_matrix()


def corner_back():
    matrix = np.zeros((4 * SMALL, BLOCK), np.float32)
    for part in range(4):
        split = CORNER_JOIN[:, part * SMALL : part * SMALL + HALF]
        matrix[part * SMALL : part * SMALL + HALF] = SPLIT_SMALL[:HALF].T @ split.T
    return matrix


CORNER_BACK = corner_back()


def product(left, right, form=NN):
    return lax.dot_general(left, right, form, preferred_element_type=F32)


def normalise(values):
    centred = values - jnp.mean(values, -1, keepdims=True)
    inverse = lax.rsqrt(jnp.mean(centred * centred, -1, keepdims=True) + 1e-5)
    return centred * inverse, inverse


def whole(*shape):
    return pl.BlockSpec(shape, lambda *i: (0,) * len(shape))


def blocks(rows, width):
    return pl.BlockSpec((rows, width), lambda i: (i, 0))


def shapes(*dims, dtype=BF16):
    return [jax.ShapeDtypeStruct(dim, dtype) for dim in dims]


def call(kernel, name, grid, ins, outs, out_shapes, scratch, cost, vmem):
    flops, moved, exps = cost
    return pl.pallas_call(
        kernel,
        grid=grid,
        in_specs=ins,
        out_specs=outs,
        out_shape=out_shapes,
        scratch_shapes=scratch,
        compiler_params=pltpu.CompilerParams(vmem_limit_bytes=vmem * 2**20),
        cost_estimate=pl.CostEstimate(flops=flops, bytes_accessed=moved, transcendentals=exps),
        name=name,
    )


def request_kernel(owner_ref, slot_ref, lists_ref, place_ref, hits, ranks):
    owner = owner_ref[...]
    slot = slot_ref[...]
    hit = owner == lax.broadcasted_iota(I32, (BANDS, TOKENS), 0)
    hits[...] = hit.astype(F32)
    step = 256
    row = lax.broadcasted_iota(I32, (step, step), 0)
    triangle = (row <= lax.broadcasted_iota(I32, (step, step), 1)).astype(F32).astype(BF16)
    before = jnp.zeros((BANDS, 1), F32)
    for at in range(0, TOKENS, step):
        part = hits[:, at : at + step]
        count = product(part.astype(BF16), triangle) + before
        ranks[:, at : at + step] = jnp.sum(part * count, 0, keepdims=True) - 1.0
        before = before + jnp.sum(part, 1, keepdims=True)
    rank = ranks[...]
    place_ref[...] = owner * CAP + rank.astype(I32)
    high = jnp.where(hit, lax.shift_right_logical(slot, 5), 0).astype(F32).astype(BF16)
    low = jnp.where(hit, slot & 31, 0).astype(F32).astype(BF16)
    chosen = rank == lax.broadcasted_iota(I32, (CAP, TOKENS), 0).astype(F32)
    chosen = jnp.where(chosen, 1.0, 0.0).astype(BF16)
    found = product(high, chosen, NT) * 32.0 + product(low, chosen, NT)
    lists_ref[...] = found.astype(I32)


def make_requests(owners, slots):
    return call(
        request_kernel, "requests", (),
        [whole(1, TOKENS)] * 2,
        [whole(BANDS, CAP), whole(1, TOKENS)],
        shapes((BANDS, CAP), (1, TOKENS), dtype=I32),
        [pltpu.VMEM((BANDS, TOKENS), F32), pltpu.VMEM((1, TOKENS), F32)],
        (100000000, 100000, 0), 20,
    )(owners, slots)


def serve_kernel(lists_ref, buffer_ref, out_ref):
    asker = pl.program_id(0)
    lane = lax.broadcasted_iota(I32, (CAP, BANDS), 1)
    wanted = jnp.sum(jnp.where(lane == asker, lists_ref[...], 0), 1, keepdims=True)
    chosen = wanted == lax.broadcasted_iota(I32, (CAP, ROWS), 1)
    chosen = jnp.where(chosen, 1.0, 0.0).astype(BF16)
    out_ref[...] = product(chosen, buffer_ref[...]).astype(BF16)


def serve(lists, buffer):
    return call(
        serve_kernel, "serve", (BANDS,),
        [whole(CAP, BANDS), whole(ROWS, D)],
        blocks(CAP, D),
        shapes((BANDS * CAP, D))[0],
        [], (5400000000, 6000000, 0), 20,
    )(lists, buffer)


def pick_kernel(place_ref, replies_ref, out_ref):
    place = place_ref[...]
    rows = place.shape[0]
    step = 512
    total = 0.0
    for at in range(0, BANDS * CAP, step):
        chosen = (place - at) == lax.broadcasted_iota(I32, (rows, step), 1)
        chosen = jnp.where(chosen, 1.0, 0.0).astype(BF16)
        total += product(chosen, replies_ref[at : at + step, :])
    out_ref[...] = total.astype(BF16)


def pick(place, replies, rows):
    count = place.shape[0]
    return call(
        pick_kernel, "pick", (count // rows,),
        [blocks(rows, 1), whole(BANDS * CAP, D)],
        blocks(rows, D),
        shapes((count, D))[0],
        [], (count * 4718592, 6000000, 0), 30,
    )(place, replies)


def sort_kernel(grid_ref, split_ref, small_ref, up_ref, side_ref, corner_ref, inner_ref, edge_ref):
    strips = [grid_ref[i * STRIP : i * STRIP + STRIP, :].astype(F32) for i in range(LAT)]

    def put(ref, at, lats, first, cols):
        part = jnp.concatenate([strips[i][first * 4 : (first + cols) * 4] for i in lats])
        matrix = split_ref if part.shape[0] == WIN else small_ref
        ref[at : at + matrix.shape[0], :] = product(matrix[...], part.astype(BF16)).astype(BF16)

    low, mid, high = range(3), range(3, 9), range(9, 12)
    for q in range(3):
        put(up_ref, q * WIN, low, 6 + 12 * q, 12)
        put(inner_ref, q * BLOCK, range(3, 6), 6 + 12 * q, 12)
        put(inner_ref, q * BLOCK + WIN, range(6, 9), 6 + 12 * q, 12)
        put(edge_ref, WIN + q * WIN, high, 6 + 12 * q, 12)
    put(up_ref, 3 * WIN, low, 42, 6)
    put(side_ref, 0, mid, 0, 6)
    put(side_ref, WIN, high, 0, 6)
    put(corner_ref, 0, low, 0, 6)
    put(edge_ref, 0, mid, 42, 6)
    put(edge_ref, 4 * WIN, high, 42, 6)


def sort_pieces(values):
    return call(
        sort_kernel, "sort_pieces", (),
        [whole(TOKENS, D), whole(WIN, WIN), whole(SMALL, HALF)],
        [whole(n, D) for n in (UP, SIDE, CORNER, INNER, EDGE)],
        shapes(*[(n, D) for n in (UP, SIDE, CORNER, INNER, EDGE)]),
        [], (400000000, 5000000, 0), 24,
    )(values, jnp.asarray(SPLIT, BF16), jnp.asarray(SPLIT_SMALL, BF16))


def order_ids():
    ids = np.arange(TOKENS).reshape(LAT, LON, 2, 2)

    def piece(lats, first, cols):
        part = ids[lats[0] : lats[-1] + 1, first : first + cols].transpose(2, 0, 1, 3).reshape(-1)
        return np.pad(part, (0, WIN - 64 - HALF if part.size == HALF else 0))

    low, mid, high = range(3), range(3, 9), range(9, 12)
    order = [piece(low, 6 + 12 * q, 12) for q in range(3)]
    order += [piece(low, 42, 6), piece(mid, 0, 6), piece(high, 0, 6), piece(low, 0, 6)]
    for q in range(3):
        order += [piece(range(3, 6), 6 + 12 * q, 12), piece(range(6, 9), 6 + 12 * q, 12)]
    order += [piece(mid, 42, 6)]
    order += [piece(high, 6 + 12 * q, 12) for q in range(3)] + [piece(high, 42, 6)]
    return np.concatenate(order)


ORDER = order_ids()
SENT = UP + SIDE + CORNER


def join_halves(first, second):
    first, second = first.astype(F32), second.astype(F32)
    return jnp.concatenate([first[:HALF], second[:HALF], first[HALF:], second[HALF:]])


def attend(x_all, c_all, bias, w_ref, gain_ref, ow_ref, x_out, c_out, h_ref, att_ref, dp_ref, packed, slopes):
    x_out[...] = x_all.astype(BF16)
    cot = c_all.astype(BF16)
    c_out[...] = cot
    slopes[...] = product(cot, ow_ref[...], NT).astype(BF16)
    normed, _ = normalise(x_all)
    hidden = (normed * gain_ref[...]).astype(BF16)
    h_ref[...] = hidden
    for part in range(3):
        cols = slice(part * D, part * D + D)
        packed[:, cols] = product(hidden, w_ref[:, cols]).astype(BF16)
    lane = lax.broadcasted_iota(I32, (1, 128), 1)
    sides = [jnp.where(lane < 64, 1.0, 0.0).astype(BF16), jnp.where(lane < 64, 0.0, 1.0).astype(BF16)]
    for window in range(2):
        rows = slice(window * WIN, window * WIN + WIN)
        for pair in range(4):
            spot = [slice(part * D + pair * 128, part * D + pair * 128 + 128) for part in range(3)]
            q2, k2, v2 = (packed[rows, cols] for cols in spot)
            g2 = slopes[rows, spot[0]]
            att = dq = dk = dv = 0.0
            for side in sides:
                qm, km, vm, gm = q2 * side, k2 * side, v2 * side, g2 * side
                scores = product(k2, qm, NT) * (SCALE * LOG2E)
                if bias is not None:
                    scores = scores + bias[...]
                grown = jnp.exp2(scores - jnp.max(scores, 0, keepdims=True))
                probs = grown * (1.0 / jnp.sum(grown, 0, keepdims=True))
                low = probs.astype(BF16)
                weighted = probs * product(v2, gm, NT)
                slope = weighted - probs * jnp.sum(weighted, 0, keepdims=True)
                slope = (slope * SCALE).astype(BF16)
                dv += product(low, gm)
                dk += product(slope, qm)
                att += product(low, vm, TN)
                dq += product(slope, km, TN)
            att_ref[rows, spot[0]] = att.astype(BF16)
            dp_ref[rows, spot[0]] = dq.astype(BF16)
            dp_ref[rows, spot[1]] = dk.astype(BF16)
            dp_ref[rows, spot[2]] = dv.astype(BF16)


def inner_kernel(x_ref, c_ref, *refs):
    x_all = join_halves(x_ref[:WIN, :], x_ref[WIN:, :])
    c_all = join_halves(c_ref[:WIN, :], c_ref[WIN:, :])
    attend(x_all, c_all, None, *refs)


def edge_kernel(xe, xu, xs, xc, ce, cu, cs, cc, join_ref, bias_ref, *refs):
    *refs, x_all, c_all = refs
    step = pl.program_id(0)

    @pl.when(step == 0)
    def _():
        x_all[...] = join_halves(xe[:WIN, :], xs[:WIN, :])
        c_all[...] = join_halves(ce[:WIN, :], cs[:WIN, :])

    for q in range(3):

        @pl.when(step == q + 1)
        def _(q=q):
            near, far = slice(WIN + q * WIN, 2 * WIN + q * WIN), slice(q * WIN, q * WIN + WIN)
            x_all[...] = join_halves(xe[near, :], xu[far, :])
            c_all[...] = join_halves(ce[near, :], cu[far, :])

    @pl.when(step == 4)
    def _():
        near, far, along = slice(4 * WIN, EDGE), slice(3 * WIN, UP), slice(WIN, SIDE)
        parts = [xe[near, :], xs[along, :], xu[far, :], xc[...]]
        x_all[...] = product(join_ref[...], jnp.concatenate(parts))
        parts = [ce[near, :], cs[along, :], cu[far, :], cc[...]]
        c_all[...] = product(join_ref[...], jnp.concatenate(parts))

    attend(x_all[...], c_all[...], bias_ref, *refs)


def attend_specs(rows):
    outs = [blocks(BLOCK, n) for n in (D, D, D, D, 3 * D)]
    out_shapes = shapes(*[(rows, n) for n in (D, D, D, D, 3 * D)])
    scratch = [pltpu.VMEM((BLOCK, 3 * D), BF16), pltpu.VMEM((BLOCK, D), BF16)]
    cost = (rows * 6000000, rows * 10000, rows * 1200)
    return outs, out_shapes, scratch, cost


WEIGHTS = [(D, 3 * D), (1, D), (D, D)]


def attend_inner(x, cot, weights):
    outs, out_shapes, scratch, cost = attend_specs(INNER)
    return call(
        inner_kernel, "attend_inner", (3,),
        [blocks(BLOCK, D)] * 2 + [whole(*dim) for dim in WEIGHTS],
        outs, out_shapes, scratch, cost, 24,
    )(x, cot, *weights)


def attend_edge(x_parts, c_parts, bias, weights):
    rows = 5 * BLOCK
    outs, out_shapes, scratch, cost = attend_specs(rows)
    parts = [whole(n, D) for n in (EDGE, UP, SIDE, CORNER)]
    return call(
        edge_kernel, "attend_edge", (5,),
        parts * 2
        + [whole(BLOCK, 4 * SMALL), pl.BlockSpec((None, WIN, WIN), lambda i: (jnp.minimum(i, 1), 0, 0))]
        + [whole(*dim) for dim in WEIGHTS],
        outs, out_shapes, scratch + [pltpu.VMEM((BLOCK, D), F32)] * 2, cost, 32,
    )(*x_parts, *c_parts, jnp.asarray(CORNER_JOIN, BF16), bias, *weights)


def weight_kernel(hi, ai, ci, di, he, ae, ce, de, out_ref, turned):
    def chunk(c):
        if c < 3:
            cols = slice(c * D, c * D + D)
            return product(hi[...], di[:, cols], TN) + product(he[...], de[:, cols], TN)
        return product(ai[...], ci[...], TN) + product(ae[...], ce[...], TN)

    upper = lax.broadcasted_iota(I32, (64, 8, D), 1) < 4
    for pair in range(2):
        first = chunk(2 * pair).reshape(64, 8, D)
        second = chunk(2 * pair + 1).reshape(64, 8, D)
        swap = lambda v: jnp.concatenate([v[:, 4:], v[:, :4]], 1)
        even = jnp.where(upper, first, swap(second))
        odd = jnp.where(upper, swap(first), second)
        turned[:, 0, pair] = even
        turned[:, 1, pair] = odd
    out_ref[...] = turned[...].reshape(2048, D).astype(BF16)


def weight_terms(inner, edge):
    dims = [(n, w) for n in (INNER, 5 * BLOCK) for w in (D, D, D, 3 * D)]
    return call(
        weight_kernel, "weight_terms", (),
        [whole(*dim) for dim in dims],
        whole(2048, D), shapes((2048, D))[0],
        [pltpu.VMEM((64, 2, 2, 8, D), F32)],
        (TOKENS * 2 * D * 4 * D, 18000000, 0), 48,
    )(*inner, *edge)


def finished(x_ref, c_ref, att_ref, dp_ref, w_ref, gain_ref, ow_ref):
    x = x_ref[...].astype(F32)
    out = x + product(att_ref[...], ow_ref[...])
    normed, inverse = normalise(x)
    hidden = product(dp_ref[...], w_ref[...], NT) * gain_ref[...]
    hidden = (
        hidden
        - jnp.mean(hidden, -1, keepdims=True)
        - normed * jnp.mean(hidden * normed, -1, keepdims=True)
    )
    grad = c_ref[...].astype(F32) + inverse * hidden
    return out, grad


def grid_pieces(split_ref, values):
    first = jnp.concatenate([values[:HALF], values[WIN : WIN + HALF]]).astype(BF16)
    second = jnp.concatenate([values[HALF:WIN], values[WIN + HALF :]]).astype(BF16)
    return [product(split_ref[...], part, TN).astype(BF16) for part in (first, second)]


def finish_inner_kernel(split_ref, *refs):
    *refs, out_ref, grad_ref = refs
    for ref, values in zip((out_ref, grad_ref), finished(*refs)):
        first, second = grid_pieces(split_ref, values)
        ref[:WIN, :] = first
        ref[WIN:, :] = second


def finish_edge_kernel(split_ref, back_ref, *refs):
    refs, outs = refs[:7], refs[7:]
    step = pl.program_id(0)
    for (edge, up, side, corner), values in zip((outs[:4], outs[4:]), finished(*refs)):

        @pl.when(step < 4)
        def _(edge=edge, up=up, side=side, values=values):
            first, second = grid_pieces(split_ref, values)
            edge[pl.ds(pl.multiple_of(step * WIN, 16), WIN), :] = first

            @pl.when(step == 0)
            def _():
                side[:WIN, :] = second

            @pl.when(step > 0)
            def _():
                up[pl.ds(pl.multiple_of((step - 1) * WIN, 16), WIN), :] = second

        @pl.when(step == 4)
        def _(edge=edge, up=up, side=side, corner=corner, values=values):
            parts = product(back_ref[...], values.astype(BF16)).astype(BF16)
            edge[4 * WIN :, :] = parts[:SMALL]
            side[WIN:, :] = parts[SMALL : 2 * SMALL]
            up[3 * WIN :, :] = parts[2 * SMALL : 3 * SMALL]
            corner[...] = parts[3 * SMALL :]


def finish_inner(values, weights):
    return call(
        finish_inner_kernel, "finish_inner", (3,),
        [whole(WIN, WIN)] + [blocks(BLOCK, n) for n in (D, D, D, 3 * D)] + [whole(*dim) for dim in WEIGHTS],
        [blocks(BLOCK, D)] * 2, shapes((INNER, D), (INNER, D)), [],
        (INNER * 2200000, INNER * 8000, INNER), 24,
    )(jnp.asarray(SPLIT, BF16), *values, *weights)


def finish_edge(values, weights):
    dims = [(n, D) for n in (EDGE, UP, SIDE, CORNER)] * 2
    rows = 5 * BLOCK
    return call(
        finish_edge_kernel, "finish_edge", (5,),
        [whole(WIN, WIN), whole(4 * SMALL, BLOCK)]
        + [blocks(BLOCK, n) for n in (D, D, D, 3 * D)]
        + [whole(*dim) for dim in WEIGHTS],
        [whole(*dim) for dim in dims], shapes(*dims), [],
        (rows * 2200000, rows * 8000, rows), 24,
    )(jnp.asarray(SPLIT, BF16), jnp.asarray(CORNER_BACK, BF16), *values, *weights)


def join_kernel(inner, edge, up, side, corner, out_ref):
    left = [corner[...].astype(F32), side[:WIN, :].astype(F32), side[WIN:, :].astype(F32)]
    right = [up[3 * WIN :, :].astype(F32), edge[:WIN, :].astype(F32), edge[4 * WIN :, :].astype(F32)]
    run, stub = 48, 24
    for i in range(LAT):
        zone, at = (0, i) if i < 3 else (1, i - 3) if i < 9 else (2, i - 9)
        parts = [left[zone][at * stub : at * stub + stub]]
        for q in range(3):
            if zone == 0:
                start, ref = q * WIN + at * run, up
            elif zone == 1:
                start, ref = q * BLOCK + at * run, inner
            else:
                start, ref = WIN + q * WIN + at * run, edge
            parts.append(ref[start : start + run, :].astype(F32))
        parts.append(right[zone][at * stub : at * stub + stub])
        out_ref[i * STRIP : i * STRIP + STRIP, :] = jnp.concatenate(parts).astype(BF16)


def join(parts):
    return call(
        join_kernel, "join", (),
        [whole(n, D) for n in (INNER, EDGE, UP, SIDE, CORNER)],
        whole(TOKENS, D), shapes((TOKENS, D))[0], [],
        (1000000, 5000000, 0), 20,
    )(*parts)


def shift_pairs(lat_step, lon_step):
    return [
        (a * SECTORS + b, (a + lat_step) % BANDS * SECTORS + (b + lon_step) % SECTORS)
        for a in range(BANDS)
        for b in range(SECTORS)
    ]


def exchange(parts, sign):
    steps = ((sign, 0), (0, sign), (sign, sign))
    return [lax.ppermute(part, BOTH, shift_pairs(*step)) for part, step in zip(parts, steps)]


def swap_blocks(values, axis):
    return lax.all_to_all(values, axis, split_axis=0, concat_axis=0, tiled=True)


def per_device(buffer, fetch_owner, fetch_slot, norm_gain, qkv_weight, out_weight, out_grad):
    weights = (qkv_weight, norm_gain.reshape(1, D), out_weight)
    lists, place = make_requests(fetch_owner.reshape(1, TOKENS), fetch_slot.reshape(1, TOKENS))
    lists = swap_blocks(lists, "lat")
    replies = swap_blocks(serve(lists.T, buffer).reshape(BANDS, CAP, D), "lat")
    replies = replies.reshape(BANDS * CAP, D)

    c_up, c_side, c_corner, c_inner, c_edge = sort_pieces(out_grad.reshape(TOKENS, D))
    c_parts = [c_edge] + exchange([c_up, c_side, c_corner], -1)
    place = place.reshape(TOKENS)[ORDER].reshape(-1, 1)

    sent = pick(place[:SENT], replies, 272)
    arrived = exchange([sent[:UP], sent[UP : UP + SIDE], sent[UP + SIDE :]], -1)
    kept = pick(place[SENT:], replies, 304)

    last = (lax.axis_index("lat") == BANDS - 1) & (jnp.arange(2) == 1)
    group = jnp.arange(WIN) >= HALF
    apart = last[:, None, None] & (group[:, None] != group[None, :])
    bias = jnp.where(apart, -jnp.inf, 0.0).astype(F32)
    xi, ci, hi, ai, di = attend_inner(kept[:INNER], c_inner, weights)
    xe, ce, he, ae, de = attend_edge([kept[INNER:]] + arrived, c_parts, bias, weights)
    terms = swap_blocks(weight_terms((hi, ai, ci, di), (he, ae, ce, de)), BOTH)

    edges = finish_edge((xe, ce, ae, de), weights)
    returned = [exchange(edges[at + 1 : at + 4], 1) for at in (0, 4)]
    inners = finish_inner((xi, ci, ai, di), weights)
    outs = [
        join([inners[n], edges[4 * n]] + returned[n]).reshape(LAT, LON, LEV, D) for n in range(2)
    ]
    total = jnp.sum(terms.reshape(DEVICES, 4, 4, D).astype(F32), 0).transpose(1, 0, 2).reshape(4, 4 * D)
    return (outs[0], outs[1], total[:, : 3 * D], total[:, 3 * D :])


def solution(mesh):
    return jax.shard_map(
        per_device,
        mesh=mesh,
        in_specs=(
            P(BOTH, None),
            P("lat", "lon", None, None),
            P("lat", "lon", None),
            P(),
            P(),
            P(),
            P("lat", "lon", None, None),
        ),
        out_specs=(
            P("lat", "lon", None, None),
            P("lat", "lon", None, None),
            P(BOTH, None),
            P(BOTH, None),
        ),
        check_vma=False,
    )
```

```python
import functools
import jax
import jax.numpy as jnp
import numpy as np
from jax import lax
from jax.experimental import pallas as pl
from jax.experimental.pallas import tpu as pltpu
from jax.sharding import PartitionSpec as P

NN = (((1,), (0,)), ((), ()))
NT = (((1,), (1,)), ((), ()))
TN = (((0,), (0,)), ((), ()))
F32 = jnp.float32
BF16 = jnp.bfloat16
I32 = jnp.int32
D = 512
BANDS, SECTORS = 16, 8
DEVICES = BANDS * SECTORS
LAT, LON, LEV = 12, 48, 4
TOKENS = LAT * LON * LEV
STRIP = LON * LEV
ROWS = 1152
CAP = 288
WIN = 144
HALF = 72
SMALL = 80
BLOCK = 2 * WIN
SCALE = 0.125
LOG2E = 1.4426950408889634
BOTH = ("lat", "lon")

UP, SIDE, CORNER = 3 * WIN + SMALL, WIN + SMALL, SMALL
INNER, EDGE = 6 * WIN, 4 * WIN + SMALL


def split_matrix(places, rows):
    matrix = np.zeros((rows, places * 4), np.float32)
    for place in range(places):
        for level in range(4):
            matrix[(level // 2) * places * 2 + place * 2 + level % 2, place * 4 + level] = 1
    return matrix


SPLIT = split_matrix(36, WIN)
SPLIT_SMALL = split_matrix(18, SMALL)


def corner_matrix():
    matrix = np.zeros((BLOCK, 4 * SMALL), np.float32)
    for r in range(2):
        for part in range(4):
            for at in range(36):
                matrix[r * WIN + part * 36 + at, part * SMALL + r * 36 + at] = 1
    return matrix


CORNER_JOIN = corner_matrix()


def corner_back():
    matrix = np.zeros((4 * SMALL, BLOCK), np.float32)
    for part in range(4):
        split = CORNER_JOIN[:, part * SMALL : part * SMALL + HALF]
        matrix[part * SMALL : part * SMALL + HALF] = SPLIT_SMALL[:HALF].T @ split.T
    return matrix


CORNER_BACK = corner_back()


def product(left, right, form=NN):
    return lax.dot_general(left, right, form, preferred_element_type=F32)


def normalise(values):
    centred = values - jnp.mean(values, -1, keepdims=True)
    inverse = lax.rsqrt(jnp.mean(centred * centred, -1, keepdims=True) + 1e-5)
    return centred * inverse, inverse


def whole(*shape):
    return pl.BlockSpec(shape, lambda *i: (0,) * len(shape))


def blocks(rows, width):
    return pl.BlockSpec((rows, width), lambda i: (i, 0))


def shapes(*dims, dtype=BF16):
    return [jax.ShapeDtypeStruct(dim, dtype) for dim in dims]


def call(kernel, name, grid, ins, outs, out_shapes, scratch, cost, vmem, aliases={}):
    flops, moved, exps = cost
    return pl.pallas_call(
        kernel,
        grid=grid,
        in_specs=ins,
        out_specs=outs,
        out_shape=out_shapes,
        scratch_shapes=scratch,
        input_output_aliases=aliases,
        compiler_params=pltpu.CompilerParams(vmem_limit_bytes=vmem * 2**20),
        cost_estimate=pl.CostEstimate(flops=flops, bytes_accessed=moved, transcendentals=exps),
        name=name,
    )


ZONES = (0, 3, 9, 12)
GROUP = 16
COMPACT = [(b - a) * STRIP + BANDS * 2 * (GROUP - 1) for a, b in zip(ZONES, ZONES[1:])]


def request_kernel(owner_ref, slot_ref, lists_ref, place_ref, table_ref, hits, ranks):
    owner = owner_ref[...]
    slot = slot_ref[...]
    hit = owner == lax.broadcasted_iota(I32, (BANDS, TOKENS), 0)
    hits[...] = hit.astype(F32)
    step = STRIP
    row = lax.broadcasted_iota(I32, (step, step), 0)
    triangle = (row <= lax.broadcasted_iota(I32, (step, step), 1)).astype(F32).astype(BF16)
    row = lax.broadcasted_iota(I32, (BANDS, BANDS), 0)
    earlier = (lax.broadcasted_iota(I32, (BANDS, BANDS), 1) < row).astype(F32).astype(BF16)
    before = jnp.zeros((BANDS, 1), F32)
    columns = []
    for zone in range(3):
        first = before
        strips = range(ZONES[zone], ZONES[zone + 1])
        for strip in strips:
            spot = slice(strip * step, strip * step + step)
            part = hits[:, spot]
            count = product(part.astype(BF16), triangle) + before
            ranks[:, spot] = jnp.sum(part * count, 0, keepdims=True) - 1.0
            before = before + jnp.sum(part, 1, keepdims=True)
        start = jnp.floor(first * (1.0 / GROUP))
        groups = jnp.floor((before + (GROUP - 1)) * (1.0 / GROUP)) - start
        groups = jnp.where(before > first, groups, 0.0)
        base = product(earlier, jnp.broadcast_to(groups, (BANDS, 128)).astype(BF16))[:, :1]
        shift = (base - start) * GROUP
        for strip in strips:
            spot = slice(strip * step, strip * step + step)
            moved = jnp.sum(hits[:, spot] * shift, 0, keepdims=True)
            place_ref[:, spot] = (ranks[:, spot] + moved).astype(I32)
        columns += [start, groups]
    columns += [jnp.zeros((BANDS, 2), F32)]
    table_ref[...] = jnp.concatenate(columns, 1).astype(I32)
    rank = ranks[...]
    high = jnp.where(hit, lax.shift_right_logical(slot, 5), 0).astype(F32).astype(BF16)
    low = jnp.where(hit, slot & 31, 0).astype(F32).astype(BF16)
    chosen = rank == lax.broadcasted_iota(I32, (CAP, TOKENS), 0).astype(F32)
    chosen = jnp.where(chosen, 1.0, 0.0).astype(BF16)
    found = product(high, chosen, NT) * 32.0 + product(low, chosen, NT)
    lists_ref[...] = found.astype(I32)


def make_requests(owners, slots):
    return call(
        request_kernel, "requests", (),
        [whole(1, TOKENS)] * 2,
        [whole(BANDS, CAP), whole(1, TOKENS), whole(BANDS, 8)],
        shapes((BANDS, CAP), (1, TOKENS), (BANDS, 8), dtype=I32),
        [pltpu.VMEM((BANDS, TOKENS), F32), pltpu.VMEM((1, TOKENS), F32)],
        (100000000, 100000, 0), 20,
    )(owners, slots)


ASKERS = 4


def serve_kernel(lists_ref, buffer_ref, out_ref):
    lane = lax.broadcasted_iota(I32, (CAP, BANDS), 1)
    wanted = []
    for at in range(ASKERS):
        asker = pl.program_id(0) * ASKERS + at
        wanted.append(jnp.sum(jnp.where(lane == asker, lists_ref[...], 0), 1, keepdims=True))
    chosen = jnp.concatenate(wanted) == lax.broadcasted_iota(I32, (ASKERS * CAP, ROWS), 1)
    chosen = jnp.where(chosen, 1.0, 0.0).astype(BF16)
    out_ref[...] = product(chosen, buffer_ref[...]).astype(BF16)


def serve(lists, buffer):
    return call(
        serve_kernel, "serve", (BANDS // ASKERS,),
        [whole(CAP, BANDS), whole(ROWS, D)],
        blocks(ASKERS * CAP, D),
        shapes((BANDS * CAP, D))[0],
        [], (5400000000, 6000000, 0), 60,
    )(lists, buffer)


def pick_kernel(table_ref, place_ref, replies_ref, up_ref, side_ref, corner_ref, inner_ref, edge_ref, compact):
    compact[...] = jnp.zeros_like(compact)
    firsts = (0, UP + CORNER, UP + CORNER + 2 * WIN + INNER)
    for zone, size in enumerate(COMPACT):
        filled = 0
        for owner in range(BANDS):
            start = owner * CAP + table_ref[owner, 2 * zone] * GROUP
            groups = table_ref[owner, 2 * zone + 1]

            def move(at, filled, start=start):
                source = pl.multiple_of(start + at * GROUP, GROUP)
                target = pl.multiple_of(filled, GROUP)
                compact[pl.ds(target, GROUP), :] = replies_ref[pl.ds(source, GROUP), :]
                return filled + GROUP

            filled = lax.fori_loop(0, groups, move, filled)

        def find(first, count, size=size):
            place = place_ref[first : first + count, :]
            chosen = place == lax.broadcasted_iota(I32, (count, size), 1)
            chosen = jnp.where(chosen, 1.0, 0.0).astype(BF16)
            return product(chosen, compact[:size, :]).astype(BF16)

        first = firsts[zone]
        if zone == 0:
            found = find(first, UP + CORNER)
            up_ref[...] = found[:UP]
            corner_ref[...] = found[UP:]
        elif zone == 1:
            found = find(first, 2 * WIN + INNER)
            side_ref[:WIN, :] = found[:WIN]
            edge_ref[:WIN, :] = found[WIN : 2 * WIN]
            inner_ref[...] = found[2 * WIN :]
        else:
            found = find(first, SMALL + EDGE - WIN)
            side_ref[WIN:, :] = found[:SMALL]
            edge_ref[WIN:, :] = found[SMALL:]


def pick(table, place, replies):
    return call(
        pick_kernel, "pick", (),
        [pl.BlockSpec(memory_space=pltpu.SMEM), whole(PLACES, 1), whole(BANDS * CAP, D)],
        [whole(n, D) for n in (UP, SIDE, CORNER, INNER, EDGE)],
        shapes(*[(n, D) for n in (UP, SIDE, CORNER, INNER, EDGE)]),
        [pltpu.VMEM((max(COMPACT), D), BF16)], (3600000000, 8000000, 0), 36,
    )(table, place, replies)


def sort_kernel(grid_ref, split_ref, small_ref, up_ref, side_ref, corner_ref, inner_ref, edge_ref):
    strips = [grid_ref[i * STRIP : i * STRIP + STRIP, :].astype(F32) for i in range(LAT)]

    def put(ref, at, lats, first, cols):
        part = jnp.concatenate([strips[i][first * 4 : (first + cols) * 4] for i in lats])
        matrix = split_ref if part.shape[0] == WIN else small_ref
        ref[at : at + matrix.shape[0], :] = product(matrix[...], part.astype(BF16)).astype(BF16)

    low, mid, high = range(3), range(3, 9), range(9, 12)
    for q in range(3):
        put(up_ref, q * WIN, low, 6 + 12 * q, 12)
        put(inner_ref, q * BLOCK, range(3, 6), 6 + 12 * q, 12)
        put(inner_ref, q * BLOCK + WIN, range(6, 9), 6 + 12 * q, 12)
        put(edge_ref, WIN + q * WIN, high, 6 + 12 * q, 12)
    put(up_ref, 3 * WIN, low, 42, 6)
    put(side_ref, 0, mid, 0, 6)
    put(side_ref, WIN, high, 0, 6)
    put(corner_ref, 0, low, 0, 6)
    put(edge_ref, 0, mid, 42, 6)
    put(edge_ref, 4 * WIN, high, 42, 6)


def sort_pieces(values):
    return call(
        sort_kernel, "sort_pieces", (),
        [whole(TOKENS, D), whole(WIN, WIN), whole(SMALL, HALF)],
        [whole(n, D) for n in (UP, SIDE, CORNER, INNER, EDGE)],
        shapes(*[(n, D) for n in (UP, SIDE, CORNER, INNER, EDGE)]),
        [], (400000000, 5000000, 0), 24,
    )(values, jnp.asarray(SPLIT, BF16), jnp.asarray(SPLIT_SMALL, BF16))


def order_ids():
    ids = np.arange(TOKENS).reshape(LAT, LON, 2, 2)

    def piece(lats, first, cols):
        part = ids[lats[0] : lats[-1] + 1, first : first + cols].transpose(2, 0, 1, 3).reshape(-1)
        return np.pad(part, (0, WIN - 64 - HALF if part.size == HALF else 0))

    low, mid, high = range(3), range(3, 9), range(9, 12)
    order = [piece(low, 6 + 12 * q, 12) for q in range(3)] + [piece(low, 42, 6), piece(low, 0, 6)]
    order += [piece(mid, 0, 6), piece(mid, 42, 6)]
    for q in range(3):
        order += [piece(range(3, 6), 6 + 12 * q, 12), piece(range(6, 9), 6 + 12 * q, 12)]
    order += [piece(high, 0, 6)]
    order += [piece(high, 6 + 12 * q, 12) for q in range(3)] + [piece(high, 42, 6)]
    return np.concatenate(order)


ORDER = order_ids()
PLACES = UP + SIDE + CORNER + INNER + EDGE


def join_halves(first, second):
    first, second = first.astype(F32), second.astype(F32)
    return jnp.concatenate([first[:HALF], second[:HALF], first[HALF:], second[HALF:]])


def attend(x_all, c_all, bias, w_ref, gain_ref, ow_ref, x_out, c_out, h_ref, att_ref, dp_ref, packed, slopes):
    x_out[...] = x_all.astype(BF16)
    cot = c_all.astype(BF16)
    c_out[...] = cot
    slopes[...] = product(cot, ow_ref[...], NT).astype(BF16)
    normed, _ = normalise(x_all)
    hidden = (normed * gain_ref[...]).astype(BF16)
    h_ref[...] = hidden
    for part in range(3):
        cols = slice(part * D, part * D + D)
        packed[:, cols] = product(hidden, w_ref[:, cols]).astype(BF16)
    lane = lax.broadcasted_iota(I32, (1, 128), 1)
    sides = [jnp.where(lane < 64, 1.0, 0.0).astype(BF16), jnp.where(lane < 64, 0.0, 1.0).astype(BF16)]
    for window in range(2):
        rows = slice(window * WIN, window * WIN + WIN)
        for pair in range(4):
            spot = [slice(part * D + pair * 128, part * D + pair * 128 + 128) for part in range(3)]
            q2, k2, v2 = (packed[rows, cols] for cols in spot)
            g2 = slopes[rows, spot[0]]
            att = dq = dk = dv = 0.0
            for side in sides:
                qm, km, vm, gm = q2 * side, k2 * side, v2 * side, g2 * side
                scores = product(k2, qm, NT) * (SCALE * LOG2E)
                if bias is not None:
                    scores = scores + bias[...]
                grown = jnp.exp2(scores - jnp.max(scores, 0, keepdims=True))
                probs = grown * (1.0 / jnp.sum(grown, 0, keepdims=True))
                low = probs.astype(BF16)
                weighted = probs * product(v2, gm, NT)
                slope = weighted - probs * jnp.sum(weighted, 0, keepdims=True)
                slope = (slope * SCALE).astype(BF16)
                dv += product(low, gm)
                dk += product(slope, qm)
                att += product(low, vm, TN)
                dq += product(slope, km, TN)
            att_ref[rows, spot[0]] = att.astype(BF16)
            dp_ref[rows, spot[0]] = dq.astype(BF16)
            dp_ref[rows, spot[1]] = dk.astype(BF16)
            dp_ref[rows, spot[2]] = dv.astype(BF16)


def inner_kernel(x_ref, c_ref, *refs):
    x_all = join_halves(x_ref[:WIN, :], x_ref[WIN:, :])
    c_all = join_halves(c_ref[:WIN, :], c_ref[WIN:, :])
    attend(x_all, c_all, None, *refs)


def edge_kernel(xe, xu, xs, xc, ce, cu, cs, cc, join_ref, bias_ref, *refs):
    weights, (*refs, x_all, c_all) = refs[:3], refs[8:]
    step = pl.program_id(0)

    @pl.when(step == 0)
    def _():
        x_all[...] = join_halves(xe[:WIN, :], xs[:WIN, :])
        c_all[...] = join_halves(ce[:WIN, :], cs[:WIN, :])

    for q in range(3):

        @pl.when(step == q + 1)
        def _(q=q):
            near, far = slice(WIN + q * WIN, 2 * WIN + q * WIN), slice(q * WIN, q * WIN + WIN)
            x_all[...] = join_halves(xe[near, :], xu[far, :])
            c_all[...] = join_halves(ce[near, :], cu[far, :])

    @pl.when(step == 4)
    def _():
        near, far, along = slice(4 * WIN, EDGE), slice(3 * WIN, UP), slice(WIN, SIDE)
        parts = [xe[near, :], xs[along, :], xu[far, :], xc[...]]
        x_all[...] = product(join_ref[...], jnp.concatenate(parts))
        parts = [ce[near, :], cs[along, :], cu[far, :], cc[...]]
        c_all[...] = product(join_ref[...], jnp.concatenate(parts))

    attend(x_all[...], c_all[...], bias_ref, *weights, *refs)


def attend_specs(rows, skip):
    widths = (D, D, D, D, 3 * D)
    outs = [pl.BlockSpec((BLOCK, n), lambda i: (i + skip, 0)) for n in widths]
    out_shapes = shapes(*[(TOKENS, n) for n in widths])
    scratch = [pltpu.VMEM((BLOCK, 3 * D), BF16), pltpu.VMEM((BLOCK, D), BF16)]
    cost = (rows * 6000000, rows * 10000, rows * 1200)
    return outs, out_shapes, scratch, cost


WEIGHTS = [(D, 3 * D), (1, D), (D, D)]


def attend_inner(x, cot, weights):
    outs, out_shapes, scratch, cost = attend_specs(INNER, 0)
    return call(
        inner_kernel, "attend_inner", (3,),
        [blocks(BLOCK, D)] * 2 + [whole(*dim) for dim in WEIGHTS],
        outs, out_shapes, scratch, cost, 18,
    )(x, cot, *weights)


def attend_edge(x_parts, c_parts, bias, weights, carried):
    outs, out_shapes, scratch, cost = attend_specs(5 * BLOCK, 3)
    parts = [whole(n, D) for n in (EDGE, UP, SIDE, CORNER)]
    return call(
        edge_kernel, "attend_edge", (5,),
        parts * 2
        + [whole(BLOCK, 4 * SMALL), pl.BlockSpec((None, WIN, WIN), lambda i: (jnp.minimum(i, 1), 0, 0))]
        + [whole(*dim) for dim in WEIGHTS]
        + [pl.BlockSpec(memory_space=pl.ANY)] * 5,
        outs, out_shapes, scratch + [pltpu.VMEM((BLOCK, D), F32)] * 2, cost, 24,
        aliases={13 + n: n for n in range(5)},
    )(*x_parts, *c_parts, jnp.asarray(CORNER_JOIN, BF16), bias, *weights, *carried)


def weight_kernel(h_ref, att_ref, c_ref, dp_ref, out_ref, turned):
    def chunk(c):
        if c < 3:
            return product(h_ref[...], dp_ref[:, c * D : c * D + D], TN)
        return product(att_ref[...], c_ref[...], TN)

    upper = lax.broadcasted_iota(I32, (64, 8, D), 1) < 4
    for pair in range(2):
        first = chunk(2 * pair).reshape(64, 8, D)
        second = chunk(2 * pair + 1).reshape(64, 8, D)
        swap = lambda v: jnp.concatenate([v[:, 4:], v[:, :4]], 1)
        even = jnp.where(upper, first, swap(second))
        odd = jnp.where(upper, swap(first), second)
        turned[:, 0, pair] = even
        turned[:, 1, pair] = odd
    out_ref[...] = turned[...].reshape(2048, D).astype(BF16)


def weight_terms(hidden, att, cot, dp):
    return call(
        weight_kernel, "weight_terms", (),
        [whole(TOKENS, n) for n in (D, D, D, 3 * D)],
        whole(2048, D), shapes((2048, D))[0],
        [pltpu.VMEM((64, 2, 2, 8, D), F32)],
        (TOKENS * 2 * D * 4 * D, 18000000, 0), 36,
    )(hidden, att, cot, dp)


def finished(x_ref, c_ref, att_ref, dp_ref, w_ref, gain_ref, ow_ref):
    x = x_ref[...].astype(F32)
    out = x + product(att_ref[...], ow_ref[...])
    normed, inverse = normalise(x)
    hidden = product(dp_ref[...], w_ref[...], NT) * gain_ref[...]
    hidden = (
        hidden
        - jnp.mean(hidden, -1, keepdims=True)
        - normed * jnp.mean(hidden * normed, -1, keepdims=True)
    )
    grad = c_ref[...].astype(F32) + inverse * hidden
    return out, grad


def grid_pieces(split_ref, values):
    first = jnp.concatenate([values[:HALF], values[WIN : WIN + HALF]]).astype(BF16)
    second = jnp.concatenate([values[HALF:WIN], values[WIN + HALF :]]).astype(BF16)
    return [product(split_ref[...], part, TN).astype(BF16) for part in (first, second)]


def finish_kernel(split_ref, back_ref, *refs):
    refs, outs = refs[:7], refs[7:]
    step = pl.program_id(0)
    for (inner, edge, up, side, corner), values in zip((outs[:5], outs[5:]), finished(*refs)):

        @pl.when(step < 3)
        def _(inner=inner, values=values):
            first, second = grid_pieces(split_ref, values)
            inner[pl.ds(pl.multiple_of(step * BLOCK, 16), WIN), :] = first
            inner[pl.ds(pl.multiple_of(step * BLOCK + WIN, 16), WIN), :] = second

        @pl.when((step >= 3) & (step < 7))
        def _(edge=edge, up=up, side=side, values=values):
            first, second = grid_pieces(split_ref, values)
            edge[pl.ds(pl.multiple_of((step - 3) * WIN, 16), WIN), :] = first

            @pl.when(step == 3)
            def _():
                side[:WIN, :] = second

            @pl.when(step > 3)
            def _():
                up[pl.ds(pl.multiple_of((step - 4) * WIN, 16), WIN), :] = second

        @pl.when(step == 7)
        def _(edge=edge, up=up, side=side, corner=corner, values=values):
            parts = product(back_ref[...], values.astype(BF16)).astype(BF16)
            edge[4 * WIN :, :] = parts[:SMALL]
            side[WIN:, :] = parts[SMALL : 2 * SMALL]
            up[3 * WIN :, :] = parts[2 * SMALL : 3 * SMALL]
            corner[...] = parts[3 * SMALL :]


def finish(values, weights):
    dims = [(n, D) for n in (INNER, EDGE, UP, SIDE, CORNER)] * 2
    return call(
        finish_kernel, "finish", (8,),
        [whole(WIN, WIN), whole(4 * SMALL, BLOCK)]
        + [blocks(BLOCK, n) for n in (D, D, D, 3 * D)]
        + [whole(*dim) for dim in WEIGHTS],
        [whole(*dim) for dim in dims], shapes(*dims), [],
        (TOKENS * 2200000, TOKENS * 8000, TOKENS), 24,
    )(jnp.asarray(SPLIT, BF16), jnp.asarray(CORNER_BACK, BF16), *values, *weights)


def join_kernel(inner, edge, up, side, corner, out_ref):
    left = [corner[...].astype(F32), side[:WIN, :].astype(F32), side[WIN:, :].astype(F32)]
    right = [up[3 * WIN :, :].astype(F32), edge[:WIN, :].astype(F32), edge[4 * WIN :, :].astype(F32)]
    run, stub = 48, 24
    for i in range(LAT):
        zone, at = (0, i) if i < 3 else (1, i - 3) if i < 9 else (2, i - 9)
        parts = [left[zone][at * stub : at * stub + stub]]
        for q in range(3):
            if zone == 0:
                start, ref = q * WIN + at * run, up
            elif zone == 1:
                start, ref = q * BLOCK + at * run, inner
            else:
                start, ref = WIN + q * WIN + at * run, edge
            parts.append(ref[start : start + run, :].astype(F32))
        parts.append(right[zone][at * stub : at * stub + stub])
        out_ref[i * STRIP : i * STRIP + STRIP, :] = jnp.concatenate(parts).astype(BF16)


def join(parts):
    return call(
        join_kernel, "join", (),
        [whole(n, D) for n in (INNER, EDGE, UP, SIDE, CORNER)],
        whole(TOKENS, D), shapes((TOKENS, D))[0], [],
        (1000000, 5000000, 0), 20,
    )(*parts)


def shift_pairs(lat_step, lon_step):
    return [
        (a * SECTORS + b, (a + lat_step) % BANDS * SECTORS + (b + lon_step) % SECTORS)
        for a in range(BANDS)
        for b in range(SECTORS)
    ]


def exchange(parts, sign):
    steps = ((sign, 0), (0, sign), (sign, sign))
    return [lax.ppermute(part, BOTH, shift_pairs(*step)) for part, step in zip(parts, steps)]


def swap_blocks(values, axis):
    return lax.all_to_all(values, axis, split_axis=0, concat_axis=0, tiled=True)


def per_device(buffer, fetch_owner, fetch_slot, norm_gain, qkv_weight, out_weight, out_grad):
    weights = (qkv_weight, norm_gain.reshape(1, D), out_weight)
    lists, place, table = make_requests(fetch_owner.reshape(1, TOKENS), fetch_slot.reshape(1, TOKENS))
    lists = swap_blocks(lists, "lat")
    replies = swap_blocks(serve(lists.T, buffer).reshape(BANDS, CAP, D), "lat")
    replies = replies.reshape(BANDS * CAP, D)

    c_up, c_side, c_corner, c_inner, c_edge = sort_pieces(out_grad.reshape(TOKENS, D))
    c_parts = [c_edge] + exchange([c_up, c_side, c_corner], -1)
    place = place.reshape(TOKENS)[ORDER].reshape(-1, 1)

    x_up, x_side, x_corner, x_inner, x_edge = pick(table, place, replies)
    x_parts = [x_edge] + exchange([x_up, x_side, x_corner], -1)

    last = (lax.axis_index("lat") == BANDS - 1) & (jnp.arange(2) == 1)
    group = jnp.arange(WIN) >= HALF
    apart = last[:, None, None] & (group[:, None] != group[None, :])
    bias = jnp.where(apart, -jnp.inf, 0.0).astype(F32)
    first = attend_inner(x_inner, c_inner, weights)
    x, cot, hidden, att, dp = attend_edge(x_parts, c_parts, bias, weights, first)
    terms = swap_blocks(weight_terms(hidden, att, cot, dp), BOTH)

    done = finish((x, cot, att, dp), weights)
    outs = []
    for at in (0, 5):
        returned = exchange(done[at + 2 : at + 5], 1)
        outs.append(join(list(done[at : at + 2]) + returned).reshape(LAT, LON, LEV, D))
    total = jnp.sum(terms.reshape(DEVICES, 4, 4, D).astype(F32), 0).transpose(1, 0, 2).reshape(4, 4 * D)
    return (outs[0], outs[1], total[:, : 3 * D], total[:, 3 * D :])


def solution(mesh):
    return jax.shard_map(
        per_device,
        mesh=mesh,
        in_specs=(
            P(BOTH, None),
            P("lat", "lon", None, None),
            P("lat", "lon", None),
            P(),
            P(),
            P(),
            P("lat", "lon", None, None),
        ),
        out_specs=(
            P("lat", "lon", None, None),
            P("lat", "lon", None, None),
            P(BOTH, None),
            P(BOTH, None),
        ),
        check_vma=False,
    )
```

```python
import functools
import jax
import jax.numpy as jnp
import numpy as np
from jax import lax
from jax.experimental import pallas as pl
from jax.experimental.pallas import tpu as pltpu
from jax.sharding import PartitionSpec as P

NN = (((1,), (0,)), ((), ()))
NT = (((1,), (1,)), ((), ()))
TN = (((0,), (0,)), ((), ()))
F32 = jnp.float32
BF16 = jnp.bfloat16
I32 = jnp.int32
D = 512
BANDS, SECTORS = 16, 8
DEVICES = BANDS * SECTORS
LAT, LON, LEV = 12, 48, 4
TOKENS = LAT * LON * LEV
STRIP = LON * LEV
ROWS = 1152
CAP = 288
WIN = 144
HALF = 72
SMALL = 80
BLOCK = 2 * WIN
QUAD = 256
SCALE = 0.125
LOG2E = 1.4426950408889634
BOTH = ("lat", "lon")

UP, SIDE, CORNER = 3 * WIN + SMALL, WIN + SMALL, SMALL
INNER, EDGE = 6 * WIN, 4 * WIN + SMALL


def split_matrix(places, rows):
    matrix = np.zeros((rows, places * 4), np.float32)
    for place in range(places):
        for level in range(4):
            matrix[(level // 2) * places * 2 + place * 2 + level % 2, place * 4 + level] = 1
    return matrix


SPLIT = split_matrix(36, WIN)
SPLIT_SMALL = split_matrix(18, SMALL)


def corner_matrix():
    matrix = np.zeros((BLOCK, 4 * SMALL), np.float32)
    for r in range(2):
        for part in range(4):
            for at in range(36):
                matrix[r * WIN + part * 36 + at, part * SMALL + r * 36 + at] = 1
    return matrix


CORNER_JOIN = corner_matrix()


def corner_back():
    matrix = np.zeros((4 * SMALL, BLOCK), np.float32)
    for part in range(4):
        split = CORNER_JOIN[:, part * SMALL : part * SMALL + HALF]
        matrix[part * SMALL : part * SMALL + HALF] = SPLIT_SMALL[:HALF].T @ split.T
    return matrix


CORNER_BACK = corner_back()


def product(left, right, form=NN):
    return lax.dot_general(left, right, form, preferred_element_type=F32)


def normalise(values):
    centred = values - jnp.mean(values, -1, keepdims=True)
    inverse = lax.rsqrt(jnp.mean(centred * centred, -1, keepdims=True) + 1e-5)
    return centred * inverse, inverse


def whole(*shape):
    return pl.BlockSpec(shape, lambda *i: (0,) * len(shape))


def blocks(rows, width):
    return pl.BlockSpec((rows, width), lambda i: (i, 0))


def shapes(*dims, dtype=BF16):
    return [jax.ShapeDtypeStruct(dim, dtype) for dim in dims]


def call(kernel, name, grid, ins, outs, out_shapes, scratch, cost, vmem, aliases={}):
    flops, moved, exps = cost
    return pl.pallas_call(
        kernel,
        grid=grid,
        in_specs=ins,
        out_specs=outs,
        out_shape=out_shapes,
        scratch_shapes=scratch,
        input_output_aliases=aliases,
        compiler_params=pltpu.CompilerParams(vmem_limit_bytes=vmem * 2**20),
        cost_estimate=pl.CostEstimate(flops=flops, bytes_accessed=moved, transcendentals=exps),
        name=name,
    )


ZONES = (0, 3, 9, 12)
GROUP = 16
COMPACT = [(b - a) * STRIP + BANDS * 2 * (GROUP - 1) for a, b in zip(ZONES, ZONES[1:])]


def request_kernel(owner_ref, slot_ref, lists_ref, place_ref, table_ref, hits, ranks):
    owner = owner_ref[...]
    slot = slot_ref[...]
    hit = owner == lax.broadcasted_iota(I32, (BANDS, TOKENS), 0)
    hits[...] = hit.astype(F32)
    step = STRIP
    row = lax.broadcasted_iota(I32, (step, step), 0)
    triangle = (row <= lax.broadcasted_iota(I32, (step, step), 1)).astype(F32).astype(BF16)
    row = lax.broadcasted_iota(I32, (BANDS, BANDS), 0)
    earlier = (lax.broadcasted_iota(I32, (BANDS, BANDS), 1) < row).astype(F32).astype(BF16)
    before = jnp.zeros((BANDS, 1), F32)
    columns = []
    for zone in range(3):
        first = before
        strips = range(ZONES[zone], ZONES[zone + 1])
        for strip in strips:
            spot = slice(strip * step, strip * step + step)
            part = hits[:, spot]
            count = product(part.astype(BF16), triangle) + before
            ranks[:, spot] = jnp.sum(part * count, 0, keepdims=True) - 1.0
            before = before + jnp.sum(part, 1, keepdims=True)
        start = jnp.floor(first * (1.0 / GROUP))
        groups = jnp.floor((before + (GROUP - 1)) * (1.0 / GROUP)) - start
        groups = jnp.where(before > first, groups, 0.0)
        base = product(earlier, jnp.broadcast_to(groups, (BANDS, 128)).astype(BF16))[:, :1]
        shift = (base - start) * GROUP
        for strip in strips:
            spot = slice(strip * step, strip * step + step)
            moved = jnp.sum(hits[:, spot] * shift, 0, keepdims=True)
            place_ref[:, spot] = (ranks[:, spot] + moved).astype(I32)
        columns += [start, groups]
    columns += [jnp.zeros((BANDS, 2), F32)]
    table_ref[...] = jnp.concatenate(columns, 1).astype(I32)
    rank = ranks[...]
    high = jnp.where(hit, lax.shift_right_logical(slot, 5), 0).astype(F32).astype(BF16)
    low = jnp.where(hit, slot & 31, 0).astype(F32).astype(BF16)
    chosen = rank == lax.broadcasted_iota(I32, (CAP, TOKENS), 0).astype(F32)
    chosen = jnp.where(chosen, 1.0, 0.0).astype(BF16)
    found = product(high, chosen, NT) * 32.0 + product(low, chosen, NT)
    lists_ref[...] = found.astype(I32)


def make_requests(owners, slots):
    return call(
        request_kernel, "requests", (),
        [whole(1, TOKENS)] * 2,
        [whole(BANDS, CAP), whole(1, TOKENS), whole(BANDS, 8)],
        shapes((BANDS, CAP), (1, TOKENS), (BANDS, 8), dtype=I32),
        [pltpu.VMEM((BANDS, TOKENS), F32), pltpu.VMEM((1, TOKENS), F32)],
        (100000000, 100000, 0), 62,
    )(owners, slots)


ASKERS = 4


def serve_kernel(lists_ref, buffer_ref, out_ref):
    lane = lax.broadcasted_iota(I32, (CAP, BANDS), 1)
    wanted = []
    for at in range(ASKERS):
        asker = pl.program_id(0) * ASKERS + at
        wanted.append(jnp.sum(jnp.where(lane == asker, lists_ref[...], 0), 1, keepdims=True))
    chosen = jnp.concatenate(wanted) == lax.broadcasted_iota(I32, (ASKERS * CAP, ROWS), 1)
    chosen = jnp.where(chosen, 1.0, 0.0).astype(BF16)
    out_ref[...] = product(chosen, buffer_ref[...]).astype(BF16)


def serve(lists, buffer):
    return call(
        serve_kernel, "serve", (BANDS // ASKERS,),
        [whole(CAP, BANDS), whole(ROWS, D)],
        blocks(ASKERS * CAP, D),
        shapes((BANDS * CAP, D))[0],
        [], (5400000000, 6000000, 0), 60,
    )(lists, buffer)


def pick_kernel(table_ref, place_ref, replies_ref, up_ref, side_ref, corner_ref, inner_ref, edge_ref, compact):
    compact[...] = jnp.zeros_like(compact)
    firsts = (0, UP + CORNER, UP + CORNER + 2 * WIN + INNER)
    for zone, size in enumerate(COMPACT):
        filled = 0
        for owner in range(BANDS):
            start = owner * CAP + table_ref[owner, 2 * zone] * GROUP
            groups = table_ref[owner, 2 * zone + 1]

            def move(at, filled, start=start):
                source = pl.multiple_of(start + at * GROUP, GROUP)
                target = pl.multiple_of(filled, GROUP)
                compact[pl.ds(target, GROUP), :] = replies_ref[pl.ds(source, GROUP), :]
                return filled + GROUP

            filled = lax.fori_loop(0, groups, move, filled)

        def find(first, count, size=size):
            place = place_ref[first : first + count, :]
            chosen = place == lax.broadcasted_iota(I32, (count, size), 1)
            chosen = jnp.where(chosen, 1.0, 0.0).astype(BF16)
            return product(chosen, compact[:size, :]).astype(BF16)

        first = firsts[zone]
        if zone == 0:
            found = find(first, UP + CORNER)
            up_ref[...] = found[:UP]
            corner_ref[...] = found[UP:]
        elif zone == 1:
            found = find(first, 2 * WIN + INNER)
            side_ref[:WIN, :] = found[:WIN]
            edge_ref[:WIN, :] = found[WIN : 2 * WIN]
            inner_ref[...] = found[2 * WIN :]
        else:
            found = find(first, SMALL + EDGE - WIN)
            side_ref[WIN:, :] = found[:SMALL]
            edge_ref[WIN:, :] = found[SMALL:]


def pick(table, place, replies):
    return call(
        pick_kernel, "pick", (),
        [pl.BlockSpec(memory_space=pltpu.SMEM), whole(PLACES, 1), whole(BANDS * CAP, D)],
        [whole(n, D) for n in (UP, SIDE, CORNER, INNER, EDGE)],
        shapes(*[(n, D) for n in (UP, SIDE, CORNER, INNER, EDGE)]),
        [pltpu.VMEM((max(COMPACT), D), BF16)], (3600000000, 8000000, 0), 60,
    )(table, place, replies)


def sort_kernel(grid_ref, split_ref, small_ref, up_ref, side_ref, corner_ref, inner_ref, edge_ref):
    strips = [grid_ref[i * STRIP : i * STRIP + STRIP, :].astype(F32) for i in range(LAT)]

    def put(ref, at, lats, first, cols):
        part = jnp.concatenate([strips[i][first * 4 : (first + cols) * 4] for i in lats])
        matrix = split_ref if part.shape[0] == WIN else small_ref
        ref[at : at + matrix.shape[0], :] = product(matrix[...], part.astype(BF16)).astype(BF16)

    low, mid, high = range(3), range(3, 9), range(9, 12)
    for q in range(3):
        put(up_ref, q * WIN, low, 6 + 12 * q, 12)
        put(inner_ref, q * BLOCK, range(3, 6), 6 + 12 * q, 12)
        put(inner_ref, q * BLOCK + WIN, range(6, 9), 6 + 12 * q, 12)
        put(edge_ref, WIN + q * WIN, high, 6 + 12 * q, 12)
    put(up_ref, 3 * WIN, low, 42, 6)
    put(side_ref, 0, mid, 0, 6)
    put(side_ref, WIN, high, 0, 6)
    put(corner_ref, 0, low, 0, 6)
    put(edge_ref, 0, mid, 42, 6)
    put(edge_ref, 4 * WIN, high, 42, 6)


def sort_pieces(values):
    return call(
        sort_kernel, "sort_pieces", (),
        [whole(TOKENS, D), whole(WIN, WIN), whole(SMALL, HALF)],
        [whole(n, D) for n in (UP, SIDE, CORNER, INNER, EDGE)],
        shapes(*[(n, D) for n in (UP, SIDE, CORNER, INNER, EDGE)]),
        [], (400000000, 5000000, 0), 24,
    )(values, jnp.asarray(SPLIT, BF16), jnp.asarray(SPLIT_SMALL, BF16))


def order_ids():
    ids = np.arange(TOKENS).reshape(LAT, LON, 2, 2)

    def piece(lats, first, cols):
        part = ids[lats[0] : lats[-1] + 1, first : first + cols].transpose(2, 0, 1, 3).reshape(-1)
        return np.pad(part, (0, WIN - 64 - HALF if part.size == HALF else 0))

    low, mid, high = range(3), range(3, 9), range(9, 12)
    order = [piece(low, 6 + 12 * q, 12) for q in range(3)] + [piece(low, 42, 6), piece(low, 0, 6)]
    order += [piece(mid, 0, 6), piece(mid, 42, 6)]
    for q in range(3):
        order += [piece(range(3, 6), 6 + 12 * q, 12), piece(range(6, 9), 6 + 12 * q, 12)]
    order += [piece(high, 0, 6)]
    order += [piece(high, 6 + 12 * q, 12) for q in range(3)] + [piece(high, 42, 6)]
    return np.concatenate(order)


ORDER = order_ids()
PLACES = UP + SIDE + CORNER + INNER + EDGE


def join_halves(first, second):
    first, second = first.astype(F32), second.astype(F32)
    return jnp.concatenate([first[:HALF], second[:HALF], first[HALF:], second[HALF:]])


def attend(x_all, c_all, bias, w_ref, gain_ref, ow_ref, x_out, c_out, h_ref, att_ref, dp_ref, packed, slopes):
    x_out[...] = x_all.astype(BF16)
    cot = c_all.astype(BF16)
    c_out[...] = cot
    slopes[...] = product(cot, ow_ref[...], NT).astype(BF16)
    normed, _ = normalise(x_all)
    hidden = (normed * gain_ref[...]).astype(BF16)
    h_ref[...] = hidden
    for part in range(3):
        cols = slice(part * D, part * D + D)
        packed[:, cols] = product(hidden, w_ref[:, cols]).astype(BF16)
    lane = lax.broadcasted_iota(I32, (1, QUAD), 1)
    sides = [jnp.where((lane >= 64 * n) & (lane < 64 * n + 64), 1.0, 0.0) for n in range(4)]
    low_sides = [side.astype(BF16) for side in sides]

    def spread(values):
        return jnp.concatenate([values * side for side in low_sides])

    def gather(matrix, values):
        parts = product(matrix, values, TN)
        return sum(parts[n * WIN : n * WIN + WIN] * side for n, side in enumerate(sides))

    for window in range(2):
        rows = slice(window * WIN, window * WIN + WIN)
        for quad in range(2):
            spot = [slice(part * D + quad * QUAD, part * D + quad * QUAD + QUAD) for part in range(3)]
            queries, keys, values = (packed[rows, cols] for cols in spot)
            queries, grads = spread(queries), spread(slopes[rows, spot[0]])
            scores = product(keys, queries, NT) * (SCALE * LOG2E)
            if bias is not None:
                scores = scores + bias[...]
            grown = jnp.exp2(scores - jnp.max(scores, 0, keepdims=True))
            probs = grown * (1.0 / jnp.sum(grown, 0, keepdims=True))
            low = probs.astype(BF16)
            weighted = probs * product(values, grads, NT)
            slope = weighted - probs * jnp.sum(weighted, 0, keepdims=True)
            slope = (slope * SCALE).astype(BF16)
            att_ref[rows, spot[0]] = gather(low, values).astype(BF16)
            dp_ref[rows, spot[0]] = gather(slope, keys).astype(BF16)
            dp_ref[rows, spot[1]] = product(slope, queries).astype(BF16)
            dp_ref[rows, spot[2]] = product(low, grads).astype(BF16)


def inner_kernel(x_ref, c_ref, *refs):
    x_all = join_halves(x_ref[:WIN, :], x_ref[WIN:, :])
    c_all = join_halves(c_ref[:WIN, :], c_ref[WIN:, :])
    attend(x_all, c_all, None, *refs)


def edge_kernel(xe, xu, xs, xc, ce, cu, cs, cc, join_ref, bias_ref, *refs):
    weights, (*refs, x_all, c_all) = refs[:3], refs[8:]
    step = pl.program_id(0)

    @pl.when(step == 0)
    def _():
        x_all[...] = join_halves(xe[:WIN, :], xs[:WIN, :])
        c_all[...] = join_halves(ce[:WIN, :], cs[:WIN, :])

    for q in range(3):

        @pl.when(step == q + 1)
        def _(q=q):
            near, far = slice(WIN + q * WIN, 2 * WIN + q * WIN), slice(q * WIN, q * WIN + WIN)
            x_all[...] = join_halves(xe[near, :], xu[far, :])
            c_all[...] = join_halves(ce[near, :], cu[far, :])

    @pl.when(step == 4)
    def _():
        near, far, along = slice(4 * WIN, EDGE), slice(3 * WIN, UP), slice(WIN, SIDE)
        parts = [xe[near, :], xs[along, :], xu[far, :], xc[...]]
        x_all[...] = product(join_ref[...], jnp.concatenate(parts))
        parts = [ce[near, :], cs[along, :], cu[far, :], cc[...]]
        c_all[...] = product(join_ref[...], jnp.concatenate(parts))

    attend(x_all[...], c_all[...], bias_ref, *weights, *refs)


def attend_specs(rows, skip):
    widths = (D, D, D, D, 3 * D)
    outs = [pl.BlockSpec((BLOCK, n), lambda i: (i + skip, 0)) for n in widths]
    out_shapes = shapes(*[(TOKENS, n) for n in widths])
    scratch = [pltpu.VMEM((BLOCK, 3 * D), BF16), pltpu.VMEM((BLOCK, D), BF16)]
    cost = (rows * 6000000, rows * 10000, rows * 1200)
    return outs, out_shapes, scratch, cost


WEIGHTS = [(D, 3 * D), (1, D), (D, D)]


def attend_inner(x, cot, weights):
    outs, out_shapes, scratch, cost = attend_specs(INNER, 0)
    return call(
        inner_kernel, "attend_inner", (3,),
        [blocks(BLOCK, D)] * 2 + [whole(*dim) for dim in WEIGHTS],
        outs, out_shapes, scratch, cost, 18,
    )(x, cot, *weights)


def attend_edge(x_parts, c_parts, bias, weights, carried):
    outs, out_shapes, scratch, cost = attend_specs(5 * BLOCK, 3)
    parts = [whole(n, D) for n in (EDGE, UP, SIDE, CORNER)]
    return call(
        edge_kernel, "attend_edge", (5,),
        parts * 2
        + [whole(BLOCK, 4 * SMALL), pl.BlockSpec((None, WIN, 4 * WIN), lambda i: (jnp.minimum(i, 1), 0, 0))]
        + [whole(*dim) for dim in WEIGHTS]
        + [pl.BlockSpec(memory_space=pl.ANY)] * 5,
        outs, out_shapes, scratch + [pltpu.VMEM((BLOCK, D), F32)] * 2, cost, 24,
        aliases={13 + n: n for n in range(5)},
    )(*x_parts, *c_parts, jnp.asarray(CORNER_JOIN, BF16), bias, *weights, *carried)


def weight_kernel(h_ref, att_ref, c_ref, dp_ref, out_ref, turned):
    def chunk(c):
        if c < 3:
            return product(h_ref[...], dp_ref[:, c * D : c * D + D], TN)
        return product(att_ref[...], c_ref[...], TN)

    upper = lax.broadcasted_iota(I32, (64, 8, D), 1) < 4
    for pair in range(2):
        first = chunk(2 * pair).reshape(64, 8, D)
        second = chunk(2 * pair + 1).reshape(64, 8, D)
        swap = lambda v: jnp.concatenate([v[:, 4:], v[:, :4]], 1)
        even = jnp.where(upper, first, swap(second))
        odd = jnp.where(upper, swap(first), second)
        turned[:, 0, pair] = even
        turned[:, 1, pair] = odd
    out_ref[...] = turned[...].reshape(2048, D).astype(BF16)


def weight_terms(hidden, att, cot, dp):
    return call(
        weight_kernel, "weight_terms", (),
        [whole(TOKENS, n) for n in (D, D, D, 3 * D)],
        whole(2048, D), shapes((2048, D))[0],
        [pltpu.VMEM((64, 2, 2, 8, D), F32)],
        (TOKENS * 2 * D * 4 * D, 18000000, 0), 36,
    )(hidden, att, cot, dp)


def finished(x_ref, c_ref, att_ref, dp_ref, w_ref, gain_ref, ow_ref):
    x = x_ref[...].astype(F32)
    out = x + product(att_ref[...], ow_ref[...])
    normed, inverse = normalise(x)
    hidden = product(dp_ref[...], w_ref[...], NT) * gain_ref[...]
    hidden = (
        hidden
        - jnp.mean(hidden, -1, keepdims=True)
        - normed * jnp.mean(hidden * normed, -1, keepdims=True)
    )
    grad = c_ref[...].astype(F32) + inverse * hidden
    return out, grad


def grid_pieces(split_ref, values):
    first = jnp.concatenate([values[:HALF], values[WIN : WIN + HALF]]).astype(BF16)
    second = jnp.concatenate([values[HALF:WIN], values[WIN + HALF :]]).astype(BF16)
    return [product(split_ref[...], part, TN).astype(BF16) for part in (first, second)]


def finish_kernel(split_ref, back_ref, *refs):
    refs, (inner, edge, up, side, corner) = refs[:7], refs[7:]
    step = pl.program_id(0)

    def put(ref, at, values):
        if not isinstance(at, int):
            at = pl.multiple_of(at, 16)
        ref[pl.ds(at, values.shape[0]), :] = values

    for n, values in enumerate(finished(*refs)):

        @pl.when(step < 3)
        def _(n=n, values=values):
            first, second = grid_pieces(split_ref, values)
            put(inner, n * INNER + step * BLOCK, first)
            put(inner, n * INNER + step * BLOCK + WIN, second)

        @pl.when((step >= 3) & (step < 7))
        def _(n=n, values=values):
            first, second = grid_pieces(split_ref, values)
            put(edge, n * EDGE + (step - 3) * WIN, first)

            @pl.when(step == 3)
            def _():
                put(side, n * SIDE, second)

            @pl.when(step > 3)
            def _():
                put(up, n * UP + (step - 4) * WIN, second)

        @pl.when(step == 7)
        def _(n=n, values=values):
            parts = product(back_ref[...], values.astype(BF16)).astype(BF16)
            put(edge, n * EDGE + 4 * WIN, parts[:SMALL])
            put(side, n * SIDE + WIN, parts[SMALL : 2 * SMALL])
            put(up, n * UP + 3 * WIN, parts[2 * SMALL : 3 * SMALL])
            put(corner, n * CORNER, parts[3 * SMALL :])


PIECES = (INNER, EDGE, UP, SIDE, CORNER)


def finish(values, weights):
    dims = [(2 * n, D) for n in PIECES]
    return call(
        finish_kernel, "finish", (8,),
        [whole(WIN, WIN), whole(4 * SMALL, BLOCK)]
        + [blocks(BLOCK, n) for n in (D, D, D, 3 * D)]
        + [whole(*dim) for dim in WEIGHTS],
        [whole(*dim) for dim in dims], shapes(*dims), [],
        (TOKENS * 2200000, TOKENS * 8000, TOKENS), 60,
    )(jnp.asarray(SPLIT, BF16), jnp.asarray(CORNER_BACK, BF16), *values, *weights)


def join_kernel(inner, edge, up, side, corner, *outs):
    run, stub = 48, 24

    def load(ref, at, count):
        return ref[at : at + count, :].astype(F32)

    for zone in range(3):

        @pl.when((pl.program_id(0) + 1) // 2 == zone)
        def _(zone=zone):
            for n, out_ref in enumerate(outs):
                if zone == 1:
                    half = pl.program_id(0) - 1
                    left = load(side, n * SIDE, WIN)
                    right = load(edge, n * EDGE, WIN)
                    left, right = (jnp.where(half == 0, v[:HALF], v[HALF:]) for v in (left, right))
                    full = []
                    for q in range(3):
                        at = pl.multiple_of(n * INNER + q * BLOCK + half * WIN, 16)
                        full.append(inner[pl.ds(at, WIN), :].astype(F32))
                elif zone == 0:
                    left, right = load(corner, n * CORNER, SMALL), load(up, n * UP + 3 * WIN, SMALL)
                    full = [load(up, n * UP + q * WIN, WIN) for q in range(3)]
                else:
                    left, right = load(side, n * SIDE + WIN, SMALL), load(edge, n * EDGE + 4 * WIN, SMALL)
                    full = [load(edge, n * EDGE + WIN + q * WIN, WIN) for q in range(3)]
                for i in range(3):
                    parts = [left[i * stub : i * stub + stub]]
                    parts += [part[i * run : i * run + run] for part in full]
                    parts.append(right[i * stub : i * stub + stub])
                    strip = jnp.concatenate(parts)
                    out_ref[i] = strip.reshape(LON, LEV, D).astype(BF16)


def join(parts):
    spec = pl.BlockSpec((3, LON, LEV, D), lambda i: (i, 0, 0, 0))
    dim = (LAT, LON, LEV, D)
    return call(
        join_kernel, "join", (4,),
        [whole(2 * n, D) for n in PIECES],
        [spec] * 2, shapes(*[dim] * 2), [],
        (1000000, 9000000, 0), 60,
    )(*parts)


def sum_kernel(terms_ref, qkv_ref, out_ref):
    total = jnp.sum(terms_ref[...].astype(F32).reshape(DEVICES, 16, D), 0)
    for c in range(3):
        qkv_ref[:, c * D : c * D + D] = total[4 * c : 4 * c + 4]
    out_ref[...] = total[12:]


def sum_terms(terms):
    return call(
        sum_kernel, "sum_terms", (),
        [whole(2048, D)], [whole(4, 3 * D), whole(4, D)],
        shapes((4, 3 * D), (4, D), dtype=F32), [], (2000000, 2200000, 0), 20,
    )(terms)


def shift_pairs(lat_step, lon_step):
    return [
        (a * SECTORS + b, (a + lat_step) % BANDS * SECTORS + (b + lon_step) % SECTORS)
        for a in range(BANDS)
        for b in range(SECTORS)
    ]


def exchange(parts, sign):
    steps = ((sign, 0), (0, sign), (sign, sign))
    return [lax.ppermute(part, BOTH, shift_pairs(*step)) for part, step in zip(parts, steps)]


def swap_blocks(values, axis):
    return lax.all_to_all(values, axis, split_axis=0, concat_axis=0, tiled=True)


def per_device(buffer, fetch_owner, fetch_slot, norm_gain, qkv_weight, out_weight, out_grad):
    weights = (qkv_weight, norm_gain.reshape(1, D), out_weight)
    lists, place, table = make_requests(fetch_owner.reshape(1, TOKENS), fetch_slot.reshape(1, TOKENS))
    lists = swap_blocks(lists, "lat")
    replies = swap_blocks(serve(lists.T, buffer).reshape(BANDS, CAP, D), "lat")
    replies = replies.reshape(BANDS * CAP, D)

    c_up, c_side, c_corner, c_inner, c_edge = sort_pieces(out_grad.reshape(TOKENS, D))
    c_parts = [c_edge] + exchange([c_up, c_side, c_corner], -1)
    place = place.reshape(TOKENS)[ORDER].reshape(-1, 1)

    x_up, x_side, x_corner, x_inner, x_edge = pick(table, place, replies)
    x_parts = [x_edge] + exchange([x_up, x_side, x_corner], -1)

    last = (lax.axis_index("lat") == BANDS - 1) & (jnp.arange(2) == 1)
    group = jnp.arange(WIN) >= HALF
    apart = last[:, None, None] & (group[:, None] != group[None, :])
    bias = jnp.tile(jnp.where(apart, -jnp.inf, 0.0).astype(F32), (1, 1, 4))
    first = attend_inner(x_inner, c_inner, weights)
    x, cot, hidden, att, dp = attend_edge(x_parts, c_parts, bias, weights, first)
    terms = swap_blocks(weight_terms(hidden, att, cot, dp), BOTH)

    inner, edge, *away = finish((x, cot, att, dp), weights)
    outs = join([inner, edge] + exchange(away, 1))
    outs = [out.reshape(LAT, LON, LEV, D) for out in outs]
    return (*outs, *sum_terms(terms))


def solution(mesh):
    return jax.shard_map(
        per_device,
        mesh=mesh,
        in_specs=(
            P(BOTH, None),
            P("lat", "lon", None, None),
            P("lat", "lon", None),
            P(),
            P(),
            P(),
            P("lat", "lon", None, None),
        ),
        out_specs=(
            P("lat", "lon", None, None),
            P("lat", "lon", None, None),
            P(BOTH, None),
            P(BOTH, None),
        ),
        check_vma=False,
    )
```

```python
import functools
import jax
import jax.numpy as jnp
import numpy as np
from jax import lax
from jax.experimental import pallas as pl
from jax.experimental.pallas import tpu as pltpu
from jax.sharding import PartitionSpec as P

NN = (((1,), (0,)), ((), ()))
NT = (((1,), (1,)), ((), ()))
TN = (((0,), (0,)), ((), ()))
F32 = jnp.float32
BF16 = jnp.bfloat16
I32 = jnp.int32
D = 512
BANDS, SECTORS = 16, 8
DEVICES = BANDS * SECTORS
LAT, LON, LEV = 12, 48, 4
TOKENS = LAT * LON * LEV
STRIP = LON * LEV
ROWS = 1152
CAP = 288
WIN = 144
HALF = 72
SMALL = 80
BLOCK = 2 * WIN
QUAD = 256
SCALE = 0.125
LOG2E = 1.4426950408889634
FAR = -1e30
BOTH = ("lat", "lon")

UP, SIDE, CORNER = 3 * WIN + SMALL, WIN + SMALL, SMALL
INNER, EDGE = 6 * WIN, 4 * WIN + SMALL


def split_matrix(places, rows):
    matrix = np.zeros((rows, places * 4), np.float32)
    for place in range(places):
        for level in range(4):
            matrix[(level // 2) * places * 2 + place * 2 + level % 2, place * 4 + level] = 1
    return matrix


SPLIT = split_matrix(36, WIN)
SPLIT_SMALL = split_matrix(18, SMALL)


def corner_matrix():
    matrix = np.zeros((BLOCK, 4 * SMALL), np.float32)
    for r in range(2):
        for part in range(4):
            for at in range(36):
                matrix[r * WIN + part * 36 + at, part * SMALL + r * 36 + at] = 1
    return matrix


CORNER_JOIN = corner_matrix()


def corner_back():
    matrix = np.zeros((4 * SMALL, BLOCK), np.float32)
    for part in range(4):
        split = CORNER_JOIN[:, part * SMALL : part * SMALL + HALF]
        matrix[part * SMALL : part * SMALL + HALF] = SPLIT_SMALL[:HALF].T @ split.T
    return matrix


CORNER_BACK = corner_back()


def product(left, right, form=NN):
    return lax.dot_general(left, right, form, preferred_element_type=F32)


def normalise(values):
    centred = values - jnp.mean(values, -1, keepdims=True)
    inverse = lax.rsqrt(jnp.mean(centred * centred, -1, keepdims=True) + 1e-5)
    return centred * inverse, inverse


def whole(*shape):
    return pl.BlockSpec(shape, lambda *i: (0,) * len(shape))


def blocks(rows, width):
    return pl.BlockSpec((rows, width), lambda i: (i, 0))


def shapes(*dims, dtype=BF16):
    return [jax.ShapeDtypeStruct(dim, dtype) for dim in dims]


def call(kernel, name, grid, ins, outs, out_shapes, scratch, cost, vmem, aliases={}):
    flops, moved, exps = cost
    return pl.pallas_call(
        kernel,
        grid=grid,
        in_specs=ins,
        out_specs=outs,
        out_shape=out_shapes,
        scratch_shapes=scratch,
        input_output_aliases=aliases,
        compiler_params=pltpu.CompilerParams(vmem_limit_bytes=vmem * 2**20),
        cost_estimate=pl.CostEstimate(flops=flops, bytes_accessed=moved, transcendentals=exps),
        name=name,
    )


ZONES = (0, 3, 9, 12)
GROUP = 16
COMPACT = [(b - a) * STRIP + BANDS * 2 * (GROUP - 1) for a, b in zip(ZONES, ZONES[1:])]


def request_kernel(owner_ref, slot_ref, lists_ref, place_ref, table_ref, hits, ranks):
    owner = owner_ref[...]
    slot = slot_ref[...]
    hit = owner == lax.broadcasted_iota(I32, (BANDS, TOKENS), 0)
    hits[...] = hit.astype(F32)
    step = STRIP
    row = lax.broadcasted_iota(I32, (step, step), 0)
    triangle = (row <= lax.broadcasted_iota(I32, (step, step), 1)).astype(F32).astype(BF16)
    row = lax.broadcasted_iota(I32, (BANDS, BANDS), 0)
    earlier = (lax.broadcasted_iota(I32, (BANDS, BANDS), 1) < row).astype(F32).astype(BF16)
    before = jnp.zeros((BANDS, 1), F32)
    columns = []
    for zone in range(3):
        first = before
        strips = range(ZONES[zone], ZONES[zone + 1])
        for strip in strips:
            spot = slice(strip * step, strip * step + step)
            part = hits[:, spot]
            count = product(part.astype(BF16), triangle) + before
            ranks[:, spot] = jnp.sum(part * count, 0, keepdims=True) - 1.0
            before = before + jnp.sum(part, 1, keepdims=True)
        start = jnp.floor(first * (1.0 / GROUP))
        groups = jnp.floor((before + (GROUP - 1)) * (1.0 / GROUP)) - start
        groups = jnp.where(before > first, groups, 0.0)
        base = product(earlier, jnp.broadcast_to(groups, (BANDS, 128)).astype(BF16))[:, :1]
        shift = (base - start) * GROUP
        for strip in strips:
            spot = slice(strip * step, strip * step + step)
            moved = jnp.sum(hits[:, spot] * shift, 0, keepdims=True)
            place_ref[:, spot] = (ranks[:, spot] + moved).astype(I32)
        columns += [start, groups]
    columns += [jnp.zeros((BANDS, 2), F32)]
    table_ref[...] = jnp.concatenate(columns, 1).astype(I32)
    rank = ranks[...]
    high = jnp.where(hit, lax.shift_right_logical(slot, 5), 0).astype(F32).astype(BF16)
    low = jnp.where(hit, slot & 31, 0).astype(F32).astype(BF16)
    chosen = rank == lax.broadcasted_iota(I32, (CAP, TOKENS), 0).astype(F32)
    chosen = jnp.where(chosen, 1.0, 0.0).astype(BF16)
    found = product(high, chosen, NT) * 32.0 + product(low, chosen, NT)
    lists_ref[...] = found.astype(I32)


def make_requests(owners, slots):
    return call(
        request_kernel, "requests", (),
        [whole(1, TOKENS)] * 2,
        [whole(BANDS, CAP), whole(1, TOKENS), whole(BANDS, 8)],
        shapes((BANDS, CAP), (1, TOKENS), (BANDS, 8), dtype=I32),
        [pltpu.VMEM((BANDS, TOKENS), F32), pltpu.VMEM((1, TOKENS), F32)],
        (100000000, 100000, 0), 62,
    )(owners, slots)


ASKERS = 4


def serve_kernel(lists_ref, buffer_ref, out_ref):
    lane = lax.broadcasted_iota(I32, (CAP, BANDS), 1)
    wanted = []
    for at in range(ASKERS):
        asker = pl.program_id(0) * ASKERS + at
        wanted.append(jnp.sum(jnp.where(lane == asker, lists_ref[...], 0), 1, keepdims=True))
    chosen = jnp.concatenate(wanted) == lax.broadcasted_iota(I32, (ASKERS * CAP, ROWS), 1)
    chosen = jnp.where(chosen, 1.0, 0.0).astype(BF16)
    out_ref[...] = product(chosen, buffer_ref[...]).astype(BF16)


def serve(lists, buffer):
    return call(
        serve_kernel, "serve", (BANDS // ASKERS,),
        [whole(CAP, BANDS), whole(ROWS, D)],
        blocks(ASKERS * CAP, D),
        shapes((BANDS * CAP, D))[0],
        [], (5400000000, 6000000, 0), 60,
    )(lists, buffer)


def pick_kernel(table_ref, place_ref, replies_ref, up_ref, side_ref, corner_ref, inner_ref, edge_ref, compact):
    compact[...] = jnp.zeros_like(compact)
    firsts = (0, UP + CORNER, UP + CORNER + 2 * WIN + INNER)
    for zone, size in enumerate(COMPACT):
        filled = 0
        for owner in range(BANDS):
            start = owner * CAP + table_ref[owner, 2 * zone] * GROUP
            groups = table_ref[owner, 2 * zone + 1]

            def move(at, filled, start=start):
                source = pl.multiple_of(start + at * GROUP, GROUP)
                target = pl.multiple_of(filled, GROUP)
                compact[pl.ds(target, GROUP), :] = replies_ref[pl.ds(source, GROUP), :]
                return filled + GROUP

            filled = lax.fori_loop(0, groups, move, filled)

        def find(first, count, size=size):
            place = place_ref[first : first + count, :]
            chosen = place == lax.broadcasted_iota(I32, (count, size), 1)
            chosen = jnp.where(chosen, 1.0, 0.0).astype(BF16)
            return product(chosen, compact[:size, :]).astype(BF16)

        first = firsts[zone]
        if zone == 0:
            found = find(first, UP + CORNER)
            up_ref[...] = found[:UP]
            corner_ref[...] = found[UP:]
        elif zone == 1:
            found = find(first, 2 * WIN + INNER)
            side_ref[:WIN, :] = found[:WIN]
            edge_ref[:WIN, :] = found[WIN : 2 * WIN]
            inner_ref[...] = found[2 * WIN :]
        else:
            found = find(first, SMALL + EDGE - WIN)
            side_ref[WIN:, :] = found[:SMALL]
            edge_ref[WIN:, :] = found[SMALL:]


def pick(table, place, replies):
    return call(
        pick_kernel, "pick", (),
        [pl.BlockSpec(memory_space=pltpu.SMEM), whole(PLACES, 1), whole(BANDS * CAP, D)],
        [whole(n, D) for n in (UP, SIDE, CORNER, INNER, EDGE)],
        shapes(*[(n, D) for n in (UP, SIDE, CORNER, INNER, EDGE)]),
        [pltpu.VMEM((max(COMPACT), D), BF16)], (3600000000, 8000000, 0), 60,
    )(table, place, replies)


def sort_kernel(grid_ref, split_ref, small_ref, up_ref, side_ref, corner_ref, inner_ref, edge_ref):
    strips = [grid_ref[i * STRIP : i * STRIP + STRIP, :].astype(F32) for i in range(LAT)]

    def put(ref, at, lats, first, cols):
        part = jnp.concatenate([strips[i][first * 4 : (first + cols) * 4] for i in lats])
        matrix = split_ref if part.shape[0] == WIN else small_ref
        ref[at : at + matrix.shape[0], :] = product(matrix[...], part.astype(BF16)).astype(BF16)

    low, mid, high = range(3), range(3, 9), range(9, 12)
    for q in range(3):
        put(up_ref, q * WIN, low, 6 + 12 * q, 12)
        put(inner_ref, q * BLOCK, range(3, 6), 6 + 12 * q, 12)
        put(inner_ref, q * BLOCK + WIN, range(6, 9), 6 + 12 * q, 12)
        put(edge_ref, WIN + q * WIN, high, 6 + 12 * q, 12)
    put(up_ref, 3 * WIN, low, 42, 6)
    put(side_ref, 0, mid, 0, 6)
    put(side_ref, WIN, high, 0, 6)
    put(corner_ref, 0, low, 0, 6)
    put(edge_ref, 0, mid, 42, 6)
    put(edge_ref, 4 * WIN, high, 42, 6)


def sort_pieces(values):
    return call(
        sort_kernel, "sort_pieces", (),
        [whole(TOKENS, D), whole(WIN, WIN), whole(SMALL, HALF)],
        [whole(n, D) for n in (UP, SIDE, CORNER, INNER, EDGE)],
        shapes(*[(n, D) for n in (UP, SIDE, CORNER, INNER, EDGE)]),
        [], (400000000, 5000000, 0), 24,
    )(values, jnp.asarray(SPLIT, BF16), jnp.asarray(SPLIT_SMALL, BF16))


def order_ids():
    ids = np.arange(TOKENS).reshape(LAT, LON, 2, 2)

    def piece(lats, first, cols):
        part = ids[lats[0] : lats[-1] + 1, first : first + cols].transpose(2, 0, 1, 3).reshape(-1)
        return np.pad(part, (0, WIN - 64 - HALF if part.size == HALF else 0))

    low, mid, high = range(3), range(3, 9), range(9, 12)
    order = [piece(low, 6 + 12 * q, 12) for q in range(3)] + [piece(low, 42, 6), piece(low, 0, 6)]
    order += [piece(mid, 0, 6), piece(mid, 42, 6)]
    for q in range(3):
        order += [piece(range(3, 6), 6 + 12 * q, 12), piece(range(6, 9), 6 + 12 * q, 12)]
    order += [piece(high, 0, 6)]
    order += [piece(high, 6 + 12 * q, 12) for q in range(3)] + [piece(high, 42, 6)]
    return np.concatenate(order)


ORDER = order_ids()
PLACES = UP + SIDE + CORNER + INNER + EDGE


EDGE_BLOCKS = (
    (WIN, lambda i: i),
    (WIN, lambda i: jnp.maximum(i - 1, 0)),
    (WIN, lambda i: i // 4),
    (SMALL, lambda i: 0),
)
EDGE_SPECS = [pl.BlockSpec((n, D), lambda i, at=at: (at(i), 0)) for n, at in EDGE_BLOCKS]
EDGE_PAIRS = [pl.BlockSpec((2, n, D), lambda i, at=at: (0, at(i), 0)) for n, at in EDGE_BLOCKS]


def join_halves(first, second):
    first, second = first.astype(F32), second.astype(F32)
    return jnp.concatenate([first[:HALF], second[:HALF], first[HALF:], second[HALF:]])


def attend(x_all, c_all, bias, w_ref, gain_ref, ow_ref, x_out, ha_ref, dp_ref, packed, slopes):
    x_out[...] = x_all.astype(BF16)
    cot = c_all.astype(BF16)
    dp_ref[:, 3 * D :] = cot
    slopes[...] = product(cot, ow_ref[...], NT).astype(BF16)
    normed, _ = normalise(x_all)
    hidden = (normed * gain_ref[...]).astype(BF16)
    ha_ref[:, :D] = hidden
    for part in range(3):
        cols = slice(part * D, part * D + D)
        packed[:, cols] = product(hidden, w_ref[:, cols]).astype(BF16)
    lane = lax.broadcasted_iota(I32, (1, QUAD), 1)
    sides = [jnp.where((lane >= 64 * n) & (lane < 64 * n + 64), 1.0, 0.0) for n in range(4)]
    low_sides = [side.astype(BF16) for side in sides]

    def spread(values):
        return jnp.concatenate([values * side for side in low_sides])

    def gather(matrix, values):
        parts = product(matrix, values, TN)
        return sum(parts[n * WIN : n * WIN + WIN] * side for n, side in enumerate(sides))

    for window in range(2):
        rows = slice(window * WIN, window * WIN + WIN)
        for quad in range(2):
            spot = [slice(part * D + quad * QUAD, part * D + quad * QUAD + QUAD) for part in range(3)]
            queries, keys, values = (packed[rows, cols] for cols in spot)
            queries, grads = spread(queries), spread(slopes[rows, spot[0]])
            scores = product(keys, queries, NT) * (SCALE * LOG2E)
            if bias is not None:
                scores = scores + bias()
            grown = jnp.exp2(scores - jnp.max(scores, 0, keepdims=True))
            probs = grown * (1.0 / jnp.sum(grown, 0, keepdims=True))
            low = probs.astype(BF16)
            weighted = probs * product(values, grads, NT)
            slope = weighted - probs * jnp.sum(weighted, 0, keepdims=True)
            slope = (slope * SCALE).astype(BF16)
            ha_ref[rows, slice(D + quad * QUAD, D + quad * QUAD + QUAD)] = gather(low, values).astype(BF16)
            dp_ref[rows, spot[0]] = gather(slope, keys).astype(BF16)
            dp_ref[rows, spot[1]] = product(slope, queries).astype(BF16)
            dp_ref[rows, spot[2]] = product(low, grads).astype(BF16)


def inner_kernel(x_ref, c_ref, *refs):
    x_all = join_halves(x_ref[:WIN, :], x_ref[WIN:, :])
    c_all = join_halves(c_ref[:WIN, :], c_ref[WIN:, :])
    attend(x_all, c_all, None, *refs)


def edge_kernel(flag_ref, xe, xu, xs, xc, ce, cu, cs, cc, join_ref, apart_ref, *refs):
    weights, (*refs, x_all, c_all) = refs[:3], refs[6:]
    step = pl.program_id(0)

    @pl.when(step == 0)
    def _():
        x_all[...] = join_halves(xe[...], xs[...])
        c_all[...] = join_halves(ce[...], cs[...])

    @pl.when((step > 0) & (step < 4))
    def _():
        x_all[...] = join_halves(xe[...], xu[...])
        c_all[...] = join_halves(ce[...], cu[...])

    @pl.when(step == 4)
    def _():
        parts = [xe[:SMALL, :], xs[:SMALL, :], xu[:SMALL, :], xc[...]]
        x_all[...] = product(join_ref[...], jnp.concatenate(parts))
        parts = [ce[:SMALL, :], cs[:SMALL, :], cu[:SMALL, :], cc[...]]
        c_all[...] = product(join_ref[...], jnp.concatenate(parts))

    seam = jnp.where(step > 0, flag_ref[0], 0).astype(F32)
    attend(x_all[...], c_all[...], lambda: apart_ref[...] * seam, *weights, *refs)


def attend_specs(rows, skip):
    widths = (D, 2 * D, 4 * D)
    outs = [pl.BlockSpec((BLOCK, n), lambda i: (i + skip, 0)) for n in widths]
    out_shapes = shapes(*[(TOKENS, n) for n in widths])
    scratch = [pltpu.VMEM((BLOCK, 3 * D), BF16), pltpu.VMEM((BLOCK, D), BF16)]
    cost = (rows * 6000000, rows * 10000, rows * 1200)
    return outs, out_shapes, scratch, cost


WEIGHTS = [(D, 3 * D), (1, D), (D, D)]


def attend_inner(x, cot, weights):
    outs, out_shapes, scratch, cost = attend_specs(INNER, 0)
    return call(
        inner_kernel, "attend_inner", (3,),
        [blocks(BLOCK, D)] * 2 + [whole(*dim) for dim in WEIGHTS],
        outs, out_shapes, scratch, cost, 60,
    )(x, cot, *weights)


def apart_matrix():
    late = np.arange(WIN) >= HALF
    return np.tile(np.where(late[:, None] != late[None, :], FAR, 0.0).astype(np.float32), (1, 4))


def attend_edge(x_parts, c_parts, flag, weights, carried):
    outs, out_shapes, scratch, cost = attend_specs(5 * BLOCK, 3)
    return call(
        edge_kernel, "attend_edge", (5,),
        [pl.BlockSpec(memory_space=pltpu.SMEM)]
        + EDGE_SPECS * 2
        + [whole(BLOCK, 4 * SMALL), whole(WIN, 4 * WIN)]
        + [whole(*dim) for dim in WEIGHTS]
        + [pl.BlockSpec(memory_space=pl.ANY)] * 3,
        outs, out_shapes, scratch + [pltpu.VMEM((BLOCK, D), F32)] * 2, cost, 60,
        aliases={14 + n: n for n in range(3)},
    )(flag, *x_parts, *c_parts, jnp.asarray(CORNER_JOIN, BF16), jnp.asarray(apart_matrix()), *weights, *carried)


def weight_kernel(core_ref, left_ref, right_ref, own_ref, away_ref, turned):
    step = pl.program_id(0)
    chunk = product(left_ref[...], right_ref[...], TN).reshape(64, 8, D)
    for c in range(4):

        @pl.when(step == c)
        def _(c=c):
            half = c % 2 * 4
            turned[:, 0, c // 2, half : half + 4] = chunk[:, :4]
            turned[:, 1, c // 2, half : half + 4] = chunk[:, 4:]

    @pl.when(step == 3)
    def _():
        core = core_ref[0]
        for at in range(BANDS // 2):
            for ref, which in ((own_ref, core), (away_ref, 1 - core)):
                part = turned[pl.ds(at * 8 + which * 4, 4)].reshape(128, D)
                ref[at * 128 : at * 128 + 128, :] = part.astype(ref.dtype)


def weight_terms(core, left, right):
    return call(
        weight_kernel, "weight_terms", (4,),
        [
            pl.BlockSpec(memory_space=pltpu.SMEM),
            pl.BlockSpec((TOKENS, D), lambda c: (0, c // 3)),
            pl.BlockSpec((TOKENS, D), lambda c: (0, c)),
        ],
        [whole(1024, D)] * 2,
        [jax.ShapeDtypeStruct((1024, D), F32), jax.ShapeDtypeStruct((1024, D), BF16)],
        [pltpu.VMEM((64, 2, 2, 8, D), F32)],
        (TOKENS * 2 * D * 4 * D, 18000000, 0), 60,
    )(core, left, right)


def add_kernel(own_ref, got_ref, out_ref):
    out_ref[...] = (own_ref[...] + got_ref[...].astype(F32)).astype(BF16)


def add_halves(own, got):
    return call(
        add_kernel, "add_halves", (4,),
        [blocks(256, D)] * 2, blocks(256, D), shapes((1024, D))[0], [],
        (1000000, 4000000, 0), 60,
    )(own, got)


def finished(x_ref, att_ref, dp_ref, w_ref, gain_ref, ow_ref):
    x = x_ref[...].astype(F32)
    out = x + product(att_ref[...], ow_ref[...])
    normed, inverse = normalise(x)
    hidden = product(dp_ref[:, : 3 * D], w_ref[...], NT) * gain_ref[...]
    hidden = (
        hidden
        - jnp.mean(hidden, -1, keepdims=True)
        - normed * jnp.mean(hidden * normed, -1, keepdims=True)
    )
    grad = dp_ref[:, 3 * D :].astype(F32) + inverse * hidden
    return out, grad


def grid_pieces(split_ref, values):
    first = jnp.concatenate([values[:HALF], values[WIN : WIN + HALF]]).astype(BF16)
    second = jnp.concatenate([values[HALF:WIN], values[WIN + HALF :]]).astype(BF16)
    return [product(split_ref[...], part, TN).astype(BF16) for part in (first, second)]


def finish_inner_kernel(split_ref, *refs):
    *refs, inner = refs
    for n, values in enumerate(finished(*refs)):
        first, second = grid_pieces(split_ref, values)
        inner[n, :WIN, :] = first
        inner[n, WIN:, :] = second


def finish_edge_kernel(split_ref, back_ref, *refs):
    refs, (edge, up, side, corner) = refs[:6], refs[6:]
    step = pl.program_id(0)
    for n, values in enumerate(finished(*refs)):

        @pl.when(step < 4)
        def _(n=n, values=values):
            first, second = grid_pieces(split_ref, values)
            edge[n] = first

            @pl.when(step == 0)
            def _():
                side[n] = second

            @pl.when(step > 0)
            def _():
                up[n] = second

        @pl.when(step == 4)
        def _(n=n, values=values):
            parts = product(back_ref[...], values.astype(BF16)).astype(BF16)
            edge[n, :SMALL, :] = parts[:SMALL]
            side[n, :SMALL, :] = parts[SMALL : 2 * SMALL]
            up[n, :SMALL, :] = parts[2 * SMALL : 3 * SMALL]
            corner[n] = parts[3 * SMALL :]


PIECES = (INNER, EDGE, UP, SIDE, CORNER)


def finish_specs(skip):
    row = lambda width, col: pl.BlockSpec((BLOCK, width), lambda i: (i + skip, col))
    return [row(D, 0), row(D, 1), row(4 * D, 0)] + [whole(*dim) for dim in WEIGHTS]


def finish_cost(rows):
    return rows * 2200000, rows * 9000, rows


def finish_inner(values, weights):
    return call(
        finish_inner_kernel, "finish_inner", (3,),
        [whole(WIN, WIN)] + finish_specs(0),
        pl.BlockSpec((2, BLOCK, D), lambda i: (0, i, 0)), shapes((2, INNER, D))[0], [],
        finish_cost(INNER), 60,
    )(jnp.asarray(SPLIT, BF16), *values, *weights)


def finish_edge(values, weights):
    return call(
        finish_edge_kernel, "finish_edge", (5,),
        [whole(WIN, WIN), whole(4 * SMALL, BLOCK)] + finish_specs(3),
        EDGE_PAIRS, shapes(*[(2, n, D) for n in PIECES[1:]]), [],
        finish_cost(5 * BLOCK), 60,
    )(jnp.asarray(SPLIT, BF16), jnp.asarray(CORNER_BACK, BF16), *values, *weights)


def join_kernel(inner, edge, up, side, corner, *outs):
    run, stub = 48, 24

    def load(ref, n, at, count):
        return ref[n, at : at + count, :].astype(F32)

    for zone in range(3):

        @pl.when((pl.program_id(0) + 1) // 2 == zone)
        def _(zone=zone):
            for n, out_ref in enumerate(outs):
                if zone == 1:
                    half = pl.program_id(0) - 1
                    left = load(side, n, 0, WIN)
                    right = load(edge, n, 0, WIN)
                    left, right = (jnp.where(half == 0, v[:HALF], v[HALF:]) for v in (left, right))
                    full = []
                    for q in range(3):
                        at = pl.multiple_of(q * BLOCK + half * WIN, 16)
                        full.append(inner[n, pl.ds(at, WIN), :].astype(F32))
                elif zone == 0:
                    left, right = load(corner, n, 0, SMALL), load(up, n, 3 * WIN, SMALL)
                    full = [load(up, n, q * WIN, WIN) for q in range(3)]
                else:
                    left, right = load(side, n, WIN, SMALL), load(edge, n, 4 * WIN, SMALL)
                    full = [load(edge, n, WIN + q * WIN, WIN) for q in range(3)]
                for i in range(3):
                    parts = [left[i * stub : i * stub + stub]]
                    parts += [part[i * run : i * run + run] for part in full]
                    parts.append(right[i * stub : i * stub + stub])
                    strip = jnp.concatenate(parts)
                    out_ref[i] = strip.reshape(LON, LEV, D).astype(BF16)


def join(parts):
    spec = pl.BlockSpec((3, LON, LEV, D), lambda i: (i, 0, 0, 0))
    dim = (LAT, LON, LEV, D)
    return call(
        join_kernel, "join", (4,),
        [whole(2, n, D) for n in PIECES],
        [spec] * 2, shapes(*[dim] * 2), [],
        (1000000, 9000000, 0), 60,
    )(*parts)


def sum_kernel(terms_ref, qkv_ref, out_ref):
    total = jnp.sum(terms_ref[...].astype(F32).reshape(DEVICES // 2, 16, D), 0)
    for c in range(3):
        qkv_ref[:, c * D : c * D + D] = total[4 * c : 4 * c + 4]
    out_ref[...] = total[12:]


def sum_terms(terms):
    return call(
        sum_kernel, "sum_terms", (),
        [whole(1024, D)], [whole(4, 3 * D), whole(4, D)],
        shapes((4, 3 * D), (4, D), dtype=F32), [], (2000000, 2200000, 0), 20,
    )(terms)


def shift_pairs(lat_step, lon_step):
    return [
        (a * SECTORS + b, (a + lat_step) % BANDS * SECTORS + (b + lon_step) % SECTORS)
        for a in range(BANDS)
        for b in range(SECTORS)
    ]


def exchange(parts, sign):
    steps = ((sign, 0), (0, sign), (sign, sign))
    return [lax.ppermute(part, BOTH, shift_pairs(*step)) for part, step in zip(parts, steps)]


def swap_blocks(values, axis, groups=None):
    return lax.all_to_all(
        values, axis, split_axis=0, concat_axis=0, axis_index_groups=groups, tiled=True
    )


SAME_CORE = [
    [a * SECTORS + b for a in range(core, BANDS, 2) for b in range(SECTORS)] for core in range(2)
]
OTHER_CORE = [(d, d ^ SECTORS) for d in range(DEVICES)]


def per_device(buffer, fetch_owner, fetch_slot, norm_gain, qkv_weight, out_weight, out_grad):
    weights = (qkv_weight, norm_gain.reshape(1, D), out_weight)
    lists, place, table = make_requests(fetch_owner.reshape(1, TOKENS), fetch_slot.reshape(1, TOKENS))
    lists = swap_blocks(lists, "lat")
    replies = swap_blocks(serve(lists.T, buffer).reshape(BANDS, CAP, D), "lat")
    replies = replies.reshape(BANDS * CAP, D)

    c_up, c_side, c_corner, c_inner, c_edge = sort_pieces(out_grad.reshape(TOKENS, D))
    c_parts = [c_edge] + exchange([c_up, c_side, c_corner], -1)
    place = place.reshape(TOKENS)[ORDER].reshape(-1, 1)

    x_up, x_side, x_corner, x_inner, x_edge = pick(table, place, replies)
    x_parts = [x_edge] + exchange([x_up, x_side, x_corner], -1)

    band = lax.axis_index("lat")
    flag = (band == BANDS - 1).astype(I32).reshape(1)
    core = (band % 2).astype(I32).reshape(1)
    first = attend_inner(x_inner, c_inner, weights)
    x, left, right = attend_edge(x_parts, c_parts, flag, weights, first)
    own, away = weight_terms(core, left, right)
    got = lax.ppermute(away, BOTH, OTHER_CORE)
    edge, *away = finish_edge((x, left, right), weights)
    returned = exchange(away, 1)
    got, edge = lax.optimization_barrier((got, edge))
    half = add_halves(own, got)
    terms = swap_blocks(half, BOTH, SAME_CORE)
    half, x = lax.optimization_barrier((half, x))
    inner = finish_inner((x, left, right), weights)
    outs = join([inner, edge] + returned)
    return (*outs, *sum_terms(terms))


def solution(mesh):
    return jax.shard_map(
        per_device,
        mesh=mesh,
        in_specs=(
            P(BOTH, None),
            P("lat", "lon", None, None),
            P("lat", "lon", None),
            P(),
            P(),
            P(),
            P("lat", "lon", None, None),
        ),
        out_specs=(
            P("lat", "lon", None, None),
            P("lat", "lon", None, None),
            P(BOTH, None),
            P(BOTH, None),
        ),
        check_vma=False,
    )
```

```python
import functools
import jax
import jax.numpy as jnp
import numpy as np
from jax import lax
from jax.experimental import pallas as pl
from jax.experimental.pallas import tpu as pltpu
from jax.sharding import PartitionSpec as P

NN = (((1,), (0,)), ((), ()))
NT = (((1,), (1,)), ((), ()))
TN = (((0,), (0,)), ((), ()))
F32 = jnp.float32
BF16 = jnp.bfloat16
I32 = jnp.int32
D = 512
BANDS, SECTORS = 16, 8
DEVICES = BANDS * SECTORS
LAT, LON, LEV = 12, 48, 4
TOKENS = LAT * LON * LEV
STRIP = LON * LEV
ROWS = 1152
CAP = 288
WIN = 144
HALF = 72
SMALL = 80
BLOCK = 2 * WIN
QUAD = 256
SCALE = 0.125
LOG2E = 1.4426950408889634
FAR = -1e30
BOTH = ("lat", "lon")

UP, SIDE, CORNER = 3 * WIN + SMALL, WIN + SMALL, SMALL
INNER, EDGE = 6 * WIN, 4 * WIN + SMALL


def split_matrix(places, rows):
    matrix = np.zeros((rows, places * 4), np.float32)
    for place in range(places):
        for level in range(4):
            matrix[(level // 2) * places * 2 + place * 2 + level % 2, place * 4 + level] = 1
    return matrix


SPLIT = split_matrix(36, WIN)
SPLIT_SMALL = split_matrix(18, SMALL)


def corner_matrix():
    matrix = np.zeros((BLOCK, 4 * SMALL), np.float32)
    for r in range(2):
        for part in range(4):
            for at in range(36):
                matrix[r * WIN + part * 36 + at, part * SMALL + r * 36 + at] = 1
    return matrix


CORNER_JOIN = corner_matrix()


def corner_back():
    matrix = np.zeros((4 * SMALL, BLOCK), np.float32)
    for part in range(4):
        split = CORNER_JOIN[:, part * SMALL : part * SMALL + HALF]
        matrix[part * SMALL : part * SMALL + HALF] = SPLIT_SMALL[:HALF].T @ split.T
    return matrix


CORNER_BACK = corner_back()


def product(left, right, form=NN):
    return lax.dot_general(left, right, form, preferred_element_type=F32)


def normalise(values):
    centred = values - jnp.mean(values, -1, keepdims=True)
    inverse = lax.rsqrt(jnp.mean(centred * centred, -1, keepdims=True) + 1e-5)
    return centred * inverse, inverse


def whole(*shape):
    return pl.BlockSpec(shape, lambda *i: (0,) * len(shape))


def blocks(rows, width):
    return pl.BlockSpec((rows, width), lambda i: (i, 0))


def shapes(*dims, dtype=BF16):
    return [jax.ShapeDtypeStruct(dim, dtype) for dim in dims]


def call(kernel, name, grid, ins, outs, out_shapes, scratch, cost, vmem, aliases={}):
    flops, moved, exps = cost
    return pl.pallas_call(
        kernel,
        grid=grid,
        in_specs=ins,
        out_specs=outs,
        out_shape=out_shapes,
        scratch_shapes=scratch,
        input_output_aliases=aliases,
        compiler_params=pltpu.CompilerParams(vmem_limit_bytes=vmem * 2**20),
        cost_estimate=pl.CostEstimate(flops=flops, bytes_accessed=moved, transcendentals=exps),
        name=name,
    )


ZONES = (0, 3, 9, 12)
GROUP = 16
COMPACT = [(b - a) * STRIP + BANDS * 2 * (GROUP - 1) for a, b in zip(ZONES, ZONES[1:])]


def request_kernel(owner_ref, slot_ref, lists_ref, place_ref, table_ref, hits, ranks):
    owner = owner_ref[...]
    slot = slot_ref[...]
    hit = owner == lax.broadcasted_iota(I32, (BANDS, TOKENS), 0)
    hits[...] = hit.astype(F32)
    step = STRIP
    row = lax.broadcasted_iota(I32, (step, step), 0)
    triangle = (row <= lax.broadcasted_iota(I32, (step, step), 1)).astype(F32).astype(BF16)
    row = lax.broadcasted_iota(I32, (BANDS, BANDS), 0)
    earlier = (lax.broadcasted_iota(I32, (BANDS, BANDS), 1) < row).astype(F32).astype(BF16)
    before = jnp.zeros((BANDS, 1), F32)
    columns = []
    for zone in range(3):
        first = before
        strips = range(ZONES[zone], ZONES[zone + 1])
        for strip in strips:
            spot = slice(strip * step, strip * step + step)
            part = hits[:, spot]
            count = product(part.astype(BF16), triangle) + before
            ranks[:, spot] = jnp.sum(part * count, 0, keepdims=True) - 1.0
            before = before + jnp.sum(part, 1, keepdims=True)
        start = jnp.floor(first * (1.0 / GROUP))
        groups = jnp.floor((before + (GROUP - 1)) * (1.0 / GROUP)) - start
        groups = jnp.where(before > first, groups, 0.0)
        base = product(earlier, jnp.broadcast_to(groups, (BANDS, 128)).astype(BF16))[:, :1]
        shift = (base - start) * GROUP
        for strip in strips:
            spot = slice(strip * step, strip * step + step)
            moved = jnp.sum(hits[:, spot] * shift, 0, keepdims=True)
            place_ref[:, spot] = (ranks[:, spot] + moved).astype(I32)
        columns += [start, groups]
    columns += [jnp.zeros((BANDS, 2), F32)]
    table_ref[...] = jnp.concatenate(columns, 1).astype(I32)
    rank = ranks[...]
    high = jnp.where(hit, lax.shift_right_logical(slot, 5), 0).astype(F32).astype(BF16)
    low = jnp.where(hit, slot & 31, 0).astype(F32).astype(BF16)
    chosen = rank == lax.broadcasted_iota(I32, (CAP, TOKENS), 0).astype(F32)
    chosen = jnp.where(chosen, 1.0, 0.0).astype(BF16)
    found = product(high, chosen, NT) * 32.0 + product(low, chosen, NT)
    lists_ref[...] = found.astype(I32)


def make_requests(owners, slots):
    return call(
        request_kernel, "requests", (),
        [whole(1, TOKENS)] * 2,
        [whole(BANDS, CAP), whole(1, TOKENS), whole(BANDS, 8)],
        shapes((BANDS, CAP), (1, TOKENS), (BANDS, 8), dtype=I32),
        [pltpu.VMEM((BANDS, TOKENS), F32), pltpu.VMEM((1, TOKENS), F32)],
        (100000000, 100000, 0), 62,
    )(owners, slots)


ASKERS = 4


def serve_kernel(lists_ref, buffer_ref, out_ref):
    lane = lax.broadcasted_iota(I32, (CAP, BANDS), 1)
    wanted = []
    for at in range(ASKERS):
        asker = pl.program_id(0) * ASKERS + at
        wanted.append(jnp.sum(jnp.where(lane == asker, lists_ref[...], 0), 1, keepdims=True))
    chosen = jnp.concatenate(wanted) == lax.broadcasted_iota(I32, (ASKERS * CAP, ROWS), 1)
    chosen = jnp.where(chosen, 1.0, 0.0).astype(BF16)
    out_ref[...] = product(chosen, buffer_ref[...]).astype(BF16)


def serve(lists, buffer):
    return call(
        serve_kernel, "serve", (BANDS // ASKERS,),
        [whole(CAP, BANDS), whole(ROWS, D)],
        blocks(ASKERS * CAP, D),
        shapes((BANDS * CAP, D))[0],
        [], (5400000000, 6000000, 0), 60,
    )(lists, buffer)


def pick_kernel(table_ref, place_ref, replies_ref, up_ref, side_ref, corner_ref, inner_ref, edge_ref, compact):
    compact[...] = jnp.zeros_like(compact)
    firsts = (0, UP + CORNER, UP + CORNER + 2 * WIN + INNER)
    for zone, size in enumerate(COMPACT):
        filled = 0
        for owner in range(BANDS):
            start = owner * CAP + table_ref[owner, 2 * zone] * GROUP
            groups = table_ref[owner, 2 * zone + 1]

            def move(at, filled, start=start):
                source = pl.multiple_of(start + at * GROUP, GROUP)
                target = pl.multiple_of(filled, GROUP)
                compact[pl.ds(target, GROUP), :] = replies_ref[pl.ds(source, GROUP), :]
                return filled + GROUP

            filled = lax.fori_loop(0, groups, move, filled)

        def find(first, count, size=size):
            place = place_ref[first : first + count, :]
            chosen = place == lax.broadcasted_iota(I32, (count, size), 1)
            chosen = jnp.where(chosen, 1.0, 0.0).astype(BF16)
            return product(chosen, compact[:size, :]).astype(BF16)

        first = firsts[zone]
        if zone == 0:
            found = find(first, UP + CORNER)
            up_ref[...] = found[:UP]
            corner_ref[...] = found[UP:]
        elif zone == 1:
            found = find(first, 2 * WIN + INNER)
            side_ref[:WIN, :] = found[:WIN]
            edge_ref[:WIN, :] = found[WIN : 2 * WIN]
            inner_ref[...] = found[2 * WIN :]
        else:
            found = find(first, SMALL + EDGE - WIN)
            side_ref[WIN:, :] = found[:SMALL]
            edge_ref[WIN:, :] = found[SMALL:]


def pick(table, place, replies):
    return call(
        pick_kernel, "pick", (),
        [pl.BlockSpec(memory_space=pltpu.SMEM), whole(PLACES, 1), whole(BANDS * CAP, D)],
        [whole(n, D) for n in (UP, SIDE, CORNER, INNER, EDGE)],
        shapes(*[(n, D) for n in (UP, SIDE, CORNER, INNER, EDGE)]),
        [pltpu.VMEM((max(COMPACT), D), BF16)], (3600000000, 8000000, 0), 60,
    )(table, place, replies)


def sort_kernel(grid_ref, split_ref, small_ref, up_ref, side_ref, corner_ref, inner_ref, edge_ref):
    strips = [grid_ref[i * STRIP : i * STRIP + STRIP, :].astype(F32) for i in range(LAT)]

    def put(ref, at, lats, first, cols):
        part = jnp.concatenate([strips[i][first * 4 : (first + cols) * 4] for i in lats])
        matrix = split_ref if part.shape[0] == WIN else small_ref
        ref[at : at + matrix.shape[0], :] = product(matrix[...], part.astype(BF16)).astype(BF16)

    low, mid, high = range(3), range(3, 9), range(9, 12)
    for q in range(3):
        put(up_ref, q * WIN, low, 6 + 12 * q, 12)
        put(inner_ref, q * BLOCK, range(3, 6), 6 + 12 * q, 12)
        put(inner_ref, q * BLOCK + WIN, range(6, 9), 6 + 12 * q, 12)
        put(edge_ref, WIN + q * WIN, high, 6 + 12 * q, 12)
    put(up_ref, 3 * WIN, low, 42, 6)
    put(side_ref, 0, mid, 0, 6)
    put(side_ref, WIN, high, 0, 6)
    put(corner_ref, 0, low, 0, 6)
    put(edge_ref, 0, mid, 42, 6)
    put(edge_ref, 4 * WIN, high, 42, 6)


def sort_pieces(values):
    return call(
        sort_kernel, "sort_pieces", (),
        [whole(TOKENS, D), whole(WIN, WIN), whole(SMALL, HALF)],
        [whole(n, D) for n in (UP, SIDE, CORNER, INNER, EDGE)],
        shapes(*[(n, D) for n in (UP, SIDE, CORNER, INNER, EDGE)]),
        [], (400000000, 5000000, 0), 24,
    )(values, jnp.asarray(SPLIT, BF16), jnp.asarray(SPLIT_SMALL, BF16))


def order_ids():
    ids = np.arange(TOKENS).reshape(LAT, LON, 2, 2)

    def piece(lats, first, cols):
        part = ids[lats[0] : lats[-1] + 1, first : first + cols].transpose(2, 0, 1, 3).reshape(-1)
        return np.pad(part, (0, WIN - 64 - HALF if part.size == HALF else 0))

    low, mid, high = range(3), range(3, 9), range(9, 12)
    order = [piece(low, 6 + 12 * q, 12) for q in range(3)] + [piece(low, 42, 6), piece(low, 0, 6)]
    order += [piece(mid, 0, 6), piece(mid, 42, 6)]
    for q in range(3):
        order += [piece(range(3, 6), 6 + 12 * q, 12), piece(range(6, 9), 6 + 12 * q, 12)]
    order += [piece(high, 0, 6)]
    order += [piece(high, 6 + 12 * q, 12) for q in range(3)] + [piece(high, 42, 6)]
    return np.concatenate(order)


ORDER = order_ids()
PLACES = UP + SIDE + CORNER + INNER + EDGE


EDGE_BLOCKS = (
    (WIN, lambda i: i),
    (WIN, lambda i: jnp.maximum(i - 1, 0)),
    (WIN, lambda i: i // 4),
    (SMALL, lambda i: 0),
)
EDGE_SPECS = [pl.BlockSpec((n, D), lambda i, at=at: (at(i), 0)) for n, at in EDGE_BLOCKS]
EDGE_PAIRS = [pl.BlockSpec((2, n, D), lambda i, at=at: (0, at(i), 0)) for n, at in EDGE_BLOCKS]


def join_halves(first, second):
    first, second = first.astype(F32), second.astype(F32)
    return jnp.concatenate([first[:HALF], second[:HALF], first[HALF:], second[HALF:]])


def attend(x_all, c_all, bias, w_ref, gain_ref, ow_ref, x_out, ha_ref, dp_ref, packed, slopes):
    x_out[...] = x_all.astype(BF16)
    cot = c_all.astype(BF16)
    dp_ref[:, 3 * D :] = cot
    slopes[...] = product(cot, ow_ref[...], NT).astype(BF16)
    normed, _ = normalise(x_all)
    hidden = (normed * gain_ref[...]).astype(BF16)
    ha_ref[:, :D] = hidden
    for part in range(3):
        cols = slice(part * D, part * D + D)
        packed[:, cols] = product(hidden, w_ref[:, cols]).astype(BF16)
    lane = lax.broadcasted_iota(I32, (1, QUAD), 1)
    sides = [jnp.where((lane >= 64 * n) & (lane < 64 * n + 64), 1.0, 0.0) for n in range(4)]
    low_sides = [side.astype(BF16) for side in sides]

    def spread(values):
        return jnp.concatenate([values * side for side in low_sides])

    def gather(matrix, values):
        parts = product(matrix, values, TN)
        return sum(parts[n * WIN : n * WIN + WIN] * side for n, side in enumerate(sides))

    for window in range(2):
        rows = slice(window * WIN, window * WIN + WIN)
        for quad in range(2):
            spot = [slice(part * D + quad * QUAD, part * D + quad * QUAD + QUAD) for part in range(3)]
            queries, keys, values = (packed[rows, cols] for cols in spot)
            queries, grads = spread(queries), spread(slopes[rows, spot[0]])
            scores = product(keys, queries, NT) * (SCALE * LOG2E)
            if bias is not None:
                scores = scores + bias()
            grown = jnp.exp2(scores - jnp.max(scores, 0, keepdims=True))
            probs = grown * (1.0 / jnp.sum(grown, 0, keepdims=True))
            low = probs.astype(BF16)
            weighted = probs * product(values, grads, NT)
            slope = weighted - probs * jnp.sum(weighted, 0, keepdims=True)
            slope = (slope * SCALE).astype(BF16)
            ha_ref[rows, slice(D + quad * QUAD, D + quad * QUAD + QUAD)] = gather(low, values).astype(BF16)
            dp_ref[rows, spot[0]] = gather(slope, keys).astype(BF16)
            dp_ref[rows, spot[1]] = product(slope, queries).astype(BF16)
            dp_ref[rows, spot[2]] = product(low, grads).astype(BF16)


def inner_kernel(x_ref, c_ref, *refs):
    x_all = join_halves(x_ref[:WIN, :], x_ref[WIN:, :])
    c_all = join_halves(c_ref[:WIN, :], c_ref[WIN:, :])
    attend(x_all, c_all, None, *refs)


def edge_kernel(flag_ref, xe, xu, xs, xc, ce, cu, cs, cc, join_ref, apart_ref, *refs):
    weights, (*refs, x_all, c_all) = refs[:3], refs[6:]
    step = pl.program_id(0)

    @pl.when(step == 0)
    def _():
        x_all[...] = join_halves(xe[...], xs[...])
        c_all[...] = join_halves(ce[...], cs[...])

    @pl.when((step > 0) & (step < 4))
    def _():
        x_all[...] = join_halves(xe[...], xu[...])
        c_all[...] = join_halves(ce[...], cu[...])

    @pl.when(step == 4)
    def _():
        parts = [xe[:SMALL, :], xs[:SMALL, :], xu[:SMALL, :], xc[...]]
        x_all[...] = product(join_ref[...], jnp.concatenate(parts))
        parts = [ce[:SMALL, :], cs[:SMALL, :], cu[:SMALL, :], cc[...]]
        c_all[...] = product(join_ref[...], jnp.concatenate(parts))

    seam = jnp.where(step > 0, flag_ref[0], 0).astype(F32)
    attend(x_all[...], c_all[...], lambda: apart_ref[...] * seam, *weights, *refs)


def attend_specs(rows, skip):
    widths = (D, 2 * D, 4 * D)
    outs = [pl.BlockSpec((BLOCK, n), lambda i: (i + skip, 0)) for n in widths]
    out_shapes = shapes(*[(TOKENS, n) for n in widths])
    scratch = [pltpu.VMEM((BLOCK, 3 * D), BF16), pltpu.VMEM((BLOCK, D), BF16)]
    cost = (rows * 6000000, rows * 10000, rows * 1200)
    return outs, out_shapes, scratch, cost


WEIGHTS = [(D, 3 * D), (1, D), (D, D)]


def attend_inner(x, cot, weights):
    outs, out_shapes, scratch, cost = attend_specs(INNER, 0)
    return call(
        inner_kernel, "attend_inner", (3,),
        [blocks(BLOCK, D)] * 2 + [whole(*dim) for dim in WEIGHTS],
        outs, out_shapes, scratch, cost, 18,
    )(x, cot, *weights)


def apart_matrix():
    late = np.arange(WIN) >= HALF
    return np.tile(np.where(late[:, None] != late[None, :], FAR, 0.0).astype(np.float32), (1, 4))


def attend_edge(x_parts, c_parts, flag, weights, carried):
    outs, out_shapes, scratch, cost = attend_specs(5 * BLOCK, 3)
    return call(
        edge_kernel, "attend_edge", (5,),
        [pl.BlockSpec(memory_space=pltpu.SMEM)]
        + EDGE_SPECS * 2
        + [whole(BLOCK, 4 * SMALL), whole(WIN, 4 * WIN)]
        + [whole(*dim) for dim in WEIGHTS]
        + [pl.BlockSpec(memory_space=pl.ANY)] * 3,
        outs, out_shapes, scratch + [pltpu.VMEM((BLOCK, D), F32)] * 2, cost, 24,
        aliases={14 + n: n for n in range(3)},
    )(flag, *x_parts, *c_parts, jnp.asarray(CORNER_JOIN, BF16), jnp.asarray(apart_matrix()), *weights, *carried)


def weight_kernel(core_ref, left_ref, right_ref, own_ref, away_ref, turned):
    step = pl.program_id(0)
    chunk = product(left_ref[...], right_ref[...], TN).reshape(64, 8, D)
    for c in range(4):

        @pl.when(step == c)
        def _(c=c):
            half = c % 2 * 4
            turned[:, 0, c // 2, half : half + 4] = chunk[:, :4]
            turned[:, 1, c // 2, half : half + 4] = chunk[:, 4:]

    @pl.when(step == 3)
    def _():
        core = core_ref[0]
        for at in range(BANDS // 2):
            for ref, which in ((own_ref, core), (away_ref, 1 - core)):
                part = turned[pl.ds(at * 8 + which * 4, 4)].reshape(128, D)
                ref[at * 128 : at * 128 + 128, :] = part.astype(ref.dtype)


def weight_terms(core, left, right):
    return call(
        weight_kernel, "weight_terms", (4,),
        [
            pl.BlockSpec(memory_space=pltpu.SMEM),
            pl.BlockSpec((TOKENS, D), lambda c: (0, c // 3)),
            pl.BlockSpec((TOKENS, D), lambda c: (0, c)),
        ],
        [whole(1024, D)] * 2,
        [jax.ShapeDtypeStruct((1024, D), F32), jax.ShapeDtypeStruct((1024, D), BF16)],
        [pltpu.VMEM((64, 2, 2, 8, D), F32)],
        (TOKENS * 2 * D * 4 * D, 18000000, 0), 24,
    )(core, left, right)


def add_kernel(own_ref, got_ref, out_ref):
    out_ref[...] = (own_ref[...] + got_ref[...].astype(F32)).astype(BF16)


def add_halves(own, got):
    return call(
        add_kernel, "add_halves", (4,),
        [blocks(256, D)] * 2, blocks(256, D), shapes((1024, D))[0], [],
        (1000000, 4000000, 0), 10,
    )(own, got)


def finished(x_ref, att_ref, dp_ref, w_ref, gain_ref, ow_ref):
    x = x_ref[...].astype(F32)
    out = x + product(att_ref[...], ow_ref[...])
    normed, inverse = normalise(x)
    hidden = product(dp_ref[:, : 3 * D], w_ref[...], NT) * gain_ref[...]
    hidden = (
        hidden
        - jnp.mean(hidden, -1, keepdims=True)
        - normed * jnp.mean(hidden * normed, -1, keepdims=True)
    )
    grad = dp_ref[:, 3 * D :].astype(F32) + inverse * hidden
    return out, grad


def grid_pieces(split_ref, values):
    first = jnp.concatenate([values[:HALF], values[WIN : WIN + HALF]]).astype(BF16)
    second = jnp.concatenate([values[HALF:WIN], values[WIN + HALF :]]).astype(BF16)
    return [product(split_ref[...], part, TN).astype(BF16) for part in (first, second)]


def finish_inner_kernel(split_ref, *refs):
    *refs, inner = refs
    for n, values in enumerate(finished(*refs)):
        first, second = grid_pieces(split_ref, values)
        inner[n, :WIN, :] = first
        inner[n, WIN:, :] = second


def finish_edge_kernel(split_ref, back_ref, *refs):
    refs, (edge, up, side, corner) = refs[:6], refs[6:]
    step = pl.program_id(0)
    for n, values in enumerate(finished(*refs)):

        @pl.when(step < 4)
        def _(n=n, values=values):
            first, second = grid_pieces(split_ref, values)
            edge[n] = first

            @pl.when(step == 0)
            def _():
                side[n] = second

            @pl.when(step > 0)
            def _():
                up[n] = second

        @pl.when(step == 4)
        def _(n=n, values=values):
            parts = product(back_ref[...], values.astype(BF16)).astype(BF16)
            edge[n, :SMALL, :] = parts[:SMALL]
            side[n, :SMALL, :] = parts[SMALL : 2 * SMALL]
            up[n, :SMALL, :] = parts[2 * SMALL : 3 * SMALL]
            corner[n] = parts[3 * SMALL :]


PIECES = (INNER, EDGE, UP, SIDE, CORNER)


def finish_specs(skip):
    row = lambda width, col: pl.BlockSpec((BLOCK, width), lambda i: (i + skip, col))
    return [row(D, 0), row(D, 1), row(4 * D, 0)] + [whole(*dim) for dim in WEIGHTS]


def finish_cost(rows):
    return rows * 2200000, rows * 9000, rows


def finish_inner(values, weights):
    return call(
        finish_inner_kernel, "finish_inner", (3,),
        [whole(WIN, WIN)] + finish_specs(0),
        pl.BlockSpec((2, BLOCK, D), lambda i: (0, i, 0)), shapes((2, INNER, D))[0], [],
        finish_cost(INNER), 20,
    )(jnp.asarray(SPLIT, BF16), *values, *weights)


def finish_edge(values, weights):
    return call(
        finish_edge_kernel, "finish_edge", (5,),
        [whole(WIN, WIN), whole(4 * SMALL, BLOCK)] + finish_specs(3),
        EDGE_PAIRS, shapes(*[(2, n, D) for n in PIECES[1:]]), [],
        finish_cost(5 * BLOCK), 24,
    )(jnp.asarray(SPLIT, BF16), jnp.asarray(CORNER_BACK, BF16), *values, *weights)


def join_kernel(inner, edge, up, side, corner, *outs):
    run, stub = 48, 24

    def load(ref, n, at, count):
        return ref[n, at : at + count, :].astype(F32)

    for zone in range(3):

        @pl.when((pl.program_id(0) + 1) // 2 == zone)
        def _(zone=zone):
            for n, out_ref in enumerate(outs):
                if zone == 1:
                    half = pl.program_id(0) - 1
                    left = load(side, n, 0, WIN)
                    right = load(edge, n, 0, WIN)
                    left, right = (jnp.where(half == 0, v[:HALF], v[HALF:]) for v in (left, right))
                    full = []
                    for q in range(3):
                        at = pl.multiple_of(q * BLOCK + half * WIN, 16)
                        full.append(inner[n, pl.ds(at, WIN), :].astype(F32))
                elif zone == 0:
                    left, right = load(corner, n, 0, SMALL), load(up, n, 3 * WIN, SMALL)
                    full = [load(up, n, q * WIN, WIN) for q in range(3)]
                else:
                    left, right = load(side, n, WIN, SMALL), load(edge, n, 4 * WIN, SMALL)
                    full = [load(edge, n, WIN + q * WIN, WIN) for q in range(3)]
                for i in range(3):
                    parts = [left[i * stub : i * stub + stub]]
                    parts += [part[i * run : i * run + run] for part in full]
                    parts.append(right[i * stub : i * stub + stub])
                    strip = jnp.concatenate(parts)
                    out_ref[i] = strip.reshape(LON, LEV, D).astype(BF16)


def join(parts):
    spec = pl.BlockSpec((3, LON, LEV, D), lambda i: (i, 0, 0, 0))
    dim = (LAT, LON, LEV, D)
    return call(
        join_kernel, "join", (4,),
        [whole(2, n, D) for n in PIECES],
        [spec] * 2, shapes(*[dim] * 2), [],
        (1000000, 9000000, 0), 26,
    )(*parts)


def sum_kernel(terms_ref, qkv_ref, out_ref):
    total = jnp.sum(terms_ref[...].astype(F32).reshape(DEVICES // 2, 16, D), 0)
    for c in range(3):
        qkv_ref[:, c * D : c * D + D] = total[4 * c : 4 * c + 4]
    out_ref[...] = total[12:]


def sum_terms(terms):
    return call(
        sum_kernel, "sum_terms", (),
        [whole(1024, D)], [whole(4, 3 * D), whole(4, D)],
        shapes((4, 3 * D), (4, D), dtype=F32), [], (2000000, 2200000, 0), 20,
    )(terms)


def shift_pairs(lat_step, lon_step):
    return [
        (a * SECTORS + b, (a + lat_step) % BANDS * SECTORS + (b + lon_step) % SECTORS)
        for a in range(BANDS)
        for b in range(SECTORS)
    ]


def exchange(parts, sign):
    steps = ((sign, 0), (0, sign), (sign, sign))
    return [lax.ppermute(part, BOTH, shift_pairs(*step)) for part, step in zip(parts, steps)]


def swap_blocks(values, axis, groups=None):
    return lax.all_to_all(
        values, axis, split_axis=0, concat_axis=0, axis_index_groups=groups, tiled=True
    )


SAME_CORE = [
    [a * SECTORS + b for a in range(core, BANDS, 2) for b in range(SECTORS)] for core in range(2)
]
OTHER_CORE = [(d, d ^ SECTORS) for d in range(DEVICES)]


def per_device(buffer, fetch_owner, fetch_slot, norm_gain, qkv_weight, out_weight, out_grad):
    weights = (qkv_weight, norm_gain.reshape(1, D), out_weight)
    lists, place, table = make_requests(fetch_owner.reshape(1, TOKENS), fetch_slot.reshape(1, TOKENS))
    lists = swap_blocks(lists, "lat")
    replies = swap_blocks(serve(lists.T, buffer).reshape(BANDS, CAP, D), "lat")
    replies = replies.reshape(BANDS * CAP, D)

    c_up, c_side, c_corner, c_inner, c_edge = sort_pieces(out_grad.reshape(TOKENS, D))
    c_parts = [c_edge] + exchange([c_up, c_side, c_corner], -1)
    place = place.reshape(TOKENS)[ORDER].reshape(-1, 1)

    x_up, x_side, x_corner, x_inner, x_edge = pick(table, place, replies)
    x_parts = [x_edge] + exchange([x_up, x_side, x_corner], -1)

    band = lax.axis_index("lat")
    flag = (band == BANDS - 1).astype(I32).reshape(1)
    core = (band % 2).astype(I32).reshape(1)
    first = attend_inner(x_inner, c_inner, weights)
    x, left, right = attend_edge(x_parts, c_parts, flag, weights, first)
    edge, *away = finish_edge((x, left, right), weights)
    returned = exchange(away, 1)
    left, right, edge = lax.optimization_barrier((left, right, edge))
    own, away = weight_terms(core, left, right)
    got = lax.ppermute(away, BOTH, OTHER_CORE)
    inner = finish_inner((x, left, right), weights)
    got, inner, returned = lax.optimization_barrier((got, inner, returned))
    terms = swap_blocks(add_halves(own, got), BOTH, SAME_CORE)
    outs = join([inner, edge] + returned)
    return (*outs, *sum_terms(terms))


def solution(mesh):
    return jax.shard_map(
        per_device,
        mesh=mesh,
        in_specs=(
            P(BOTH, None),
            P("lat", "lon", None, None),
            P("lat", "lon", None),
            P(),
            P(),
            P(),
            P("lat", "lon", None, None),
        ),
        out_specs=(
            P("lat", "lon", None, None),
            P("lat", "lon", None, None),
            P(BOTH, None),
            P(BOTH, None),
        ),
        check_vma=False,
    )
```

```python
import functools
import jax
import jax.numpy as jnp
import numpy as np
from jax import lax
from jax.experimental import pallas as pl
from jax.experimental.pallas import tpu as pltpu
from jax.sharding import PartitionSpec as P

NN = (((1,), (0,)), ((), ()))
NT = (((1,), (1,)), ((), ()))
TN = (((0,), (0,)), ((), ()))
F32 = jnp.float32
BF16 = jnp.bfloat16
I32 = jnp.int32
D = 512
BANDS, SECTORS = 16, 8
DEVICES = BANDS * SECTORS
LAT, LON, LEV = 12, 48, 4
TOKENS = LAT * LON * LEV
STRIP = LON * LEV
ROWS = 1152
CAP = 288
WIN = 144
HALF = 72
SMALL = 80
BLOCK = 2 * WIN
QUAD = 256
SCALE = 0.125
LOG2E = 1.4426950408889634
FAR = -1e30
BOTH = ("lat", "lon")

UP, SIDE, CORNER = 3 * WIN + SMALL, WIN + SMALL, SMALL
INNER, EDGE = 6 * WIN, 4 * WIN + SMALL


def split_matrix(places, rows):
    matrix = np.zeros((rows, places * 4), np.float32)
    for place in range(places):
        for level in range(4):
            matrix[(level // 2) * places * 2 + place * 2 + level % 2, place * 4 + level] = 1
    return matrix


SPLIT = split_matrix(36, WIN)
SPLIT_SMALL = split_matrix(18, SMALL)


def corner_matrix():
    matrix = np.zeros((BLOCK, 4 * SMALL), np.float32)
    for r in range(2):
        for part in range(4):
            for at in range(36):
                matrix[r * WIN + part * 36 + at, part * SMALL + r * 36 + at] = 1
    return matrix


CORNER_JOIN = corner_matrix()


def corner_back():
    matrix = np.zeros((4 * SMALL, BLOCK), np.float32)
    for part in range(4):
        split = CORNER_JOIN[:, part * SMALL : part * SMALL + HALF]
        matrix[part * SMALL : part * SMALL + HALF] = SPLIT_SMALL[:HALF].T @ split.T
    return matrix


CORNER_BACK = corner_back()


def product(left, right, form=NN):
    return lax.dot_general(left, right, form, preferred_element_type=F32)


def normalise(values):
    centred = values - jnp.mean(values, -1, keepdims=True)
    inverse = lax.rsqrt(jnp.mean(centred * centred, -1, keepdims=True) + 1e-5)
    return centred * inverse, inverse


def whole(*shape):
    return pl.BlockSpec(shape, lambda *i: (0,) * len(shape))


def blocks(rows, width):
    return pl.BlockSpec((rows, width), lambda i: (i, 0))


def shapes(*dims, dtype=BF16):
    return [jax.ShapeDtypeStruct(dim, dtype) for dim in dims]


def call(kernel, name, grid, ins, outs, out_shapes, scratch, cost, vmem, aliases={}):
    flops, moved, exps = cost
    return pl.pallas_call(
        kernel,
        grid=grid,
        in_specs=ins,
        out_specs=outs,
        out_shape=out_shapes,
        scratch_shapes=scratch,
        input_output_aliases=aliases,
        compiler_params=pltpu.CompilerParams(vmem_limit_bytes=vmem * 2**20),
        cost_estimate=pl.CostEstimate(flops=flops, bytes_accessed=moved, transcendentals=exps),
        name=name,
    )


ZONES = (0, 3, 9, 12)
GROUP = 16
COMPACT = [(b - a) * STRIP + BANDS * 2 * (GROUP - 1) for a, b in zip(ZONES, ZONES[1:])]


def request_kernel(owner_ref, slot_ref, lists_ref, place_ref, table_ref, hits, ranks):
    owner = owner_ref[...]
    slot = slot_ref[...]
    hit = owner == lax.broadcasted_iota(I32, (BANDS, TOKENS), 0)
    hits[...] = hit.astype(F32)
    step = STRIP
    row = lax.broadcasted_iota(I32, (step, step), 0)
    triangle = (row <= lax.broadcasted_iota(I32, (step, step), 1)).astype(F32).astype(BF16)
    row = lax.broadcasted_iota(I32, (BANDS, BANDS), 0)
    earlier = (lax.broadcasted_iota(I32, (BANDS, BANDS), 1) < row).astype(F32).astype(BF16)
    before = jnp.zeros((BANDS, 1), F32)
    columns = []
    for zone in range(3):
        first = before
        strips = range(ZONES[zone], ZONES[zone + 1])
        for strip in strips:
            spot = slice(strip * step, strip * step + step)
            part = hits[:, spot]
            count = product(part.astype(BF16), triangle) + before
            ranks[:, spot] = jnp.sum(part * count, 0, keepdims=True) - 1.0
            before = before + jnp.sum(part, 1, keepdims=True)
        start = jnp.floor(first * (1.0 / GROUP))
        groups = jnp.floor((before + (GROUP - 1)) * (1.0 / GROUP)) - start
        groups = jnp.where(before > first, groups, 0.0)
        base = product(earlier, jnp.broadcast_to(groups, (BANDS, 128)).astype(BF16))[:, :1]
        shift = (base - start) * GROUP
        for strip in strips:
            spot = slice(strip * step, strip * step + step)
            moved = jnp.sum(hits[:, spot] * shift, 0, keepdims=True)
            place_ref[:, spot] = (ranks[:, spot] + moved).astype(I32)
        columns += [start, groups]
    columns += [jnp.zeros((BANDS, 2), F32)]
    table_ref[...] = jnp.concatenate(columns, 1).astype(I32)
    rank = ranks[...]
    high = jnp.where(hit, lax.shift_right_logical(slot, 5), 0).astype(F32).astype(BF16)
    low = jnp.where(hit, slot & 31, 0).astype(F32).astype(BF16)
    chosen = rank == lax.broadcasted_iota(I32, (CAP, TOKENS), 0).astype(F32)
    chosen = jnp.where(chosen, 1.0, 0.0).astype(BF16)
    found = product(high, chosen, NT) * 32.0 + product(low, chosen, NT)
    lists_ref[...] = found.astype(I32)


def make_requests(owners, slots):
    return call(
        request_kernel, "requests", (),
        [whole(1, TOKENS)] * 2,
        [whole(BANDS, CAP), whole(1, TOKENS), whole(BANDS, 8)],
        shapes((BANDS, CAP), (1, TOKENS), (BANDS, 8), dtype=I32),
        [pltpu.VMEM((BANDS, TOKENS), F32), pltpu.VMEM((1, TOKENS), F32)],
        (100000000, 100000, 0), 62,
    )(owners, slots)


ASKERS = 4


def serve_kernel(lists_ref, buffer_ref, out_ref):
    lane = lax.broadcasted_iota(I32, (CAP, BANDS), 1)
    for at in range(ASKERS):
        asker = pl.program_id(0) * ASKERS + at
        wanted = jnp.sum(jnp.where(lane == asker, lists_ref[...], 0), 1, keepdims=True)
        for half in range(2):
            chosen = wanted[half * 144 : half * 144 + 144] == lax.broadcasted_iota(I32, (144, ROWS), 1)
            chosen = jnp.where(chosen, 1.0, 0.0).astype(BF16)
            rows = slice(at * CAP + half * 144, at * CAP + half * 144 + 144)
            out_ref[rows, :] = product(chosen, buffer_ref[...]).astype(BF16)


def serve(lists, buffer):
    return call(
        serve_kernel, "serve", (BANDS // ASKERS,),
        [whole(CAP, BANDS), whole(ROWS, D)],
        blocks(ASKERS * CAP, D),
        shapes((BANDS * CAP, D))[0],
        [], (5400000000, 6000000, 0), 60,
    )(lists, buffer)


def pick_kernel(table_ref, place_ref, replies_ref, up_ref, side_ref, corner_ref, inner_ref, edge_ref, compact, held, sems):
    def fetch(owner):
        rows = pl.ds(owner * CAP, CAP)
        return pltpu.make_async_copy(replies_ref.at[rows, :], held.at[rows, :], sems.at[owner])

    for owner in range(BANDS):
        fetch(owner).start()
    compact[...] = jnp.zeros_like(compact)
    firsts = (0, UP + CORNER, UP + CORNER + 2 * WIN + INNER)
    for zone, size in enumerate(COMPACT):
        filled = 0
        for owner in range(BANDS):
            if zone == 0:
                fetch(owner).wait()
            start = owner * CAP + table_ref[owner, 2 * zone] * GROUP
            groups = table_ref[owner, 2 * zone + 1]

            def move(at, filled, start=start):
                source = pl.multiple_of(start + at * GROUP, GROUP)
                target = pl.multiple_of(filled, GROUP)
                compact[pl.ds(target, GROUP), :] = held[pl.ds(source, GROUP), :]
                return filled + GROUP

            filled = lax.fori_loop(0, groups, move, filled)

        def find(first, count, size=size):
            place = place_ref[first : first + count, :]
            chosen = place == lax.broadcasted_iota(I32, (count, size), 1)
            chosen = jnp.where(chosen, 1.0, 0.0).astype(BF16)
            return product(chosen, compact[:size, :]).astype(BF16)

        first = firsts[zone]
        if zone == 0:
            found = find(first, UP + CORNER)
            up_ref[...] = found[:UP]
            corner_ref[...] = found[UP:]
        elif zone == 1:
            found = find(first, 2 * WIN + INNER)
            side_ref[:WIN, :] = found[:WIN]
            edge_ref[:WIN, :] = found[WIN : 2 * WIN]
            inner_ref[...] = found[2 * WIN :]
        else:
            found = find(first, SMALL + EDGE - WIN)
            side_ref[WIN:, :] = found[:SMALL]
            edge_ref[WIN:, :] = found[SMALL:]


def pick(table, place, replies):
    return call(
        pick_kernel, "pick", (),
        [pl.BlockSpec(memory_space=pltpu.SMEM), whole(PLACES, 1), pl.BlockSpec(memory_space=pl.ANY)],
        [whole(n, D) for n in (UP, SIDE, CORNER, INNER, EDGE)],
        shapes(*[(n, D) for n in (UP, SIDE, CORNER, INNER, EDGE)]),
        [
            pltpu.VMEM((max(COMPACT), D), BF16),
            pltpu.VMEM((BANDS * CAP, D), BF16),
            pltpu.SemaphoreType.DMA((BANDS,)),
        ],
        (3600000000, 8000000, 0), 60,
    )(table, place, replies)


def sort_kernel(grid_ref, split_ref, small_ref, up_ref, side_ref, corner_ref, inner_ref, edge_ref):
    strips = [grid_ref[i * STRIP : i * STRIP + STRIP, :].astype(F32) for i in range(LAT)]

    def put(ref, at, lats, first, cols):
        part = jnp.concatenate([strips[i][first * 4 : (first + cols) * 4] for i in lats])
        matrix = split_ref if part.shape[0] == WIN else small_ref
        ref[at : at + matrix.shape[0], :] = product(matrix[...], part.astype(BF16)).astype(BF16)

    low, mid, high = range(3), range(3, 9), range(9, 12)
    for q in range(3):
        put(up_ref, q * WIN, low, 6 + 12 * q, 12)
        put(inner_ref, q * BLOCK, range(3, 6), 6 + 12 * q, 12)
        put(inner_ref, q * BLOCK + WIN, range(6, 9), 6 + 12 * q, 12)
        put(edge_ref, WIN + q * WIN, high, 6 + 12 * q, 12)
    put(up_ref, 3 * WIN, low, 42, 6)
    put(side_ref, 0, mid, 0, 6)
    put(side_ref, WIN, high, 0, 6)
    put(corner_ref, 0, low, 0, 6)
    put(edge_ref, 0, mid, 42, 6)
    put(edge_ref, 4 * WIN, high, 42, 6)


def sort_pieces(values):
    return call(
        sort_kernel, "sort_pieces", (),
        [whole(TOKENS, D), whole(WIN, WIN), whole(SMALL, HALF)],
        [whole(n, D) for n in (UP, SIDE, CORNER, INNER, EDGE)],
        shapes(*[(n, D) for n in (UP, SIDE, CORNER, INNER, EDGE)]),
        [], (400000000, 5000000, 0), 24,
    )(values, jnp.asarray(SPLIT, BF16), jnp.asarray(SPLIT_SMALL, BF16))


def order_ids():
    ids = np.arange(TOKENS).reshape(LAT, LON, 2, 2)

    def piece(lats, first, cols):
        part = ids[lats[0] : lats[-1] + 1, first : first + cols].transpose(2, 0, 1, 3).reshape(-1)
        return np.pad(part, (0, WIN - 64 - HALF if part.size == HALF else 0))

    low, mid, high = range(3), range(3, 9), range(9, 12)
    order = [piece(low, 6 + 12 * q, 12) for q in range(3)] + [piece(low, 42, 6), piece(low, 0, 6)]
    order += [piece(mid, 0, 6), piece(mid, 42, 6)]
    for q in range(3):
        order += [piece(range(3, 6), 6 + 12 * q, 12), piece(range(6, 9), 6 + 12 * q, 12)]
    order += [piece(high, 0, 6)]
    order += [piece(high, 6 + 12 * q, 12) for q in range(3)] + [piece(high, 42, 6)]
    return np.concatenate(order)


ORDER = order_ids()
PLACES = UP + SIDE + CORNER + INNER + EDGE


EDGE_BLOCKS = (
    (WIN, lambda i: i),
    (WIN, lambda i: jnp.maximum(i - 1, 0)),
    (WIN, lambda i: i // 4),
    (SMALL, lambda i: 0),
)
EDGE_SPECS = [pl.BlockSpec((n, D), lambda i, at=at: (at(i), 0)) for n, at in EDGE_BLOCKS]
EDGE_PAIRS = [pl.BlockSpec((2, n, D), lambda i, at=at: (0, at(i), 0)) for n, at in EDGE_BLOCKS]


def join_halves(first, second):
    first, second = first.astype(F32), second.astype(F32)
    return jnp.concatenate([first[:HALF], second[:HALF], first[HALF:], second[HALF:]])


def attend(x_all, c_all, bias, w_ref, gain_ref, ow_ref, x_out, ha_ref, dp_ref, packed, slopes):
    x_out[...] = x_all.astype(BF16)
    cot = c_all.astype(BF16)
    dp_ref[:, 3 * D :] = cot
    slopes[...] = product(cot, ow_ref[...], NT).astype(BF16)
    normed, _ = normalise(x_all)
    hidden = (normed * gain_ref[...]).astype(BF16)
    ha_ref[:, :D] = hidden
    for part in range(3):
        cols = slice(part * D, part * D + D)
        packed[:, cols] = product(hidden, w_ref[:, cols]).astype(BF16)
    lane = lax.broadcasted_iota(I32, (1, QUAD), 1)
    sides = [jnp.where((lane >= 64 * n) & (lane < 64 * n + 64), 1.0, 0.0) for n in range(4)]
    low_sides = [side.astype(BF16) for side in sides]

    def spread(values):
        return jnp.concatenate([values * side for side in low_sides])

    def gather(matrix, values):
        parts = product(matrix, values, TN)
        return sum(parts[n * WIN : n * WIN + WIN] * side for n, side in enumerate(sides))

    for window in range(2):
        rows = slice(window * WIN, window * WIN + WIN)
        for quad in range(2):
            spot = [slice(part * D + quad * QUAD, part * D + quad * QUAD + QUAD) for part in range(3)]
            queries, keys, values = (packed[rows, cols] for cols in spot)
            queries, grads = spread(queries), spread(slopes[rows, spot[0]])
            scores = product(keys, queries, NT) * (SCALE * LOG2E)
            if bias is not None:
                scores = scores + bias()
            grown = jnp.exp2(scores - jnp.max(scores, 0, keepdims=True))
            probs = grown * (1.0 / jnp.sum(grown, 0, keepdims=True))
            low = probs.astype(BF16)
            weighted = probs * product(values, grads, NT)
            slope = weighted - probs * jnp.sum(weighted, 0, keepdims=True)
            slope = (slope * SCALE).astype(BF16)
            ha_ref[rows, slice(D + quad * QUAD, D + quad * QUAD + QUAD)] = gather(low, values).astype(BF16)
            dp_ref[rows, spot[0]] = gather(slope, keys).astype(BF16)
            dp_ref[rows, spot[1]] = product(slope, queries).astype(BF16)
            dp_ref[rows, spot[2]] = product(low, grads).astype(BF16)


def inner_kernel(x_ref, c_ref, *refs):
    x_all = join_halves(x_ref[:WIN, :], x_ref[WIN:, :])
    c_all = join_halves(c_ref[:WIN, :], c_ref[WIN:, :])
    attend(x_all, c_all, None, *refs)


def edge_kernel(flag_ref, xe, xu, xs, xc, ce, cu, cs, cc, join_ref, apart_ref, *refs):
    weights, (*refs, x_all, c_all) = refs[:3], refs[6:]
    step = pl.program_id(0)

    @pl.when(step == 0)
    def _():
        x_all[...] = join_halves(xe[...], xs[...])
        c_all[...] = join_halves(ce[...], cs[...])

    @pl.when((step > 0) & (step < 4))
    def _():
        x_all[...] = join_halves(xe[...], xu[...])
        c_all[...] = join_halves(ce[...], cu[...])

    @pl.when(step == 4)
    def _():
        parts = [xe[:SMALL, :], xs[:SMALL, :], xu[:SMALL, :], xc[...]]
        x_all[...] = product(join_ref[...], jnp.concatenate(parts))
        parts = [ce[:SMALL, :], cs[:SMALL, :], cu[:SMALL, :], cc[...]]
        c_all[...] = product(join_ref[...], jnp.concatenate(parts))

    seam = jnp.where(step > 0, flag_ref[0], 0).astype(F32)
    attend(x_all[...], c_all[...], lambda: apart_ref[...] * seam, *weights, *refs)


def attend_specs(rows, skip):
    widths = (D, 2 * D, 4 * D)
    outs = [pl.BlockSpec((BLOCK, n), lambda i: (i + skip, 0)) for n in widths]
    out_shapes = shapes(*[(TOKENS, n) for n in widths])
    scratch = [pltpu.VMEM((BLOCK, 3 * D), BF16), pltpu.VMEM((BLOCK, D), BF16)]
    cost = (rows * 6000000, rows * 10000, rows * 1200)
    return outs, out_shapes, scratch, cost


WEIGHTS = [(D, 3 * D), (1, D), (D, D)]


def attend_inner(x, cot, weights):
    outs, out_shapes, scratch, cost = attend_specs(INNER, 0)
    return call(
        inner_kernel, "attend_inner", (3,),
        [blocks(BLOCK, D)] * 2 + [whole(*dim) for dim in WEIGHTS],
        outs, out_shapes, scratch, cost, 18,
    )(x, cot, *weights)


def apart_matrix():
    late = np.arange(WIN) >= HALF
    return np.tile(np.where(late[:, None] != late[None, :], FAR, 0.0).astype(np.float32), (1, 4))


def attend_edge(x_parts, c_parts, flag, weights, carried):
    outs, out_shapes, scratch, cost = attend_specs(5 * BLOCK, 3)
    return call(
        edge_kernel, "attend_edge", (5,),
        [pl.BlockSpec(memory_space=pltpu.SMEM)]
        + EDGE_SPECS * 2
        + [whole(BLOCK, 4 * SMALL), whole(WIN, 4 * WIN)]
        + [whole(*dim) for dim in WEIGHTS]
        + [pl.BlockSpec(memory_space=pl.ANY)] * 3,
        outs, out_shapes, scratch + [pltpu.VMEM((BLOCK, D), F32)] * 2, cost, 24,
        aliases={14 + n: n for n in range(3)},
    )(flag, *x_parts, *c_parts, jnp.asarray(CORNER_JOIN, BF16), jnp.asarray(apart_matrix()), *weights, *carried)


def weight_kernel(core_ref, left_ref, right_ref, own_ref, away_ref, turned):
    for c in range(4):
        side, cols = slice(c // 3 * D, c // 3 * D + D), slice(c * D, c * D + D)
        chunk = product(left_ref[:, side], right_ref[:, cols], TN).reshape(64, 8, D)
        half = c % 2 * 4
        turned[:, 0, c // 2, half : half + 4] = chunk[:, :4]
        turned[:, 1, c // 2, half : half + 4] = chunk[:, 4:]
    core = core_ref[0]
    for at in range(BANDS // 2):
        for ref, which in ((own_ref, core), (away_ref, 1 - core)):
            part = turned[pl.ds(at * 8 + which * 4, 4)].reshape(128, D)
            ref[at * 128 : at * 128 + 128, :] = part.astype(ref.dtype)


def weight_terms(core, left, right):
    return call(
        weight_kernel, "weight_terms", (),
        [pl.BlockSpec(memory_space=pltpu.SMEM), whole(TOKENS, 2 * D), whole(TOKENS, 4 * D)],
        [whole(1024, D)] * 2,
        [jax.ShapeDtypeStruct((1024, D), F32), jax.ShapeDtypeStruct((1024, D), BF16)],
        [pltpu.VMEM((64, 2, 2, 8, D), F32)],
        (1000, 1000, 0), 22,
    )(core, left, right)


def add_kernel(own_ref, got_ref, out_ref):
    out_ref[...] = (own_ref[...] + got_ref[...].astype(F32)).astype(BF16)


def add_halves(own, got):
    return call(
        add_kernel, "add_halves", (4,),
        [blocks(256, D)] * 2, blocks(256, D), shapes((1024, D))[0], [],
        (1000000, 4000000, 0), 10,
    )(own, got)


def finished(x_ref, att_ref, dp_ref, w_ref, gain_ref, ow_ref):
    x = x_ref[...].astype(F32)
    out = x + product(att_ref[...], ow_ref[...])
    normed, inverse = normalise(x)
    hidden = product(dp_ref[:, : 3 * D], w_ref[...], NT) * gain_ref[...]
    hidden = (
        hidden
        - jnp.mean(hidden, -1, keepdims=True)
        - normed * jnp.mean(hidden * normed, -1, keepdims=True)
    )
    grad = dp_ref[:, 3 * D :].astype(F32) + inverse * hidden
    return out, grad


def grid_pieces(split_ref, values):
    first = jnp.concatenate([values[:HALF], values[WIN : WIN + HALF]]).astype(BF16)
    second = jnp.concatenate([values[HALF:WIN], values[WIN + HALF :]]).astype(BF16)
    return [product(split_ref[...], part, TN).astype(BF16) for part in (first, second)]


def finish_inner_kernel(split_ref, *refs):
    *refs, inner = refs
    for n, values in enumerate(finished(*refs)):
        first, second = grid_pieces(split_ref, values)
        inner[n, :WIN, :] = first
        inner[n, WIN:, :] = second


def finish_edge_kernel(split_ref, back_ref, *refs):
    refs, (edge, up, side, corner) = refs[:6], refs[6:]
    step = pl.program_id(0)
    for n, values in enumerate(finished(*refs)):

        @pl.when(step < 4)
        def _(n=n, values=values):
            first, second = grid_pieces(split_ref, values)
            edge[n] = first

            @pl.when(step == 0)
            def _():
                side[n] = second

            @pl.when(step > 0)
            def _():
                up[n] = second

        @pl.when(step == 4)
        def _(n=n, values=values):
            parts = product(back_ref[...], values.astype(BF16)).astype(BF16)
            edge[n, :SMALL, :] = parts[:SMALL]
            side[n, :SMALL, :] = parts[SMALL : 2 * SMALL]
            up[n, :SMALL, :] = parts[2 * SMALL : 3 * SMALL]
            corner[n] = parts[3 * SMALL :]


PIECES = (INNER, EDGE, UP, SIDE, CORNER)


def finish_specs(skip):
    row = lambda width, col: pl.BlockSpec((BLOCK, width), lambda i: (i + skip, col))
    return [row(D, 0), row(D, 1), row(4 * D, 0)] + [whole(*dim) for dim in WEIGHTS]


def finish_cost(rows):
    return rows * 2200000, rows * 9000, rows


def finish_inner(values, weights):
    return call(
        finish_inner_kernel, "finish_inner", (3,),
        [whole(WIN, WIN)] + finish_specs(0),
        pl.BlockSpec((2, BLOCK, D), lambda i: (0, i, 0)), shapes((2, INNER, D))[0], [],
        (1000, 1000, 0), 20,
    )(jnp.asarray(SPLIT, BF16), *values, *weights)


def finish_edge(values, weights):
    return call(
        finish_edge_kernel, "finish_edge", (5,),
        [whole(WIN, WIN), whole(4 * SMALL, BLOCK)] + finish_specs(3),
        EDGE_PAIRS, shapes(*[(2, n, D) for n in PIECES[1:]]), [],
        finish_cost(5 * BLOCK), 24,
    )(jnp.asarray(SPLIT, BF16), jnp.asarray(CORNER_BACK, BF16), *values, *weights)


def join_kernel(inner, edge, up, side, corner, *outs):
    run, stub = 48, 24

    def load(ref, n, at, count):
        return ref[n, at : at + count, :].astype(F32)

    for zone in range(3):

        @pl.when((pl.program_id(0) + 1) // 2 == zone)
        def _(zone=zone):
            for n, out_ref in enumerate(outs):
                if zone == 1:
                    half = pl.program_id(0) - 1
                    left = load(side, n, 0, WIN)
                    right = load(edge, n, 0, WIN)
                    left, right = (jnp.where(half == 0, v[:HALF], v[HALF:]) for v in (left, right))
                    full = []
                    for q in range(3):
                        at = pl.multiple_of(q * BLOCK + half * WIN, 16)
                        full.append(inner[n, pl.ds(at, WIN), :].astype(F32))
                elif zone == 0:
                    left, right = load(corner, n, 0, SMALL), load(up, n, 3 * WIN, SMALL)
                    full = [load(up, n, q * WIN, WIN) for q in range(3)]
                else:
                    left, right = load(side, n, WIN, SMALL), load(edge, n, 4 * WIN, SMALL)
                    full = [load(edge, n, WIN + q * WIN, WIN) for q in range(3)]
                for i in range(3):
                    parts = [left[i * stub : i * stub + stub]]
                    parts += [part[i * run : i * run + run] for part in full]
                    parts.append(right[i * stub : i * stub + stub])
                    strip = jnp.concatenate(parts)
                    out_ref[i] = strip.reshape(LON, LEV, D).astype(BF16)


def join(parts):
    spec = pl.BlockSpec((3, LON, LEV, D), lambda i: (i, 0, 0, 0))
    dim = (LAT, LON, LEV, D)
    return call(
        join_kernel, "join", (4,),
        [whole(2, n, D) for n in PIECES],
        [spec] * 2, shapes(*[dim] * 2), [],
        (1000000, 9000000, 0), 26,
    )(*parts)


def sum_kernel(terms_ref, qkv_ref, out_ref):
    total = jnp.sum(terms_ref[...].astype(F32).reshape(DEVICES // 2, 16, D), 0)
    for c in range(3):
        qkv_ref[:, c * D : c * D + D] = total[4 * c : 4 * c + 4]
    out_ref[...] = total[12:]


def sum_terms(terms):
    return call(
        sum_kernel, "sum_terms", (),
        [whole(1024, D)], [whole(4, 3 * D), whole(4, D)],
        shapes((4, 3 * D), (4, D), dtype=F32), [], (2000000, 2200000, 0), 20,
    )(terms)


def shift_pairs(lat_step, lon_step):
    return [
        (a * SECTORS + b, (a + lat_step) % BANDS * SECTORS + (b + lon_step) % SECTORS)
        for a in range(BANDS)
        for b in range(SECTORS)
    ]


def exchange(parts, sign):
    steps = ((sign, 0), (0, sign), (sign, sign))
    return [lax.ppermute(part, BOTH, shift_pairs(*step)) for part, step in zip(parts, steps)]


def swap_blocks(values, axis, groups=None):
    return lax.all_to_all(
        values, axis, split_axis=0, concat_axis=0, axis_index_groups=groups, tiled=True
    )


SAME_CORE = [
    [a * SECTORS + b for a in range(core, BANDS, 2) for b in range(SECTORS)] for core in range(2)
]
OTHER_CORE = [(d, d ^ SECTORS) for d in range(DEVICES)]


def per_device(buffer, fetch_owner, fetch_slot, norm_gain, qkv_weight, out_weight, out_grad):
    weights = (qkv_weight, norm_gain.reshape(1, D), out_weight)
    lists, place, table = make_requests(fetch_owner.reshape(1, TOKENS), fetch_slot.reshape(1, TOKENS))
    lists = swap_blocks(lists, "lat")
    replies = swap_blocks(serve(lists.T, buffer).reshape(BANDS, CAP, D), "lat")
    replies = replies.reshape(BANDS * CAP, D)

    c_up, c_side, c_corner, c_inner, c_edge = sort_pieces(out_grad.reshape(TOKENS, D))
    c_parts = [c_edge] + exchange([c_up, c_side, c_corner], -1)
    place = place.reshape(TOKENS)[ORDER].reshape(-1, 1)

    x_up, x_side, x_corner, x_inner, x_edge = pick(table, place, replies)
    x_parts = [x_edge] + exchange([x_up, x_side, x_corner], -1)

    band = lax.axis_index("lat")
    flag = (band == BANDS - 1).astype(I32).reshape(1)
    core = (band % 2).astype(I32).reshape(1)
    first = attend_inner(x_inner, c_inner, weights)
    x, left, right = attend_edge(x_parts, c_parts, flag, weights, first)
    edge, *away = finish_edge((x, left, right), weights)
    returned = exchange(away, 1)
    left, right, edge = lax.optimization_barrier((left, right, edge))
    own, away = weight_terms(core, left, right)
    got = lax.ppermute(away, BOTH, OTHER_CORE)
    inner = finish_inner((x, left, right), weights)
    got, inner = lax.optimization_barrier((got, inner))
    terms = swap_blocks(add_halves(own, got), BOTH, SAME_CORE)
    outs = join([inner, edge] + returned)
    return (*outs, *sum_terms(terms))


def solution(mesh):
    return jax.shard_map(
        per_device,
        mesh=mesh,
        in_specs=(
            P(BOTH, None),
            P("lat", "lon", None, None),
            P("lat", "lon", None),
            P(),
            P(),
            P(),
            P("lat", "lon", None, None),
        ),
        out_specs=(
            P("lat", "lon", None, None),
            P("lat", "lon", None, None),
            P(BOTH, None),
            P(BOTH, None),
        ),
        check_vma=False,
    )
```

```python
import functools
import jax
import jax.numpy as jnp
import numpy as np
from jax import lax
from jax.experimental import pallas as pl
from jax.experimental.pallas import tpu as pltpu
from jax.sharding import PartitionSpec as P

NN = (((1,), (0,)), ((), ()))
NT = (((1,), (1,)), ((), ()))
TN = (((0,), (0,)), ((), ()))
F32 = jnp.float32
BF16 = jnp.bfloat16
I32 = jnp.int32
D = 512
BANDS, SECTORS = 16, 8
DEVICES = BANDS * SECTORS
LAT, LON, LEV = 12, 48, 4
TOKENS = LAT * LON * LEV
STRIP = LON * LEV
ROWS = 1152
CAP = 288
WIN = 144
HALF = 72
SMALL = 80
BLOCK = 2 * WIN
QUAD = 256
SCALE = 0.125
LOG2E = 1.4426950408889634
FAR = -1e30
BOTH = ("lat", "lon")

UP, SIDE, CORNER = 3 * WIN + SMALL, WIN + SMALL, SMALL
INNER, EDGE = 6 * WIN, 4 * WIN + SMALL


def split_matrix(places, rows):
    matrix = np.zeros((rows, places * 4), np.float32)
    for place in range(places):
        for level in range(4):
            matrix[(level // 2) * places * 2 + place * 2 + level % 2, place * 4 + level] = 1
    return matrix


SPLIT = split_matrix(36, WIN)
SPLIT_SMALL = split_matrix(18, SMALL)


def corner_matrix():
    matrix = np.zeros((BLOCK, 4 * SMALL), np.float32)
    for r in range(2):
        for part in range(4):
            for at in range(36):
                matrix[r * WIN + part * 36 + at, part * SMALL + r * 36 + at] = 1
    return matrix


CORNER_JOIN = corner_matrix()


def corner_back():
    matrix = np.zeros((4 * SMALL, BLOCK), np.float32)
    for part in range(4):
        split = CORNER_JOIN[:, part * SMALL : part * SMALL + HALF]
        matrix[part * SMALL : part * SMALL + HALF] = SPLIT_SMALL[:HALF].T @ split.T
    return matrix


CORNER_BACK = corner_back()


def product(left, right, form=NN):
    return lax.dot_general(left, right, form, preferred_element_type=F32)


def normalise(values):
    centred = values - jnp.mean(values, -1, keepdims=True)
    inverse = lax.rsqrt(jnp.mean(centred * centred, -1, keepdims=True) + 1e-5)
    return centred * inverse, inverse


def whole(*shape):
    return pl.BlockSpec(shape, lambda *i: (0,) * len(shape))


def blocks(rows, width):
    return pl.BlockSpec((rows, width), lambda i: (i, 0))


def shapes(*dims, dtype=BF16):
    return [jax.ShapeDtypeStruct(dim, dtype) for dim in dims]


def call(kernel, name, grid, ins, outs, out_shapes, scratch, cost, vmem, aliases={}):
    flops, moved, exps = cost
    return pl.pallas_call(
        kernel,
        grid=grid,
        in_specs=ins,
        out_specs=outs,
        out_shape=out_shapes,
        scratch_shapes=scratch,
        input_output_aliases=aliases,
        compiler_params=pltpu.CompilerParams(vmem_limit_bytes=vmem * 2**20),
        cost_estimate=pl.CostEstimate(flops=flops, bytes_accessed=moved, transcendentals=exps),
        name=name,
    )


ZONES = (0, 3, 9, 12)
GROUP = 16
COMPACT = [(b - a) * STRIP + BANDS * 2 * (GROUP - 1) for a, b in zip(ZONES, ZONES[1:])]


def request_kernel(owner_ref, slot_ref, lists_ref, place_ref, table_ref, hits, ranks):
    owner = owner_ref[...]
    slot = slot_ref[...]
    hit = owner == lax.broadcasted_iota(I32, (BANDS, TOKENS), 0)
    hits[...] = hit.astype(F32)
    step = STRIP
    row = lax.broadcasted_iota(I32, (step, step), 0)
    triangle = (row <= lax.broadcasted_iota(I32, (step, step), 1)).astype(F32).astype(BF16)
    row = lax.broadcasted_iota(I32, (BANDS, BANDS), 0)
    earlier = (lax.broadcasted_iota(I32, (BANDS, BANDS), 1) < row).astype(F32).astype(BF16)
    before = jnp.zeros((BANDS, 1), F32)
    columns = []
    for zone in range(3):
        first = before
        strips = range(ZONES[zone], ZONES[zone + 1])
        for strip in strips:
            spot = slice(strip * step, strip * step + step)
            part = hits[:, spot]
            count = product(part.astype(BF16), triangle) + before
            ranks[:, spot] = jnp.sum(part * count, 0, keepdims=True) - 1.0
            before = before + jnp.sum(part, 1, keepdims=True)
        start = jnp.floor(first * (1.0 / GROUP))
        groups = jnp.floor((before + (GROUP - 1)) * (1.0 / GROUP)) - start
        groups = jnp.where(before > first, groups, 0.0)
        base = product(earlier, jnp.broadcast_to(groups, (BANDS, 128)).astype(BF16))[:, :1]
        shift = (base - start) * GROUP
        for strip in strips:
            spot = slice(strip * step, strip * step + step)
            moved = jnp.sum(hits[:, spot] * shift, 0, keepdims=True)
            place_ref[:, spot] = (ranks[:, spot] + moved).astype(I32)
        columns += [start, groups]
    columns += [jnp.zeros((BANDS, 2), F32)]
    table_ref[...] = jnp.concatenate(columns, 1).astype(I32)
    rank = ranks[...]
    high = jnp.where(hit, lax.shift_right_logical(slot, 5), 0).astype(F32).astype(BF16)
    low = jnp.where(hit, slot & 31, 0).astype(F32).astype(BF16)
    chosen = rank == lax.broadcasted_iota(I32, (CAP, TOKENS), 0).astype(F32)
    chosen = jnp.where(chosen, 1.0, 0.0).astype(BF16)
    found = product(high, chosen, NT) * 32.0 + product(low, chosen, NT)
    lists_ref[...] = found.astype(I32).reshape(BANDS, 1, CAP)


def make_requests(owners, slots):
    return call(
        request_kernel, "requests", (),
        [whole(1, TOKENS)] * 2,
        [whole(BANDS, 1, CAP), whole(1, TOKENS), whole(BANDS, 8)],
        shapes((BANDS, 1, CAP), (1, TOKENS), (BANDS, 8), dtype=I32),
        [pltpu.VMEM((BANDS, TOKENS), F32), pltpu.VMEM((1, TOKENS), F32)],
        (100000000, 100000, 0), 62,
    )(owners, slots)


ASKERS = 4


def serve_kernel(lists_ref, buffer_ref, out_ref):
    for at in range(ASKERS):
        row = jnp.broadcast_to(lists_ref[at].astype(F32), (8, CAP))
        wanted = row.T[:, :1].astype(I32)
        for half in range(2):
            chosen = wanted[half * 144 : half * 144 + 144] == lax.broadcasted_iota(I32, (144, ROWS), 1)
            chosen = jnp.where(chosen, 1.0, 0.0).astype(BF16)
            rows = slice(at * CAP + half * 144, at * CAP + half * 144 + 144)
            out_ref[rows, :] = product(chosen, buffer_ref[...]).astype(BF16)


def serve(lists, buffer):
    return call(
        serve_kernel, "serve", (BANDS // ASKERS,),
        [pl.BlockSpec((ASKERS, 1, CAP), lambda i: (i, 0, 0)), whole(ROWS, D)],
        blocks(ASKERS * CAP, D),
        shapes((BANDS * CAP, D))[0],
        [], (5400000000, 6000000, 0), 60,
    )(lists, buffer)


def pick_kernel(table_ref, place_ref, replies_ref, up_ref, side_ref, corner_ref, inner_ref, edge_ref, compact):
    compact[...] = jnp.zeros_like(compact)
    firsts = (0, UP + CORNER, UP + CORNER + 2 * WIN + INNER)
    for zone, size in enumerate(COMPACT):
        filled = 0
        for owner in range(BANDS):
            start = owner * CAP + table_ref[owner, 2 * zone] * GROUP
            groups = table_ref[owner, 2 * zone + 1]

            def move(at, filled, start=start):
                source = pl.multiple_of(start + at * GROUP, GROUP)
                target = pl.multiple_of(filled, GROUP)
                compact[pl.ds(target, GROUP), :] = replies_ref[pl.ds(source, GROUP), :]
                return filled + GROUP

            filled = lax.fori_loop(0, groups, move, filled)

        def find(first, count, size=size):
            place = place_ref[first : first + count, :]
            chosen = place == lax.broadcasted_iota(I32, (count, size), 1)
            chosen = jnp.where(chosen, 1.0, 0.0).astype(BF16)
            return product(chosen, compact[:size, :]).astype(BF16)

        first = firsts[zone]
        if zone == 0:
            found = find(first, UP + CORNER)
            up_ref[...] = found[:UP]
            corner_ref[...] = found[UP:]
        elif zone == 1:
            found = find(first, 2 * WIN + INNER)
            side_ref[:WIN, :] = found[:WIN]
            edge_ref[:WIN, :] = found[WIN : 2 * WIN]
            inner_ref[...] = found[2 * WIN :]
        else:
            found = find(first, SMALL + EDGE - WIN)
            side_ref[WIN:, :] = found[:SMALL]
            edge_ref[WIN:, :] = found[SMALL:]


def pick(table, place, replies):
    return call(
        pick_kernel, "pick", (),
        [pl.BlockSpec(memory_space=pltpu.SMEM), whole(PLACES, 1), whole(BANDS * CAP, D)],
        [whole(n, D) for n in (UP, SIDE, CORNER, INNER, EDGE)],
        shapes(*[(n, D) for n in (UP, SIDE, CORNER, INNER, EDGE)]),
        [pltpu.VMEM((max(COMPACT), D), BF16)], (3600000000, 8000000, 0), 60,
    )(table, place, replies)


def sort_kernel(grid_ref, split_ref, small_ref, up_ref, side_ref, corner_ref, inner_ref, edge_ref):
    strips = [grid_ref[i * STRIP : i * STRIP + STRIP, :].astype(F32) for i in range(LAT)]

    def put(ref, at, lats, first, cols):
        part = jnp.concatenate([strips[i][first * 4 : (first + cols) * 4] for i in lats])
        matrix = split_ref if part.shape[0] == WIN else small_ref
        ref[at : at + matrix.shape[0], :] = product(matrix[...], part.astype(BF16)).astype(BF16)

    low, mid, high = range(3), range(3, 9), range(9, 12)
    for q in range(3):
        put(up_ref, q * WIN, low, 6 + 12 * q, 12)
        put(inner_ref, q * BLOCK, range(3, 6), 6 + 12 * q, 12)
        put(inner_ref, q * BLOCK + WIN, range(6, 9), 6 + 12 * q, 12)
        put(edge_ref, WIN + q * WIN, high, 6 + 12 * q, 12)
    put(up_ref, 3 * WIN, low, 42, 6)
    put(side_ref, 0, mid, 0, 6)
    put(side_ref, WIN, high, 0, 6)
    put(corner_ref, 0, low, 0, 6)
    put(edge_ref, 0, mid, 42, 6)
    put(edge_ref, 4 * WIN, high, 42, 6)


def sort_pieces(values):
    return call(
        sort_kernel, "sort_pieces", (),
        [whole(TOKENS, D), whole(WIN, WIN), whole(SMALL, HALF)],
        [whole(n, D) for n in (UP, SIDE, CORNER, INNER, EDGE)],
        shapes(*[(n, D) for n in (UP, SIDE, CORNER, INNER, EDGE)]),
        [], (400000000, 5000000, 0), 24,
    )(values, jnp.asarray(SPLIT, BF16), jnp.asarray(SPLIT_SMALL, BF16))


def order_ids():
    ids = np.arange(TOKENS).reshape(LAT, LON, 2, 2)

    def piece(lats, first, cols):
        part = ids[lats[0] : lats[-1] + 1, first : first + cols].transpose(2, 0, 1, 3).reshape(-1)
        return np.pad(part, (0, WIN - 64 - HALF if part.size == HALF else 0))

    low, mid, high = range(3), range(3, 9), range(9, 12)
    order = [piece(low, 6 + 12 * q, 12) for q in range(3)] + [piece(low, 42, 6), piece(low, 0, 6)]
    order += [piece(mid, 0, 6), piece(mid, 42, 6)]
    for q in range(3):
        order += [piece(range(3, 6), 6 + 12 * q, 12), piece(range(6, 9), 6 + 12 * q, 12)]
    order += [piece(high, 0, 6)]
    order += [piece(high, 6 + 12 * q, 12) for q in range(3)] + [piece(high, 42, 6)]
    return np.concatenate(order)


ORDER = order_ids()
PLACES = UP + SIDE + CORNER + INNER + EDGE


EDGE_BLOCKS = (
    (WIN, lambda i: i),
    (WIN, lambda i: jnp.maximum(i - 1, 0)),
    (WIN, lambda i: i // 4),
    (SMALL, lambda i: 0),
)
EDGE_SPECS = [pl.BlockSpec((n, D), lambda i, at=at: (at(i), 0)) for n, at in EDGE_BLOCKS]
EDGE_PAIRS = [pl.BlockSpec((2, n, D), lambda i, at=at: (0, at(i), 0)) for n, at in EDGE_BLOCKS]


def join_halves(first, second):
    first, second = first.astype(F32), second.astype(F32)
    return jnp.concatenate([first[:HALF], second[:HALF], first[HALF:], second[HALF:]])


def attend(x_all, c_all, bias, w_ref, gain_ref, ow_ref, x_out, ha_ref, dp_ref, packed, slopes):
    x_out[...] = x_all.astype(BF16)
    cot = c_all.astype(BF16)
    dp_ref[:, 3 * D :] = cot
    slopes[...] = product(cot, ow_ref[...], NT).astype(BF16)
    normed, _ = normalise(x_all)
    hidden = (normed * gain_ref[...]).astype(BF16)
    ha_ref[:, :D] = hidden
    for part in range(3):
        cols = slice(part * D, part * D + D)
        packed[:, cols] = product(hidden, w_ref[:, cols]).astype(BF16)
    lane = lax.broadcasted_iota(I32, (1, QUAD), 1)
    sides = [jnp.where((lane >= 64 * n) & (lane < 64 * n + 64), 1.0, 0.0) for n in range(4)]
    low_sides = [side.astype(BF16) for side in sides]

    def spread(values):
        return jnp.concatenate([values * side for side in low_sides])

    def gather(matrix, values):
        parts = product(matrix, values, TN)
        return sum(parts[n * WIN : n * WIN + WIN] * side for n, side in enumerate(sides))

    for window in range(2):
        rows = slice(window * WIN, window * WIN + WIN)
        for quad in range(2):
            spot = [slice(part * D + quad * QUAD, part * D + quad * QUAD + QUAD) for part in range(3)]
            queries, keys, values = (packed[rows, cols] for cols in spot)
            queries, grads = spread(queries), spread(slopes[rows, spot[0]])
            scores = product(keys, queries, NT) * (SCALE * LOG2E)
            if bias is not None:
                scores = scores + bias()
            grown = jnp.exp2(scores - jnp.max(scores, 0, keepdims=True))
            probs = grown * (1.0 / jnp.sum(grown, 0, keepdims=True))
            low = probs.astype(BF16)
            weighted = probs * product(values, grads, NT)
            slope = weighted - probs * jnp.sum(weighted, 0, keepdims=True)
            slope = (slope * SCALE).astype(BF16)
            ha_ref[rows, slice(D + quad * QUAD, D + quad * QUAD + QUAD)] = gather(low, values).astype(BF16)
            dp_ref[rows, spot[0]] = gather(slope, keys).astype(BF16)
            dp_ref[rows, spot[1]] = product(slope, queries).astype(BF16)
            dp_ref[rows, spot[2]] = product(low, grads).astype(BF16)


def inner_kernel(x_ref, c_ref, *refs):
    x_all = join_halves(x_ref[:WIN, :], x_ref[WIN:, :])
    c_all = join_halves(c_ref[:WIN, :], c_ref[WIN:, :])
    attend(x_all, c_all, None, *refs)


def edge_kernel(flag_ref, xe, xu, xs, xc, ce, cu, cs, cc, join_ref, apart_ref, *refs):
    weights, (*refs, x_all, c_all) = refs[:3], refs[6:]
    step = pl.program_id(0)

    @pl.when(step == 0)
    def _():
        x_all[...] = join_halves(xe[...], xs[...])
        c_all[...] = join_halves(ce[...], cs[...])

    @pl.when((step > 0) & (step < 4))
    def _():
        x_all[...] = join_halves(xe[...], xu[...])
        c_all[...] = join_halves(ce[...], cu[...])

    @pl.when(step == 4)
    def _():
        parts = [xe[:SMALL, :], xs[:SMALL, :], xu[:SMALL, :], xc[...]]
        x_all[...] = product(join_ref[...], jnp.concatenate(parts))
        parts = [ce[:SMALL, :], cs[:SMALL, :], cu[:SMALL, :], cc[...]]
        c_all[...] = product(join_ref[...], jnp.concatenate(parts))

    seam = jnp.where(step > 0, flag_ref[0], 0).astype(F32)
    attend(x_all[...], c_all[...], lambda: apart_ref[...] * seam, *weights, *refs)


def attend_specs(rows, skip):
    widths = (D, 2 * D, 4 * D)
    outs = [pl.BlockSpec((BLOCK, n), lambda i: (i + skip, 0)) for n in widths]
    out_shapes = shapes(*[(TOKENS, n) for n in widths])
    scratch = [pltpu.VMEM((BLOCK, 3 * D), BF16), pltpu.VMEM((BLOCK, D), BF16)]
    cost = (rows * 6000000, rows * 10000, rows * 1200)
    return outs, out_shapes, scratch, cost


WEIGHTS = [(D, 3 * D), (1, D), (D, D)]


def attend_inner(x, cot, weights):
    outs, out_shapes, scratch, cost = attend_specs(INNER, 0)
    return call(
        inner_kernel, "attend_inner", (3,),
        [blocks(BLOCK, D)] * 2 + [whole(*dim) for dim in WEIGHTS],
        outs, out_shapes, scratch, cost, 18,
    )(x, cot, *weights)


def apart_matrix():
    late = np.arange(WIN) >= HALF
    return np.tile(np.where(late[:, None] != late[None, :], FAR, 0.0).astype(np.float32), (1, 4))


def attend_edge(x_parts, c_parts, flag, weights, carried):
    outs, out_shapes, scratch, cost = attend_specs(5 * BLOCK, 3)
    return call(
        edge_kernel, "attend_edge", (5,),
        [pl.BlockSpec(memory_space=pltpu.SMEM)]
        + EDGE_SPECS * 2
        + [whole(BLOCK, 4 * SMALL), whole(WIN, 4 * WIN)]
        + [whole(*dim) for dim in WEIGHTS]
        + [pl.BlockSpec(memory_space=pl.ANY)] * 3,
        outs, out_shapes, scratch + [pltpu.VMEM((BLOCK, D), F32)] * 2, cost, 24,
        aliases={14 + n: n for n in range(3)},
    )(flag, *x_parts, *c_parts, jnp.asarray(CORNER_JOIN, BF16), jnp.asarray(apart_matrix()), *weights, *carried)


def weight_kernel(core_ref, left_ref, right_ref, own_ref, away_ref, turned):
    for c in range(4):
        side, cols = slice(c // 3 * D, c // 3 * D + D), slice(c * D, c * D + D)
        chunk = product(left_ref[:, side], right_ref[:, cols], TN).reshape(64, 8, D)
        half = c % 2 * 4
        turned[:, 0, c // 2, half : half + 4] = chunk[:, :4]
        turned[:, 1, c // 2, half : half + 4] = chunk[:, 4:]
    core = core_ref[0]
    for at in range(BANDS // 2):
        for ref, which in ((own_ref, core), (away_ref, 1 - core)):
            part = turned[pl.ds(at * 8 + which * 4, 4)].reshape(128, D)
            ref[at * 128 : at * 128 + 128, :] = part.astype(ref.dtype)


def weight_terms(core, left, right):
    return call(
        weight_kernel, "weight_terms", (),
        [pl.BlockSpec(memory_space=pltpu.SMEM), whole(TOKENS, 2 * D), whole(TOKENS, 4 * D)],
        [whole(1024, D)] * 2,
        [jax.ShapeDtypeStruct((1024, D), F32), jax.ShapeDtypeStruct((1024, D), BF16)],
        [pltpu.VMEM((64, 2, 2, 8, D), F32)],
        (1000, 1000, 0), 22,
    )(core, left, right)


def add_kernel(own_ref, got_ref, out_ref):
    out_ref[...] = (own_ref[...] + got_ref[...].astype(F32)).astype(BF16)


def add_halves(own, got):
    return call(
        add_kernel, "add_halves", (4,),
        [blocks(256, D)] * 2, blocks(256, D), shapes((1024, D))[0], [],
        (1000000, 4000000, 0), 10,
    )(own, got)


def finished(x_ref, att_ref, dp_ref, w_ref, gain_ref, ow_ref):
    x = x_ref[...].astype(F32)
    out = x + product(att_ref[...], ow_ref[...])
    normed, inverse = normalise(x)
    hidden = product(dp_ref[:, : 3 * D], w_ref[...], NT) * gain_ref[...]
    hidden = (
        hidden
        - jnp.mean(hidden, -1, keepdims=True)
        - normed * jnp.mean(hidden * normed, -1, keepdims=True)
    )
    grad = dp_ref[:, 3 * D :].astype(F32) + inverse * hidden
    return out, grad


def grid_pieces(split_ref, values):
    first = jnp.concatenate([values[:HALF], values[WIN : WIN + HALF]]).astype(BF16)
    second = jnp.concatenate([values[HALF:WIN], values[WIN + HALF :]]).astype(BF16)
    return [product(split_ref[...], part, TN).astype(BF16) for part in (first, second)]


def finish_inner_kernel(split_ref, *refs):
    *refs, inner = refs
    for n, values in enumerate(finished(*refs)):
        first, second = grid_pieces(split_ref, values)
        inner[n, :WIN, :] = first
        inner[n, WIN:, :] = second


def finish_edge_kernel(split_ref, back_ref, *refs):
    refs, (edge, up, side, corner) = refs[:6], refs[6:]
    step = pl.program_id(0)
    for n, values in enumerate(finished(*refs)):

        @pl.when(step < 4)
        def _(n=n, values=values):
            first, second = grid_pieces(split_ref, values)
            edge[n] = first

            @pl.when(step == 0)
            def _():
                side[n] = second

            @pl.when(step > 0)
            def _():
                up[n] = second

        @pl.when(step == 4)
        def _(n=n, values=values):
            parts = product(back_ref[...], values.astype(BF16)).astype(BF16)
            edge[n, :SMALL, :] = parts[:SMALL]
            side[n, :SMALL, :] = parts[SMALL : 2 * SMALL]
            up[n, :SMALL, :] = parts[2 * SMALL : 3 * SMALL]
            corner[n] = parts[3 * SMALL :]


PIECES = (INNER, EDGE, UP, SIDE, CORNER)


def finish_specs(skip):
    row = lambda width, col: pl.BlockSpec((BLOCK, width), lambda i: (i + skip, col))
    return [row(D, 0), row(D, 1), row(4 * D, 0)] + [whole(*dim) for dim in WEIGHTS]


def finish_cost(rows):
    return rows * 2200000, rows * 9000, rows


def finish_inner(values, weights):
    return call(
        finish_inner_kernel, "finish_inner", (3,),
        [whole(WIN, WIN)] + finish_specs(0),
        pl.BlockSpec((2, BLOCK, D), lambda i: (0, i, 0)), shapes((2, INNER, D))[0], [],
        (1000, 1000, 0), 20,
    )(jnp.asarray(SPLIT, BF16), *values, *weights)


def finish_edge(values, weights):
    return call(
        finish_edge_kernel, "finish_edge", (5,),
        [whole(WIN, WIN), whole(4 * SMALL, BLOCK)] + finish_specs(3),
        EDGE_PAIRS, shapes(*[(2, n, D) for n in PIECES[1:]]), [],
        finish_cost(5 * BLOCK), 24,
    )(jnp.asarray(SPLIT, BF16), jnp.asarray(CORNER_BACK, BF16), *values, *weights)


def join_kernel(inner, edge, up, side, corner, *outs):
    run, stub = 48, 24

    def load(ref, n, at, count):
        return ref[n, at : at + count, :].astype(F32)

    for zone in range(3):

        @pl.when((pl.program_id(0) + 1) // 2 == zone)
        def _(zone=zone):
            for n, out_ref in enumerate(outs):
                if zone == 1:
                    half = pl.program_id(0) - 1
                    left = load(side, n, 0, WIN)
                    right = load(edge, n, 0, WIN)
                    left, right = (jnp.where(half == 0, v[:HALF], v[HALF:]) for v in (left, right))
                    full = []
                    for q in range(3):
                        at = pl.multiple_of(q * BLOCK + half * WIN, 16)
                        full.append(inner[n, pl.ds(at, WIN), :].astype(F32))
                elif zone == 0:
                    left, right = load(corner, n, 0, SMALL), load(up, n, 3 * WIN, SMALL)
                    full = [load(up, n, q * WIN, WIN) for q in range(3)]
                else:
                    left, right = load(side, n, WIN, SMALL), load(edge, n, 4 * WIN, SMALL)
                    full = [load(edge, n, WIN + q * WIN, WIN) for q in range(3)]
                for i in range(3):
                    parts = [left[i * stub : i * stub + stub]]
                    parts += [part[i * run : i * run + run] for part in full]
                    parts.append(right[i * stub : i * stub + stub])
                    strip = jnp.concatenate(parts)
                    out_ref[i] = strip.reshape(LON, LEV, D).astype(BF16)


def join(parts):
    spec = pl.BlockSpec((3, LON, LEV, D), lambda i: (i, 0, 0, 0))
    dim = (LAT, LON, LEV, D)
    return call(
        join_kernel, "join", (4,),
        [whole(2, n, D) for n in PIECES],
        [spec] * 2, shapes(*[dim] * 2), [],
        (1000000, 9000000, 0), 26,
    )(*parts)


def sum_kernel(terms_ref, qkv_ref, out_ref):
    total = jnp.sum(terms_ref[...].astype(F32).reshape(DEVICES // 2, 16, D), 0)
    for c in range(3):
        qkv_ref[:, c * D : c * D + D] = total[4 * c : 4 * c + 4]
    out_ref[...] = total[12:]


def sum_terms(terms):
    return call(
        sum_kernel, "sum_terms", (),
        [whole(1024, D)], [whole(4, 3 * D), whole(4, D)],
        shapes((4, 3 * D), (4, D), dtype=F32), [], (2000000, 2200000, 0), 20,
    )(terms)


def shift_pairs(lat_step, lon_step):
    return [
        (a * SECTORS + b, (a + lat_step) % BANDS * SECTORS + (b + lon_step) % SECTORS)
        for a in range(BANDS)
        for b in range(SECTORS)
    ]


def exchange(parts, sign):
    steps = ((sign, 0), (0, sign), (sign, sign))
    return [lax.ppermute(part, BOTH, shift_pairs(*step)) for part, step in zip(parts, steps)]


def swap_blocks(values, axis, groups=None):
    return lax.all_to_all(
        values, axis, split_axis=0, concat_axis=0, axis_index_groups=groups, tiled=True
    )


SAME_CORE = [
    [a * SECTORS + b for a in range(core, BANDS, 2) for b in range(SECTORS)] for core in range(2)
]
OTHER_CORE = [(d, d ^ SECTORS) for d in range(DEVICES)]


def per_device(buffer, fetch_owner, fetch_slot, norm_gain, qkv_weight, out_weight, out_grad):
    weights = (qkv_weight, norm_gain.reshape(1, D), out_weight)
    lists, place, table = make_requests(fetch_owner.reshape(1, TOKENS), fetch_slot.reshape(1, TOKENS))
    lists = swap_blocks(lists, "lat")
    replies = swap_blocks(serve(lists, buffer).reshape(BANDS, CAP, D), "lat")
    replies = replies.reshape(BANDS * CAP, D)

    c_up, c_side, c_corner, c_inner, c_edge = sort_pieces(out_grad.reshape(TOKENS, D))
    c_parts = [c_edge] + exchange([c_up, c_side, c_corner], -1)
    place = place.reshape(TOKENS)[ORDER].reshape(-1, 1)

    x_up, x_side, x_corner, x_inner, x_edge = pick(table, place, replies)
    x_parts = [x_edge] + exchange([x_up, x_side, x_corner], -1)

    band = lax.axis_index("lat")
    flag = (band == BANDS - 1).astype(I32).reshape(1)
    core = (band % 2).astype(I32).reshape(1)
    first = attend_inner(x_inner, c_inner, weights)
    x, left, right = attend_edge(x_parts, c_parts, flag, weights, first)
    own, away = weight_terms(core, left, right)
    got = lax.ppermute(away, BOTH, OTHER_CORE)
    edge, *away = finish_edge((x, left, right), weights)
    up, side, corner = exchange(away, 1)
    inner = finish_inner((x, left, right), weights)
    half = add_halves(own, got)
    half, inner, side, corner = lax.optimization_barrier((half, inner, side, corner))
    terms = swap_blocks(half, BOTH, SAME_CORE)
    returned = [up, side, corner]
    outs = join([inner, edge] + returned)
    return (*outs, *sum_terms(terms))


def solution(mesh):
    return jax.shard_map(
        per_device,
        mesh=mesh,
        in_specs=(
            P(BOTH, None),
            P("lat", "lon", None, None),
            P("lat", "lon", None),
            P(),
            P(),
            P(),
            P("lat", "lon", None, None),
        ),
        out_specs=(
            P("lat", "lon", None, None),
            P("lat", "lon", None, None),
            P(BOTH, None),
            P(BOTH, None),
        ),
        check_vma=False,
    )
```

```python
import functools
import jax
import jax.numpy as jnp
import numpy as np
from jax import lax
from jax.experimental import pallas as pl
from jax.experimental.pallas import tpu as pltpu
from jax.sharding import PartitionSpec as P

NN = (((1,), (0,)), ((), ()))
NT = (((1,), (1,)), ((), ()))
TN = (((0,), (0,)), ((), ()))
F32 = jnp.float32
BF16 = jnp.bfloat16
I32 = jnp.int32
D = 512
BANDS, SECTORS = 16, 8
DEVICES = BANDS * SECTORS
LAT, LON, LEV = 12, 48, 4
TOKENS = LAT * LON * LEV
STRIP = LON * LEV
ROWS = 1152
CAP = 288
WIN = 144
HALF = 72
SMALL = 80
BLOCK = 2 * WIN
QUAD = 256
SCALE = 0.125
LOG2E = 1.4426950408889634
FAR = -1e30
BOTH = ("lat", "lon")

UP, SIDE, CORNER = 3 * WIN + SMALL, WIN + SMALL, SMALL
INNER, EDGE = 6 * WIN, 4 * WIN + SMALL


def split_matrix(places, rows):
    matrix = np.zeros((rows, places * 4), np.float32)
    for place in range(places):
        for level in range(4):
            matrix[(level // 2) * places * 2 + place * 2 + level % 2, place * 4 + level] = 1
    return matrix


SPLIT = split_matrix(36, WIN)
SPLIT_SMALL = split_matrix(18, SMALL)


def corner_matrix():
    matrix = np.zeros((BLOCK, 4 * SMALL), np.float32)
    for r in range(2):
        for part in range(4):
            for at in range(36):
                matrix[r * WIN + part * 36 + at, part * SMALL + r * 36 + at] = 1
    return matrix


CORNER_JOIN = corner_matrix()


def corner_back():
    matrix = np.zeros((4 * SMALL, BLOCK), np.float32)
    for part in range(4):
        split = CORNER_JOIN[:, part * SMALL : part * SMALL + HALF]
        matrix[part * SMALL : part * SMALL + HALF] = SPLIT_SMALL[:HALF].T @ split.T
    return matrix


CORNER_BACK = corner_back()


def back_matrices():
    back = np.zeros((2, WIN + 3 * SMALL, BLOCK), np.float32)
    rows = np.arange(WIN)
    first = rows + np.where(rows < HALF, 0, HALF)
    for part in range(2):
        back[0, part * WIN : part * WIN + WIN, first + part * HALF] = SPLIT
    edge, side, up, corner = CORNER_BACK.reshape(4, SMALL, BLOCK)
    back[1, :SMALL] = edge
    for at, part in enumerate((up, side, corner)):
        back[1, WIN + at * SMALL : WIN + at * SMALL + SMALL] = part
    return back


BACK = back_matrices()


def product(left, right, form=NN):
    return lax.dot_general(left, right, form, preferred_element_type=F32)


def normalise(values):
    centred = values - jnp.mean(values, -1, keepdims=True)
    inverse = lax.rsqrt(jnp.mean(centred * centred, -1, keepdims=True) + 1e-5)
    return centred * inverse, inverse


def whole(*shape):
    return pl.BlockSpec(shape, lambda *i: (0,) * len(shape))


def blocks(rows, width):
    return pl.BlockSpec((rows, width), lambda i: (i, 0))


def shapes(*dims, dtype=BF16):
    return [jax.ShapeDtypeStruct(dim, dtype) for dim in dims]


def call(kernel, name, grid, ins, outs, out_shapes, scratch, cost, vmem, aliases={}):
    flops, moved, exps = cost
    return pl.pallas_call(
        kernel,
        grid=grid,
        in_specs=ins,
        out_specs=outs,
        out_shape=out_shapes,
        scratch_shapes=scratch,
        input_output_aliases=aliases,
        compiler_params=pltpu.CompilerParams(vmem_limit_bytes=vmem * 2**20),
        cost_estimate=pl.CostEstimate(flops=flops, bytes_accessed=moved, transcendentals=exps),
        name=name,
    )


ZONES = (0, 3, 9, 12)
GROUP = 16
COMPACT = [(b - a) * STRIP + BANDS * 2 * (GROUP - 1) for a, b in zip(ZONES, ZONES[1:])]


def request_kernel(owner_ref, slot_ref, lists_ref, place_ref, table_ref, hits, ranks):
    owner = owner_ref[...]
    slot = slot_ref[...]
    hit = owner == lax.broadcasted_iota(I32, (BANDS, TOKENS), 0)
    hits[...] = hit.astype(F32)
    step = STRIP
    row = lax.broadcasted_iota(I32, (step, step), 0)
    triangle = (row <= lax.broadcasted_iota(I32, (step, step), 1)).astype(F32).astype(BF16)
    row = lax.broadcasted_iota(I32, (BANDS, BANDS), 0)
    earlier = (lax.broadcasted_iota(I32, (BANDS, BANDS), 1) < row).astype(F32).astype(BF16)
    before = jnp.zeros((BANDS, 1), F32)
    columns = []
    for zone in range(3):
        first = before
        strips = range(ZONES[zone], ZONES[zone + 1])
        for strip in strips:
            spot = slice(strip * step, strip * step + step)
            part = hits[:, spot]
            count = product(part.astype(BF16), triangle) + before
            ranks[:, spot] = jnp.sum(part * count, 0, keepdims=True) - 1.0
            before = before + jnp.sum(part, 1, keepdims=True)
        start = jnp.floor(first * (1.0 / GROUP))
        groups = jnp.floor((before + (GROUP - 1)) * (1.0 / GROUP)) - start
        groups = jnp.where(before > first, groups, 0.0)
        base = product(earlier, jnp.broadcast_to(groups, (BANDS, 128)).astype(BF16))[:, :1]
        shift = (base - start) * GROUP
        for strip in strips:
            spot = slice(strip * step, strip * step + step)
            moved = jnp.sum(hits[:, spot] * shift, 0, keepdims=True)
            place_ref[:, spot] = (ranks[:, spot] + moved).astype(I32)
        columns += [start, groups]
    columns += [jnp.zeros((BANDS, 2), F32)]
    table_ref[...] = jnp.concatenate(columns, 1).astype(I32)
    rank = ranks[...]
    high = jnp.where(hit, lax.shift_right_logical(slot, 5), 0).astype(F32).astype(BF16)
    low = jnp.where(hit, slot & 31, 0).astype(F32).astype(BF16)
    chosen = rank == lax.broadcasted_iota(I32, (CAP, TOKENS), 0).astype(F32)
    chosen = jnp.where(chosen, 1.0, 0.0).astype(BF16)
    found = product(high, chosen, NT) * 32.0 + product(low, chosen, NT)
    lists_ref[...] = found.astype(I32).reshape(BANDS, 1, CAP)


def make_requests(owners, slots):
    return call(
        request_kernel, "requests", (),
        [whole(1, TOKENS)] * 2,
        [whole(BANDS, 1, CAP), whole(1, TOKENS), whole(BANDS, 8)],
        shapes((BANDS, 1, CAP), (1, TOKENS), (BANDS, 8), dtype=I32),
        [pltpu.VMEM((BANDS, TOKENS), F32), pltpu.VMEM((1, TOKENS), F32)],
        (100000000, 100000, 0), 62,
    )(owners, slots)


ASKERS = 4


def serve_kernel(lists_ref, buffer_ref, out_ref):
    for at in range(ASKERS):
        row = jnp.broadcast_to(lists_ref[at].astype(F32), (8, CAP))
        wanted = row.T[:, :1].astype(I32)
        for half in range(2):
            chosen = wanted[half * 144 : half * 144 + 144] == lax.broadcasted_iota(I32, (144, ROWS), 1)
            chosen = jnp.where(chosen, 1.0, 0.0).astype(BF16)
            rows = slice(at * CAP + half * 144, at * CAP + half * 144 + 144)
            out_ref[rows, :] = product(chosen, buffer_ref[...]).astype(BF16)


def serve(lists, buffer):
    return call(
        serve_kernel, "serve", (BANDS // ASKERS,),
        [pl.BlockSpec((ASKERS, 1, CAP), lambda i: (i, 0, 0)), whole(ROWS, D)],
        blocks(ASKERS * CAP, D),
        shapes((BANDS * CAP, D))[0],
        [], (5400000000, 6000000, 0), 60,
    )(lists, buffer)


def pick_kernel(table_ref, place_ref, replies_ref, up_ref, side_ref, corner_ref, inner_ref, edge_ref, compact):
    compact[...] = jnp.zeros_like(compact)
    firsts = (0, UP + CORNER, UP + CORNER + 2 * WIN + INNER)
    for zone, size in enumerate(COMPACT):
        filled = 0
        for owner in range(BANDS):
            start = owner * CAP + table_ref[owner, 2 * zone] * GROUP
            groups = table_ref[owner, 2 * zone + 1]

            def move(at, filled, start=start):
                source = pl.multiple_of(start + at * GROUP, GROUP)
                target = pl.multiple_of(filled, GROUP)
                compact[pl.ds(target, GROUP), :] = replies_ref[pl.ds(source, GROUP), :]
                return filled + GROUP

            filled = lax.fori_loop(0, groups, move, filled)

        def find(first, count, size=size):
            place = place_ref[first : first + count, :]
            chosen = place == lax.broadcasted_iota(I32, (count, size), 1)
            chosen = jnp.where(chosen, 1.0, 0.0).astype(BF16)
            return product(chosen, compact[:size, :]).astype(BF16)

        first = firsts[zone]
        if zone == 0:
            found = find(first, UP + CORNER)
            up_ref[...] = found[:UP]
            corner_ref[...] = found[UP:]
        elif zone == 1:
            found = find(first, 2 * WIN + INNER)
            side_ref[:WIN, :] = found[:WIN]
            edge_ref[:WIN, :] = found[WIN : 2 * WIN]
            inner_ref[...] = found[2 * WIN :]
        else:
            found = find(first, SMALL + EDGE - WIN)
            side_ref[WIN:, :] = found[:SMALL]
            edge_ref[WIN:, :] = found[SMALL:]


def pick(table, place, replies):
    return call(
        pick_kernel, "pick", (),
        [pl.BlockSpec(memory_space=pltpu.SMEM), whole(PLACES, 1), whole(BANDS * CAP, D)],
        [whole(n, D) for n in (UP, SIDE, CORNER, INNER, EDGE)],
        shapes(*[(n, D) for n in (UP, SIDE, CORNER, INNER, EDGE)]),
        [pltpu.VMEM((max(COMPACT), D), BF16)], (3600000000, 8000000, 0), 60,
    )(table, place, replies)


def sort_kernel(grid_ref, split_ref, small_ref, up_ref, side_ref, corner_ref, inner_ref, edge_ref):
    strips = [grid_ref[i * STRIP : i * STRIP + STRIP, :].astype(F32) for i in range(LAT)]

    def put(ref, at, lats, first, cols):
        part = jnp.concatenate([strips[i][first * 4 : (first + cols) * 4] for i in lats])
        matrix = split_ref if part.shape[0] == WIN else small_ref
        ref[at : at + matrix.shape[0], :] = product(matrix[...], part.astype(BF16)).astype(BF16)

    low, mid, high = range(3), range(3, 9), range(9, 12)
    for q in range(3):
        put(up_ref, q * WIN, low, 6 + 12 * q, 12)
        put(inner_ref, q * BLOCK, range(3, 6), 6 + 12 * q, 12)
        put(inner_ref, q * BLOCK + WIN, range(6, 9), 6 + 12 * q, 12)
        put(edge_ref, WIN + q * WIN, high, 6 + 12 * q, 12)
    put(up_ref, 3 * WIN, low, 42, 6)
    put(side_ref, 0, mid, 0, 6)
    put(side_ref, WIN, high, 0, 6)
    put(corner_ref, 0, low, 0, 6)
    put(edge_ref, 0, mid, 42, 6)
    put(edge_ref, 4 * WIN, high, 42, 6)


def sort_pieces(values):
    return call(
        sort_kernel, "sort_pieces", (),
        [whole(TOKENS, D), whole(WIN, WIN), whole(SMALL, HALF)],
        [whole(n, D) for n in (UP, SIDE, CORNER, INNER, EDGE)],
        shapes(*[(n, D) for n in (UP, SIDE, CORNER, INNER, EDGE)]),
        [], (400000000, 5000000, 0), 24,
    )(values, jnp.asarray(SPLIT, BF16), jnp.asarray(SPLIT_SMALL, BF16))


def order_ids():
    ids = np.arange(TOKENS).reshape(LAT, LON, 2, 2)

    def piece(lats, first, cols):
        part = ids[lats[0] : lats[-1] + 1, first : first + cols].transpose(2, 0, 1, 3).reshape(-1)
        return np.pad(part, (0, WIN - 64 - HALF if part.size == HALF else 0))

    low, mid, high = range(3), range(3, 9), range(9, 12)
    order = [piece(low, 6 + 12 * q, 12) for q in range(3)] + [piece(low, 42, 6), piece(low, 0, 6)]
    order += [piece(mid, 0, 6), piece(mid, 42, 6)]
    for q in range(3):
        first, second = piece(range(3, 6), 6 + 12 * q, 12), piece(range(6, 9), 6 + 12 * q, 12)
        order += [first[:HALF], second[:HALF], first[HALF:], second[HALF:]]
    order += [piece(high, 0, 6)]
    order += [piece(high, 6 + 12 * q, 12) for q in range(3)] + [piece(high, 42, 6)]
    return np.concatenate(order)


ORDER = order_ids()
PLACES = UP + SIDE + CORNER + INNER + EDGE


EDGE_BLOCKS = (
    (WIN, lambda i: i),
    (WIN, lambda i: jnp.maximum(i - 1, 0)),
    (WIN, lambda i: i // 4),
    (SMALL, lambda i: 0),
)
EDGE_SPECS = [pl.BlockSpec((n, D), lambda i, at=at: (at(i), 0)) for n, at in EDGE_BLOCKS]
EDGE_PAIRS = [pl.BlockSpec((2, n, D), lambda i, at=at: (0, at(i), 0)) for n, at in EDGE_BLOCKS]


def join_halves(first, second):
    first, second = first.astype(F32), second.astype(F32)
    return jnp.concatenate([first[:HALF], second[:HALF], first[HALF:], second[HALF:]])


def attend(x_all, bias, ga_ref, w_ref, gain_ref, x_out, ha_ref, dp_ref, packed):
    x_out[...] = x_all.astype(BF16)
    normed, _ = normalise(x_all)
    hidden = (normed * gain_ref[...]).astype(BF16)
    ha_ref[:, :D] = hidden
    for part in range(3):
        cols = slice(part * D, part * D + D)
        packed[:, cols] = product(hidden, w_ref[:, cols]).astype(BF16)
    lane = lax.broadcasted_iota(I32, (1, QUAD), 1)
    sides = [jnp.where((lane >= 64 * n) & (lane < 64 * n + 64), 1.0, 0.0) for n in range(4)]
    low_sides = [side.astype(BF16) for side in sides]

    def spread(values):
        return jnp.concatenate([values * side for side in low_sides])

    def gather(matrix, values):
        parts = product(matrix, values, TN)
        return sum(parts[n * WIN : n * WIN + WIN] * side for n, side in enumerate(sides))

    for window in range(2):
        rows = slice(window * WIN, window * WIN + WIN)
        for quad in range(2):
            spot = [slice(part * D + quad * QUAD, part * D + quad * QUAD + QUAD) for part in range(3)]
            queries, keys, values = (packed[rows, cols] for cols in spot)
            queries, grads = spread(queries), spread(ga_ref[rows, spot[0]])
            scores = product(keys, queries, NT) * (SCALE * LOG2E)
            if bias is not None:
                scores = scores + bias()
            grown = jnp.exp2(scores - jnp.max(scores, 0, keepdims=True))
            probs = grown * (1.0 / jnp.sum(grown, 0, keepdims=True))
            low = probs.astype(BF16)
            weighted = probs * product(values, grads, NT)
            slope = weighted - probs * jnp.sum(weighted, 0, keepdims=True)
            slope = (slope * SCALE).astype(BF16)
            ha_ref[rows, slice(D + quad * QUAD, D + quad * QUAD + QUAD)] = gather(low, values).astype(BF16)
            dp_ref[rows, spot[0]] = gather(slope, keys).astype(BF16)
            dp_ref[rows, spot[1]] = product(slope, queries).astype(BF16)
            dp_ref[rows, spot[2]] = product(low, grads).astype(BF16)


def join_corner(join_ref, edge, side, up, corner):
    parts = [edge[:SMALL, :], side[:SMALL, :], up[:SMALL, :], corner[...]]
    return product(join_ref[...], jnp.concatenate(parts))


def slopes(c_all, ow_ref, cot_ref, ga_ref):
    cot = c_all.astype(BF16)
    cot_ref[...] = cot
    ga_ref[...] = product(cot, ow_ref[...], NT).astype(BF16)


def prepare_inner_kernel(inner, ow_ref, cot_ref, ga_ref):
    slopes(join_halves(inner[:WIN, :], inner[WIN:, :]), ow_ref, cot_ref, ga_ref)


def prepare_edge_kernel(edge, up, side, corner, join_ref, ow_ref, _, cot_ref, ga_ref, c_all):
    step = pl.program_id(0)

    @pl.when(step == 0)
    def _():
        c_all[...] = join_halves(edge[...], side[...])

    @pl.when((step > 0) & (step < 4))
    def _():
        c_all[...] = join_halves(edge[...], up[...])

    @pl.when(step == 4)
    def _():
        c_all[...] = join_corner(join_ref, edge, side, up, corner)

    slopes(c_all[...], ow_ref, cot_ref, ga_ref)


def prepare_inner(inner, ow):
    return call(
        prepare_inner_kernel, "prepare_inner", (3,),
        [blocks(BLOCK, D), whole(D, D)],
        [blocks(BLOCK, D)] * 2, shapes((TOKENS, D), (INNER, D)),
        [], (500000000, 3000000, 0), 20,
    )(inner, ow)


def prepare_edge(parts, ow, cot):
    return call(
        prepare_edge_kernel, "prepare_edge", (5,),
        EDGE_SPECS + [whole(BLOCK, 4 * SMALL), whole(D, D), pl.BlockSpec(memory_space=pl.ANY)],
        [pl.BlockSpec((BLOCK, D), lambda i: (i + 3, 0)), blocks(BLOCK, D)],
        shapes((TOKENS, D), (5 * BLOCK, D)),
        [pltpu.VMEM((BLOCK, D), F32)], (800000000, 5000000, 0), 20,
        aliases={6: 0},
    )(*parts, jnp.asarray(CORNER_JOIN, BF16), ow, cot)


def inner_kernel(x_ref, *refs):
    attend(x_ref[...].astype(F32), None, *refs)


def edge_kernel(flag_ref, xe, xu, xs, xc, join_ref, apart_ref, *refs):
    sources, (*refs, x_all) = refs[:3], refs[6:]
    step = pl.program_id(0)

    @pl.when(step == 0)
    def _():
        x_all[...] = join_halves(xe[...], xs[...])

    @pl.when((step > 0) & (step < 4))
    def _():
        x_all[...] = join_halves(xe[...], xu[...])

    @pl.when(step == 4)
    def _():
        x_all[...] = join_corner(join_ref, xe, xs, xu, xc)

    seam = jnp.where(step > 0, flag_ref[0], 0).astype(F32)
    attend(x_all[...], lambda: apart_ref[...] * seam, *sources, *refs)


def attend_specs(rows, skip):
    widths = (D, 2 * D, 3 * D)
    row = lambda n: pl.BlockSpec((BLOCK, n), lambda i: (i + skip, 0))
    sources = [blocks(BLOCK, D), whole(D, 3 * D), whole(1, D)]
    out_shapes = shapes(*[(TOKENS, n) for n in widths])
    scratch = [pltpu.VMEM((BLOCK, 3 * D), BF16)]
    cost = (rows * 6000000, rows * 10000, rows * 1200)
    return sources, [row(n) for n in widths], out_shapes, scratch, cost


WEIGHTS = [(D, 3 * D), (1, D), (D, D)]


def attend_inner(x, ga, weights):
    sources, outs, out_shapes, scratch, cost = attend_specs(INNER, 0)
    return call(
        inner_kernel, "attend_inner", (3,),
        [blocks(BLOCK, D)] + sources,
        outs, out_shapes, scratch, cost, 18,
    )(x, ga, *weights[:2])


def apart_matrix():
    late = np.arange(WIN) >= HALF
    return np.tile(np.where(late[:, None] != late[None, :], FAR, 0.0).astype(np.float32), (1, 4))


def attend_edge(parts, ga, flag, weights, carried):
    sources, outs, out_shapes, scratch, cost = attend_specs(5 * BLOCK, 3)
    return call(
        edge_kernel, "attend_edge", (5,),
        [pl.BlockSpec(memory_space=pltpu.SMEM)]
        + EDGE_SPECS
        + [whole(BLOCK, 4 * SMALL), whole(WIN, 4 * WIN)]
        + sources
        + [pl.BlockSpec(memory_space=pl.ANY)] * 3,
        outs, out_shapes, scratch + [pltpu.VMEM((BLOCK, D), F32)], cost, 24,
        aliases={10 + n: n for n in range(3)},
    )(flag, *parts, jnp.asarray(CORNER_JOIN, BF16), jnp.asarray(apart_matrix()), ga, *weights[:2], *carried)


def weight_kernel(core_ref, left_ref, dp_ref, cot_ref, own_ref, away_ref, turned):
    for c in range(4):
        right = dp_ref[:, c * D : c * D + D] if c < 3 else cot_ref[...]
        chunk = product(left_ref[:, c // 3 * D : c // 3 * D + D], right, TN).reshape(64, 8, D)
        half = c % 2 * 4
        turned[:, 0, c // 2, half : half + 4] = chunk[:, :4]
        turned[:, 1, c // 2, half : half + 4] = chunk[:, 4:]
    core = core_ref[0]
    for at in range(BANDS // 2):
        for ref, which in ((own_ref, core), (away_ref, 1 - core)):
            part = turned[pl.ds(at * 8 + which * 4, 4)].reshape(128, D)
            ref[at * 128 : at * 128 + 128, :] = part.astype(ref.dtype)


def weight_terms(core, left, dp, cot):
    return call(
        weight_kernel, "weight_terms", (),
        [pl.BlockSpec(memory_space=pltpu.SMEM), whole(TOKENS, 2 * D), whole(TOKENS, 3 * D), whole(TOKENS, D)],
        [whole(1024, D)] * 2,
        [jax.ShapeDtypeStruct((1024, D), F32), jax.ShapeDtypeStruct((1024, D), BF16)],
        [pltpu.VMEM((64, 2, 2, 8, D), F32)],
        (1000, 1000, 0), 22,
    )(core, left, dp, cot)


def add_kernel(own_ref, got_ref, out_ref):
    out_ref[...] = (own_ref[...] + got_ref[...].astype(F32)).astype(BF16)


def add_halves(own, got):
    return call(
        add_kernel, "add_halves", (4,),
        [blocks(256, D)] * 2, blocks(256, D), shapes((1024, D))[0], [],
        (1000000, 4000000, 0), 10,
    )(own, got)


def finished(x_ref, att_ref, dp_ref, c_ref, w_ref, gain_ref, ow_ref):
    x = x_ref[...].astype(F32)
    out = x + product(att_ref[...], ow_ref[...])
    normed, inverse = normalise(x)
    hidden = product(dp_ref[...], w_ref[...], NT) * gain_ref[...]
    hidden = (
        hidden
        - jnp.mean(hidden, -1, keepdims=True)
        - normed * jnp.mean(hidden * normed, -1, keepdims=True)
    )
    grad = c_ref[...].astype(F32) + inverse * hidden
    return out, grad


def grid_pieces(split_ref, values):
    first = jnp.concatenate([values[:HALF], values[WIN : WIN + HALF]]).astype(BF16)
    second = jnp.concatenate([values[HALF:WIN], values[WIN + HALF :]]).astype(BF16)
    return [product(split_ref[...], part, TN).astype(BF16) for part in (first, second)]


def finish_inner_kernel(split_ref, *refs):
    *refs, inner = refs
    for n, values in enumerate(finished(*refs)):
        first, second = grid_pieces(split_ref, values)
        inner[n, :WIN, :] = first
        inner[n, WIN:, :] = second


def finish_edge_kernel(back_ref, *refs):
    refs, (edge, up, side, corner) = refs[:7], refs[7:]
    step = pl.program_id(0)
    for n, values in enumerate(finished(*refs)):
        parts = product(back_ref[...], values.astype(BF16)).astype(BF16)
        edge[n] = parts[:WIN]
        up[n] = parts[WIN:BLOCK]

        @pl.when(step == 0)
        def _(n=n, parts=parts):
            side[n] = parts[WIN:BLOCK]

        @pl.when(step == 4)
        def _(n=n, parts=parts):
            side[n, :SMALL, :] = parts[WIN + SMALL : WIN + 2 * SMALL]
            corner[n] = parts[WIN + 2 * SMALL :]


PIECES = (INNER, EDGE, UP, SIDE, CORNER)


def finish_specs(skip):
    row = lambda width, col: pl.BlockSpec((BLOCK, width), lambda i: (i + skip, col))
    return [row(D, 0), row(D, 1), row(3 * D, 0), row(D, 0)] + [whole(*dim) for dim in WEIGHTS]


def finish_cost(rows):
    return rows * 2200000, rows * 9000, rows


def finish_inner(values, weights):
    return call(
        finish_inner_kernel, "finish_inner", (3,),
        [whole(WIN, WIN)] + finish_specs(0),
        pl.BlockSpec((2, BLOCK, D), lambda i: (0, i, 0)), shapes((2, INNER, D))[0], [],
        (1000, 1000, 0), 20,
    )(jnp.asarray(SPLIT, BF16), *values, *weights)


def finish_edge(values, weights):
    return call(
        finish_edge_kernel, "finish_edge", (5,),
        [pl.BlockSpec((None,) + BACK.shape[1:], lambda i: (i // 4, 0, 0))] + finish_specs(3),
        EDGE_PAIRS, shapes(*[(2, n, D) for n in PIECES[1:]]), [],
        finish_cost(5 * BLOCK), 24,
    )(jnp.asarray(BACK, BF16), *values, *weights)


def join_kernel(inner, edge, up, side, corner, *outs):
    run, stub = 48, 24

    def load(ref, n, at, count):
        return ref[n, at : at + count, :].astype(F32)

    for zone in range(3):

        @pl.when((pl.program_id(0) + 1) // 2 == zone)
        def _(zone=zone):
            for n, out_ref in enumerate(outs):
                if zone == 1:
                    half = pl.program_id(0) - 1
                    left = load(side, n, 0, WIN)
                    right = load(edge, n, 0, WIN)
                    left, right = (jnp.where(half == 0, v[:HALF], v[HALF:]) for v in (left, right))
                    full = []
                    for q in range(3):
                        at = pl.multiple_of(q * BLOCK + half * WIN, 16)
                        full.append(inner[n, pl.ds(at, WIN), :].astype(F32))
                elif zone == 0:
                    left, right = load(corner, n, 0, SMALL), load(up, n, 3 * WIN, SMALL)
                    full = [load(up, n, q * WIN, WIN) for q in range(3)]
                else:
                    left, right = load(side, n, WIN, SMALL), load(edge, n, 4 * WIN, SMALL)
                    full = [load(edge, n, WIN + q * WIN, WIN) for q in range(3)]
                for i in range(3):
                    parts = [left[i * stub : i * stub + stub]]
                    parts += [part[i * run : i * run + run] for part in full]
                    parts.append(right[i * stub : i * stub + stub])
                    strip = jnp.concatenate(parts)
                    out_ref[i] = strip.reshape(LON, LEV, D).astype(BF16)


def join(parts):
    spec = pl.BlockSpec((3, LON, LEV, D), lambda i: (i, 0, 0, 0))
    dim = (LAT, LON, LEV, D)
    return call(
        join_kernel, "join", (4,),
        [whole(2, n, D) for n in PIECES],
        [spec] * 2, shapes(*[dim] * 2), [],
        (60000000000, 9000000, 0), 26,
    )(*parts)


def sum_kernel(terms_ref, qkv_ref, out_ref):
    total = jnp.sum(terms_ref[...].astype(F32).reshape(DEVICES // 2, 16, D), 0)
    for c in range(3):
        qkv_ref[:, c * D : c * D + D] = total[4 * c : 4 * c + 4]
    out_ref[...] = total[12:]


def sum_terms(terms):
    return call(
        sum_kernel, "sum_terms", (),
        [whole(1024, D)], [whole(4, 3 * D), whole(4, D)],
        shapes((4, 3 * D), (4, D), dtype=F32), [], (2000000, 2200000, 0), 20,
    )(terms)


def shift_pairs(lat_step, lon_step):
    return [
        (a * SECTORS + b, (a + lat_step) % BANDS * SECTORS + (b + lon_step) % SECTORS)
        for a in range(BANDS)
        for b in range(SECTORS)
    ]


def exchange(parts, sign):
    steps = ((sign, 0), (0, sign), (sign, sign))
    return [lax.ppermute(part, BOTH, shift_pairs(*step)) for part, step in zip(parts, steps)]


def swap_blocks(values, axis, groups=None):
    return lax.all_to_all(
        values, axis, split_axis=0, concat_axis=0, axis_index_groups=groups, tiled=True
    )


SAME_CORE = [
    [a * SECTORS + b for a in range(core, BANDS, 2) for b in range(SECTORS)] for core in range(2)
]
OTHER_CORE = [(d, d ^ SECTORS) for d in range(DEVICES)]


def per_device(buffer, fetch_owner, fetch_slot, norm_gain, qkv_weight, out_weight, out_grad):
    weights = (qkv_weight, norm_gain.reshape(1, D), out_weight)
    lists, place, table = make_requests(fetch_owner.reshape(1, TOKENS), fetch_slot.reshape(1, TOKENS))
    lists = swap_blocks(lists, "lat")
    replies = swap_blocks(serve(lists, buffer).reshape(BANDS, CAP, D), "lat")
    replies = replies.reshape(BANDS * CAP, D)

    c_up, c_side, c_corner, c_inner, c_edge = sort_pieces(out_grad.reshape(TOKENS, D))
    c_parts = [c_edge] + exchange([c_up, c_side, c_corner], -1)
    cot, ga_inner = prepare_inner(c_inner, out_weight)
    cot, ga_edge = prepare_edge(c_parts, out_weight, cot)
    place = place.reshape(TOKENS)[ORDER].reshape(-1, 1)

    replies, ga_inner = lax.optimization_barrier((replies, ga_inner))
    x_up, x_side, x_corner, x_inner, x_edge = pick(table, place, replies)
    x_parts = [x_edge] + exchange([x_up, x_side, x_corner], -1)

    band = lax.axis_index("lat")
    flag = (band == BANDS - 1).astype(I32).reshape(1)
    core = (band % 2).astype(I32).reshape(1)
    first = attend_inner(x_inner, ga_inner, weights)
    x, left, dp = attend_edge(x_parts, ga_edge, flag, weights, first)
    edge, *away = finish_edge((x, left, dp, cot), weights)
    up, side, corner = exchange(away, 1)
    left, dp, edge = lax.optimization_barrier((left, dp, edge))
    own, away = weight_terms(core, left, dp, cot)
    got = lax.ppermute(away, BOTH, OTHER_CORE)
    inner = finish_inner((x, left, dp, cot), weights)
    got, inner = lax.optimization_barrier((got, inner))
    terms = swap_blocks(add_halves(own, got), BOTH, SAME_CORE)
    returned = [up, side, corner]
    outs = join([inner, edge] + returned)
    return (*outs, *sum_terms(terms))


def solution(mesh):
    return jax.shard_map(
        per_device,
        mesh=mesh,
        in_specs=(
            P(BOTH, None),
            P("lat", "lon", None, None),
            P("lat", "lon", None),
            P(),
            P(),
            P(),
            P("lat", "lon", None, None),
        ),
        out_specs=(
            P("lat", "lon", None, None),
            P("lat", "lon", None, None),
            P(BOTH, None),
            P(BOTH, None),
        ),
        check_vma=False,
    )
```

```python
import functools
import jax
import jax.numpy as jnp
import numpy as np
from jax import lax
from jax.experimental import pallas as pl
from jax.experimental.pallas import tpu as pltpu
from jax.sharding import PartitionSpec as P

NN = (((1,), (0,)), ((), ()))
NT = (((1,), (1,)), ((), ()))
TN = (((0,), (0,)), ((), ()))
F32 = jnp.float32
BF16 = jnp.bfloat16
I32 = jnp.int32
D = 512
BANDS, SECTORS = 16, 8
DEVICES = BANDS * SECTORS
LAT, LON, LEV = 12, 48, 4
TOKENS = LAT * LON * LEV
STRIP = LON * LEV
ROWS = 1152
CAP = 288
WIN = 144
HALF = 72
SMALL = 80
BLOCK = 2 * WIN
QUAD = 256
SCALE = 0.125
LOG2E = 1.4426950408889634
FAR = -1e30
BOTH = ("lat", "lon")

UP, SIDE, CORNER = 3 * WIN + SMALL, WIN + SMALL, SMALL
INNER, EDGE = 6 * WIN, 4 * WIN + SMALL


def split_matrix(places, rows):
    matrix = np.zeros((rows, places * 4), np.float32)
    for place in range(places):
        for level in range(4):
            matrix[(level // 2) * places * 2 + place * 2 + level % 2, place * 4 + level] = 1
    return matrix


SPLIT = split_matrix(36, WIN)
SPLIT_SMALL = split_matrix(18, SMALL)


def corner_matrix():
    matrix = np.zeros((BLOCK, 4 * SMALL), np.float32)
    for r in range(2):
        for part in range(4):
            for at in range(36):
                matrix[r * WIN + part * 36 + at, part * SMALL + r * 36 + at] = 1
    return matrix


CORNER_JOIN = corner_matrix()


def corner_back():
    matrix = np.zeros((4 * SMALL, BLOCK), np.float32)
    for part in range(4):
        split = CORNER_JOIN[:, part * SMALL : part * SMALL + HALF]
        matrix[part * SMALL : part * SMALL + HALF] = SPLIT_SMALL[:HALF].T @ split.T
    return matrix


CORNER_BACK = corner_back()


def back_matrices():
    back = np.zeros((2, WIN + 3 * SMALL, BLOCK), np.float32)
    rows = np.arange(WIN)
    first = rows + np.where(rows < HALF, 0, HALF)
    for part in range(2):
        back[0, part * WIN : part * WIN + WIN, first + part * HALF] = SPLIT
    edge, side, up, corner = CORNER_BACK.reshape(4, SMALL, BLOCK)
    back[1, :SMALL] = edge
    for at, part in enumerate((up, side, corner)):
        back[1, WIN + at * SMALL : WIN + at * SMALL + SMALL] = part
    return back


BACK = back_matrices()


def product(left, right, form=NN):
    return lax.dot_general(left, right, form, preferred_element_type=F32)


def normalise(values):
    centred = values - jnp.mean(values, -1, keepdims=True)
    inverse = lax.rsqrt(jnp.mean(centred * centred, -1, keepdims=True) + 1e-5)
    return centred * inverse, inverse


def whole(*shape):
    return pl.BlockSpec(shape, lambda *i: (0,) * len(shape))


def blocks(rows, width):
    return pl.BlockSpec((rows, width), lambda i: (i, 0))


def shapes(*dims, dtype=BF16):
    return [jax.ShapeDtypeStruct(dim, dtype) for dim in dims]


def call(kernel, name, grid, ins, outs, out_shapes, scratch, cost, vmem, aliases={}):
    flops, moved, exps = cost
    return pl.pallas_call(
        kernel,
        grid=grid,
        in_specs=ins,
        out_specs=outs,
        out_shape=out_shapes,
        scratch_shapes=scratch,
        input_output_aliases=aliases,
        compiler_params=pltpu.CompilerParams(vmem_limit_bytes=vmem * 2**20),
        cost_estimate=pl.CostEstimate(flops=flops, bytes_accessed=moved, transcendentals=exps),
        name=name,
    )


ZONES = (0, 3, 9, 12)
GROUP = 16
COMPACT = [(b - a) * STRIP + BANDS * 2 * (GROUP - 1) for a, b in zip(ZONES, ZONES[1:])]


def request_kernel(owner_ref, slot_ref, lists_ref, place_ref, table_ref, hits, ranks):
    owner = owner_ref[...]
    slot = slot_ref[...]
    hit = owner == lax.broadcasted_iota(I32, (BANDS, TOKENS), 0)
    hits[...] = hit.astype(F32)
    step = STRIP
    row = lax.broadcasted_iota(I32, (step, step), 0)
    triangle = (row <= lax.broadcasted_iota(I32, (step, step), 1)).astype(F32).astype(BF16)
    row = lax.broadcasted_iota(I32, (BANDS, BANDS), 0)
    earlier = (lax.broadcasted_iota(I32, (BANDS, BANDS), 1) < row).astype(F32).astype(BF16)
    before = jnp.zeros((BANDS, 1), F32)
    columns = []
    for zone in range(3):
        first = before
        strips = range(ZONES[zone], ZONES[zone + 1])
        for strip in strips:
            spot = slice(strip * step, strip * step + step)
            part = hits[:, spot]
            count = product(part.astype(BF16), triangle) + before
            ranks[:, spot] = jnp.sum(part * count, 0, keepdims=True) - 1.0
            before = before + jnp.sum(part, 1, keepdims=True)
        start = jnp.floor(first * (1.0 / GROUP))
        groups = jnp.floor((before + (GROUP - 1)) * (1.0 / GROUP)) - start
        groups = jnp.where(before > first, groups, 0.0)
        base = product(earlier, jnp.broadcast_to(groups, (BANDS, 128)).astype(BF16))[:, :1]
        shift = (base - start) * GROUP
        for strip in strips:
            spot = slice(strip * step, strip * step + step)
            moved = jnp.sum(hits[:, spot] * shift, 0, keepdims=True)
            place_ref[:, spot] = (ranks[:, spot] + moved).astype(I32)
        columns += [start, groups]
    columns += [jnp.zeros((BANDS, 2), F32)]
    table_ref[...] = jnp.concatenate(columns, 1).astype(I32)
    rank = ranks[...]
    high = jnp.where(hit, lax.shift_right_logical(slot, 5), 0).astype(F32).astype(BF16)
    low = jnp.where(hit, slot & 31, 0).astype(F32).astype(BF16)
    chosen = rank == lax.broadcasted_iota(I32, (CAP, TOKENS), 0).astype(F32)
    chosen = jnp.where(chosen, 1.0, 0.0).astype(BF16)
    found = product(high, chosen, NT) * 32.0 + product(low, chosen, NT)
    lists_ref[...] = found.astype(I32).reshape(BANDS, 1, CAP)


def make_requests(owners, slots):
    return call(
        request_kernel, "requests", (),
        [whole(1, TOKENS)] * 2,
        [whole(BANDS, 1, CAP), whole(1, TOKENS), whole(BANDS, 8)],
        shapes((BANDS, 1, CAP), (1, TOKENS), (BANDS, 8), dtype=I32),
        [pltpu.VMEM((BANDS, TOKENS), F32), pltpu.VMEM((1, TOKENS), F32)],
        (100000000, 100000, 0), 62,
    )(owners, slots)


ASKERS = 4


def serve_kernel(lists_ref, buffer_ref, out_ref):
    for at in range(ASKERS):
        row = jnp.broadcast_to(lists_ref[at].astype(F32), (8, CAP))
        wanted = row.T[:, :1].astype(I32)
        for half in range(2):
            chosen = wanted[half * 144 : half * 144 + 144] == lax.broadcasted_iota(I32, (144, ROWS), 1)
            chosen = jnp.where(chosen, 1.0, 0.0).astype(BF16)
            rows = slice(at * CAP + half * 144, at * CAP + half * 144 + 144)
            out_ref[rows, :] = product(chosen, buffer_ref[...]).astype(BF16)


def serve(lists, buffer):
    return call(
        serve_kernel, "serve", (BANDS // ASKERS,),
        [pl.BlockSpec((ASKERS, 1, CAP), lambda i: (i, 0, 0)), whole(ROWS, D)],
        blocks(ASKERS * CAP, D),
        shapes((BANDS * CAP, D))[0],
        [], (5400000000, 6000000, 0), 60,
    )(lists, buffer)


def pick_kernel(table_ref, place_ref, replies_ref, up_ref, side_ref, corner_ref, inner_ref, edge_ref, compact):
    compact[...] = jnp.zeros_like(compact)
    firsts = (0, UP + CORNER, UP + CORNER + 2 * WIN + INNER)
    for zone, size in enumerate(COMPACT):
        filled = 0
        for owner in range(BANDS):
            start = owner * CAP + table_ref[owner, 2 * zone] * GROUP
            groups = table_ref[owner, 2 * zone + 1]

            def move(at, filled, start=start):
                source = pl.multiple_of(start + at * GROUP, GROUP)
                target = pl.multiple_of(filled, GROUP)
                compact[pl.ds(target, GROUP), :] = replies_ref[pl.ds(source, GROUP), :]
                return filled + GROUP

            filled = lax.fori_loop(0, groups, move, filled)

        def find(first, count, size=size):
            place = place_ref[first : first + count, :]
            chosen = place == lax.broadcasted_iota(I32, (count, size), 1)
            chosen = jnp.where(chosen, 1.0, 0.0).astype(BF16)
            return product(chosen, compact[:size, :]).astype(BF16)

        first = firsts[zone]
        if zone == 0:
            found = find(first, UP + CORNER)
            up_ref[...] = found[:UP]
            corner_ref[...] = found[UP:]
        elif zone == 1:
            found = find(first, 2 * WIN + INNER)
            side_ref[:WIN, :] = found[:WIN]
            edge_ref[:WIN, :] = found[WIN : 2 * WIN]
            inner_ref[...] = found[2 * WIN :]
        else:
            found = find(first, SMALL + EDGE - WIN)
            side_ref[WIN:, :] = found[:SMALL]
            edge_ref[WIN:, :] = found[SMALL:]


def pick(table, place, replies):
    return call(
        pick_kernel, "pick", (),
        [pl.BlockSpec(memory_space=pltpu.SMEM), whole(PLACES, 1), whole(BANDS * CAP, D)],
        [whole(n, D) for n in (UP, SIDE, CORNER, INNER, EDGE)],
        shapes(*[(n, D) for n in (UP, SIDE, CORNER, INNER, EDGE)]),
        [pltpu.VMEM((max(COMPACT), D), BF16)], (3600000000, 8000000, 0), 60,
    )(table, place, replies)


def sort_kernel(grid_ref, split_ref, small_ref, up_ref, side_ref, corner_ref, inner_ref, edge_ref):
    strips = [grid_ref[i * STRIP : i * STRIP + STRIP, :].astype(F32) for i in range(LAT)]

    def put(ref, at, lats, first, cols):
        part = jnp.concatenate([strips[i][first * 4 : (first + cols) * 4] for i in lats])
        matrix = split_ref if part.shape[0] == WIN else small_ref
        ref[at : at + matrix.shape[0], :] = product(matrix[...], part.astype(BF16)).astype(BF16)

    low, mid, high = range(3), range(3, 9), range(9, 12)
    for q in range(3):
        put(up_ref, q * WIN, low, 6 + 12 * q, 12)
        put(inner_ref, q * BLOCK, range(3, 6), 6 + 12 * q, 12)
        put(inner_ref, q * BLOCK + WIN, range(6, 9), 6 + 12 * q, 12)
        put(edge_ref, WIN + q * WIN, high, 6 + 12 * q, 12)
    put(up_ref, 3 * WIN, low, 42, 6)
    put(side_ref, 0, mid, 0, 6)
    put(side_ref, WIN, high, 0, 6)
    put(corner_ref, 0, low, 0, 6)
    put(edge_ref, 0, mid, 42, 6)
    put(edge_ref, 4 * WIN, high, 42, 6)


def sort_pieces(values):
    return call(
        sort_kernel, "sort_pieces", (),
        [whole(TOKENS, D), whole(WIN, WIN), whole(SMALL, HALF)],
        [whole(n, D) for n in (UP, SIDE, CORNER, INNER, EDGE)],
        shapes(*[(n, D) for n in (UP, SIDE, CORNER, INNER, EDGE)]),
        [], (400000000, 5000000, 0), 24,
    )(values, jnp.asarray(SPLIT, BF16), jnp.asarray(SPLIT_SMALL, BF16))


def order_ids():
    ids = np.arange(TOKENS).reshape(LAT, LON, 2, 2)

    def piece(lats, first, cols):
        part = ids[lats[0] : lats[-1] + 1, first : first + cols].transpose(2, 0, 1, 3).reshape(-1)
        return np.pad(part, (0, WIN - 64 - HALF if part.size == HALF else 0))

    low, mid, high = range(3), range(3, 9), range(9, 12)
    order = [piece(low, 6 + 12 * q, 12) for q in range(3)] + [piece(low, 42, 6), piece(low, 0, 6)]
    order += [piece(mid, 0, 6), piece(mid, 42, 6)]
    for q in range(3):
        first, second = piece(range(3, 6), 6 + 12 * q, 12), piece(range(6, 9), 6 + 12 * q, 12)
        order += [first[:HALF], second[:HALF], first[HALF:], second[HALF:]]
    order += [piece(high, 0, 6)]
    order += [piece(high, 6 + 12 * q, 12) for q in range(3)] + [piece(high, 42, 6)]
    return np.concatenate(order)


ORDER = order_ids()
PLACES = UP + SIDE + CORNER + INNER + EDGE


EDGE_BLOCKS = (
    (WIN, lambda i: i),
    (WIN, lambda i: jnp.maximum(i - 1, 0)),
    (WIN, lambda i: i // 4),
    (SMALL, lambda i: 0),
)
EDGE_SPECS = [pl.BlockSpec((n, D), lambda i, at=at: (at(i), 0)) for n, at in EDGE_BLOCKS]
EDGE_PAIRS = [pl.BlockSpec((2, n, D), lambda i, at=at: (0, at(i), 0)) for n, at in EDGE_BLOCKS]


def join_halves(first, second):
    first, second = first.astype(F32), second.astype(F32)
    return jnp.concatenate([first[:HALF], second[:HALF], first[HALF:], second[HALF:]])


def attend(x_all, bias, ga_ref, w_ref, gain_ref, x_out, ha_ref, dp_ref, packed):
    x_out[...] = x_all.astype(BF16)
    normed, _ = normalise(x_all)
    hidden = (normed * gain_ref[...]).astype(BF16)
    ha_ref[:, :D] = hidden
    for part in range(3):
        cols = slice(part * D, part * D + D)
        packed[:, cols] = product(hidden, w_ref[:, cols]).astype(BF16)
    lane = lax.broadcasted_iota(I32, (1, QUAD), 1)
    sides = [jnp.where((lane >= 64 * n) & (lane < 64 * n + 64), 1.0, 0.0) for n in range(4)]
    low_sides = [side.astype(BF16) for side in sides]

    def spread(values):
        return jnp.concatenate([values * side for side in low_sides])

    def gather(matrix, values):
        parts = product(matrix, values, TN)
        return sum(parts[n * WIN : n * WIN + WIN] * side for n, side in enumerate(sides))

    for window in range(2):
        rows = slice(window * WIN, window * WIN + WIN)
        for quad in range(2):
            spot = [slice(part * D + quad * QUAD, part * D + quad * QUAD + QUAD) for part in range(3)]
            queries, keys, values = (packed[rows, cols] for cols in spot)
            queries, grads = spread(queries), spread(ga_ref[rows, spot[0]])
            scores = product(keys, queries, NT) * (SCALE * LOG2E)
            if bias is not None:
                scores = scores + bias()
            grown = jnp.exp2(scores - jnp.max(scores, 0, keepdims=True))
            probs = grown * (1.0 / jnp.sum(grown, 0, keepdims=True))
            low = probs.astype(BF16)
            weighted = probs * product(values, grads, NT)
            slope = weighted - probs * jnp.sum(weighted, 0, keepdims=True)
            slope = slope.astype(BF16)
            ha_ref[rows, slice(D + quad * QUAD, D + quad * QUAD + QUAD)] = gather(low, values).astype(BF16)
            dp_ref[rows, spot[0]] = (gather(slope, keys) * SCALE).astype(BF16)
            dp_ref[rows, spot[1]] = (product(slope, queries) * SCALE).astype(BF16)
            dp_ref[rows, spot[2]] = product(low, grads).astype(BF16)


def join_corner(join_ref, edge, side, up, corner):
    parts = [edge[:SMALL, :], side[:SMALL, :], up[:SMALL, :], corner[...]]
    return product(join_ref[...], jnp.concatenate(parts))


def slopes(c_all, ow_ref, cot_ref, ga_ref):
    cot = c_all.astype(BF16)
    cot_ref[...] = cot
    ga_ref[...] = product(cot, ow_ref[...], NT).astype(BF16)


def prepare_inner_kernel(inner, ow_ref, cot_ref, ga_ref):
    slopes(join_halves(inner[:WIN, :], inner[WIN:, :]), ow_ref, cot_ref, ga_ref)


def prepare_edge_kernel(edge, up, side, corner, join_ref, ow_ref, _, cot_ref, ga_ref, c_all):
    step = pl.program_id(0)

    @pl.when(step == 0)
    def _():
        c_all[...] = join_halves(edge[...], side[...])

    @pl.when((step > 0) & (step < 4))
    def _():
        c_all[...] = join_halves(edge[...], up[...])

    @pl.when(step == 4)
    def _():
        c_all[...] = join_corner(join_ref, edge, side, up, corner)

    slopes(c_all[...], ow_ref, cot_ref, ga_ref)


def prepare_inner(inner, ow):
    return call(
        prepare_inner_kernel, "prepare_inner", (3,),
        [blocks(BLOCK, D), whole(D, D)],
        [blocks(BLOCK, D)] * 2, shapes((TOKENS, D), (INNER, D)),
        [], (500000000, 3000000, 0), 10,
    )(inner, ow)


def prepare_edge(parts, ow, cot):
    return call(
        prepare_edge_kernel, "prepare_edge", (5,),
        EDGE_SPECS + [whole(BLOCK, 4 * SMALL), whole(D, D), pl.BlockSpec(memory_space=pl.ANY)],
        [pl.BlockSpec((BLOCK, D), lambda i: (i + 3, 0)), blocks(BLOCK, D)],
        shapes((TOKENS, D), (5 * BLOCK, D)),
        [pltpu.VMEM((BLOCK, D), F32)], (800000000, 5000000, 0), 12,
        aliases={6: 0},
    )(*parts, jnp.asarray(CORNER_JOIN, BF16), ow, cot)


def inner_kernel(x_ref, *refs):
    attend(x_ref[...].astype(F32), None, *refs)


def edge_kernel(flag_ref, xe, xu, xs, xc, join_ref, apart_ref, *refs):
    sources, (*refs, x_all) = refs[:3], refs[6:]
    step = pl.program_id(0)

    @pl.when(step == 0)
    def _():
        x_all[...] = join_halves(xe[...], xs[...])

    @pl.when((step > 0) & (step < 4))
    def _():
        x_all[...] = join_halves(xe[...], xu[...])

    @pl.when(step == 4)
    def _():
        x_all[...] = join_corner(join_ref, xe, xs, xu, xc)

    seam = jnp.where(step > 0, flag_ref[0], 0).astype(F32)
    attend(x_all[...], lambda: apart_ref[...] * seam, *sources, *refs)


def attend_specs(rows, skip):
    widths = (D, 2 * D, 3 * D)
    row = lambda n: pl.BlockSpec((BLOCK, n), lambda i: (i + skip, 0))
    sources = [blocks(BLOCK, D), whole(D, 3 * D), whole(1, D)]
    out_shapes = shapes(*[(TOKENS, n) for n in widths])
    scratch = [pltpu.VMEM((BLOCK, 3 * D), BF16)]
    cost = (rows * 6000000, rows * 10000, rows * 1200)
    return sources, [row(n) for n in widths], out_shapes, scratch, cost


WEIGHTS = [(D, 3 * D), (1, D), (D, D)]


def attend_inner(x, ga, weights):
    sources, outs, out_shapes, scratch, cost = attend_specs(INNER, 0)
    return call(
        inner_kernel, "attend_inner", (3,),
        [blocks(BLOCK, D)] + sources,
        outs, out_shapes, scratch, cost, 14,
    )(x, ga, *weights[:2])


def apart_matrix():
    late = np.arange(WIN) >= HALF
    return np.tile(np.where(late[:, None] != late[None, :], FAR, 0.0).astype(np.float32), (1, 4))


def attend_edge(parts, ga, flag, weights, carried):
    sources, outs, out_shapes, scratch, cost = attend_specs(5 * BLOCK, 3)
    return call(
        edge_kernel, "attend_edge", (5,),
        [pl.BlockSpec(memory_space=pltpu.SMEM)]
        + EDGE_SPECS
        + [whole(BLOCK, 4 * SMALL), whole(WIN, 4 * WIN)]
        + sources
        + [pl.BlockSpec(memory_space=pl.ANY)] * 3,
        outs, out_shapes, scratch + [pltpu.VMEM((BLOCK, D), F32)], cost, 16,
        aliases={10 + n: n for n in range(3)},
    )(flag, *parts, jnp.asarray(CORNER_JOIN, BF16), jnp.asarray(apart_matrix()), ga, *weights[:2], *carried)


def weight_kernel(core_ref, left_ref, dp_ref, cot_ref, own_ref, away_ref, turned):
    for c in range(4):
        right = dp_ref[:, c * D : c * D + D] if c < 3 else cot_ref[...]
        chunk = product(left_ref[:, c // 3 * D : c // 3 * D + D], right, TN).reshape(64, 8, D)
        half = c % 2 * 4
        turned[:, 0, c // 2, half : half + 4] = chunk[:, :4]
        turned[:, 1, c // 2, half : half + 4] = chunk[:, 4:]
    core = core_ref[0]
    for at in range(BANDS // 2):
        for ref, which in ((own_ref, core), (away_ref, 1 - core)):
            part = turned[pl.ds(at * 8 + which * 4, 4)].reshape(128, D)
            ref[at * 128 : at * 128 + 128, :] = part.astype(ref.dtype)


def weight_terms(core, left, dp, cot):
    return call(
        weight_kernel, "weight_terms", (),
        [pl.BlockSpec(memory_space=pltpu.SMEM), whole(TOKENS, 2 * D), whole(TOKENS, 3 * D), whole(TOKENS, D)],
        [whole(1024, D)] * 2,
        [jax.ShapeDtypeStruct((1024, D), F32), jax.ShapeDtypeStruct((1024, D), BF16)],
        [pltpu.VMEM((64, 2, 2, 8, D), F32)],
        (1000, 1000, 0), 14,
    )(core, left, dp, cot)


def add_kernel(own_ref, got_ref, out_ref):
    out_ref[...] = (own_ref[...] + got_ref[...].astype(F32)).astype(BF16)


def add_halves(own, got):
    return call(
        add_kernel, "add_halves", (4,),
        [blocks(256, D)] * 2, blocks(256, D), shapes((1024, D))[0], [],
        (1000000, 4000000, 0), 6,
    )(own, got)


def finished(x_ref, att_ref, dp_ref, c_ref, w_ref, gain_ref, ow_ref):
    x = x_ref[...].astype(F32)
    out = x + product(att_ref[...], ow_ref[...])
    normed, inverse = normalise(x)
    hidden = product(dp_ref[...], w_ref[...], NT) * gain_ref[...]
    hidden = (
        hidden
        - jnp.mean(hidden, -1, keepdims=True)
        - normed * jnp.mean(hidden * normed, -1, keepdims=True)
    )
    grad = c_ref[...].astype(F32) + inverse * hidden
    return out, grad


def grid_pieces(split_ref, values):
    first = jnp.concatenate([values[:HALF], values[WIN : WIN + HALF]]).astype(BF16)
    second = jnp.concatenate([values[HALF:WIN], values[WIN + HALF :]]).astype(BF16)
    return [product(split_ref[...], part, TN).astype(BF16) for part in (first, second)]


def finish_inner_kernel(split_ref, *refs):
    *refs, inner = refs
    for n, values in enumerate(finished(*refs)):
        first, second = grid_pieces(split_ref, values)
        inner[n, :WIN, :] = first
        inner[n, WIN:, :] = second


def finish_edge_kernel(back_ref, *refs):
    refs, (edge, up, side, corner) = refs[:7], refs[7:]
    step = pl.program_id(0)
    for n, values in enumerate(finished(*refs)):
        parts = product(back_ref[...], values.astype(BF16)).astype(BF16)
        edge[n] = parts[:WIN]
        up[n] = parts[WIN:BLOCK]

        @pl.when(step == 0)
        def _(n=n, parts=parts):
            side[n] = parts[WIN:BLOCK]

        @pl.when(step == 4)
        def _(n=n, parts=parts):
            side[n, :SMALL, :] = parts[WIN + SMALL : WIN + 2 * SMALL]
            corner[n] = parts[WIN + 2 * SMALL :]


PIECES = (INNER, EDGE, UP, SIDE, CORNER)


def finish_specs(skip):
    row = lambda width, col: pl.BlockSpec((BLOCK, width), lambda i: (i + skip, col))
    return [row(D, 0), row(D, 1), row(3 * D, 0), row(D, 0)] + [whole(*dim) for dim in WEIGHTS]


def finish_cost(rows):
    return rows * 2200000, rows * 9000, rows


def finish_inner(values, weights):
    return call(
        finish_inner_kernel, "finish_inner", (3,),
        [whole(WIN, WIN)] + finish_specs(0),
        pl.BlockSpec((2, BLOCK, D), lambda i: (0, i, 0)), shapes((2, INNER, D))[0], [],
        (1000, 1000, 0), 14,
    )(jnp.asarray(SPLIT, BF16), *values, *weights)


def finish_edge(values, weights):
    return call(
        finish_edge_kernel, "finish_edge", (5,),
        [pl.BlockSpec((None,) + BACK.shape[1:], lambda i: (i // 4, 0, 0))] + finish_specs(3),
        EDGE_PAIRS, shapes(*[(2, n, D) for n in PIECES[1:]]), [],
        finish_cost(5 * BLOCK), 16,
    )(jnp.asarray(BACK, BF16), *values, *weights)


def join_kernel(inner, edge, up, side, corner, *outs):
    run, stub = 48, 24

    def load(ref, n, at, count):
        return ref[n, at : at + count, :].astype(F32)

    for zone in range(3):

        @pl.when((pl.program_id(0) + 1) // 2 == zone)
        def _(zone=zone):
            for n, out_ref in enumerate(outs):
                if zone == 1:
                    half = pl.program_id(0) - 1
                    left = load(side, n, 0, WIN)
                    right = load(edge, n, 0, WIN)
                    left, right = (jnp.where(half == 0, v[:HALF], v[HALF:]) for v in (left, right))
                    full = []
                    for q in range(3):
                        at = pl.multiple_of(q * BLOCK + half * WIN, 16)
                        full.append(inner[n, pl.ds(at, WIN), :].astype(F32))
                elif zone == 0:
                    left, right = load(corner, n, 0, SMALL), load(up, n, 3 * WIN, SMALL)
                    full = [load(up, n, q * WIN, WIN) for q in range(3)]
                else:
                    left, right = load(side, n, WIN, SMALL), load(edge, n, 4 * WIN, SMALL)
                    full = [load(edge, n, WIN + q * WIN, WIN) for q in range(3)]
                for i in range(3):
                    parts = [left[i * stub : i * stub + stub]]
                    parts += [part[i * run : i * run + run] for part in full]
                    parts.append(right[i * stub : i * stub + stub])
                    strip = jnp.concatenate(parts)
                    out_ref[i] = strip.reshape(LON, LEV, D).astype(BF16)


def join(parts):
    spec = pl.BlockSpec((3, LON, LEV, D), lambda i: (i, 0, 0, 0))
    dim = (LAT, LON, LEV, D)
    return call(
        join_kernel, "join", (4,),
        [whole(2, n, D) for n in PIECES],
        [spec] * 2, shapes(*[dim] * 2), [],
        (60000000000, 9000000, 0), 16,
    )(*parts)


def sum_kernel(terms_ref, qkv_ref, out_ref):
    total = jnp.sum(terms_ref[...].astype(F32).reshape(DEVICES // 2, 16, D), 0)
    for c in range(3):
        qkv_ref[:, c * D : c * D + D] = total[4 * c : 4 * c + 4]
    out_ref[...] = total[12:]


def sum_terms(terms):
    return call(
        sum_kernel, "sum_terms", (),
        [whole(1024, D)], [whole(4, 3 * D), whole(4, D)],
        shapes((4, 3 * D), (4, D), dtype=F32), [], (2000000, 2200000, 0), 20,
    )(terms)


def shift_pairs(lat_step, lon_step):
    return [
        (a * SECTORS + b, (a + lat_step) % BANDS * SECTORS + (b + lon_step) % SECTORS)
        for a in range(BANDS)
        for b in range(SECTORS)
    ]


def exchange(parts, sign):
    steps = ((sign, 0), (0, sign), (sign, sign))
    return [lax.ppermute(part, BOTH, shift_pairs(*step)) for part, step in zip(parts, steps)]


def swap_blocks(values, axis, groups=None):
    return lax.all_to_all(
        values, axis, split_axis=0, concat_axis=0, axis_index_groups=groups, tiled=True
    )


SAME_CORE = [
    [a * SECTORS + b for a in range(core, BANDS, 2) for b in range(SECTORS)] for core in range(2)
]
OTHER_CORE = [(d, d ^ SECTORS) for d in range(DEVICES)]


def per_device(buffer, fetch_owner, fetch_slot, norm_gain, qkv_weight, out_weight, out_grad):
    weights = (qkv_weight, norm_gain.reshape(1, D), out_weight)
    lists, place, table = make_requests(fetch_owner.reshape(1, TOKENS), fetch_slot.reshape(1, TOKENS))
    lists = swap_blocks(lists, "lat")
    replies = swap_blocks(serve(lists, buffer).reshape(BANDS, CAP, D), "lat")
    replies = replies.reshape(BANDS * CAP, D)

    c_up, c_side, c_corner, c_inner, c_edge = sort_pieces(out_grad.reshape(TOKENS, D))
    c_parts = [c_edge] + exchange([c_up, c_side, c_corner], -1)
    cot, ga_inner = prepare_inner(c_inner, out_weight)
    cot, ga_edge = prepare_edge(c_parts, out_weight, cot)
    place = place.reshape(TOKENS)[ORDER].reshape(-1, 1)

    replies, ga_inner = lax.optimization_barrier((replies, ga_inner))
    x_up, x_side, x_corner, x_inner, x_edge = pick(table, place, replies)
    x_parts = [x_edge] + exchange([x_up, x_side, x_corner], -1)

    band = lax.axis_index("lat")
    flag = (band == BANDS - 1).astype(I32).reshape(1)
    core = (band % 2).astype(I32).reshape(1)
    first = attend_inner(x_inner, ga_inner, weights)
    x, left, dp = attend_edge(x_parts, ga_edge, flag, weights, first)
    edge, *away = finish_edge((x, left, dp, cot), weights)
    up, side, corner = exchange(away, 1)
    left, dp, edge = lax.optimization_barrier((left, dp, edge))
    own, away = weight_terms(core, left, dp, cot)
    got = lax.ppermute(away, BOTH, OTHER_CORE)
    inner = finish_inner((x, left, dp, cot), weights)
    got, inner = lax.optimization_barrier((got, inner))
    terms = swap_blocks(add_halves(own, got), BOTH, SAME_CORE)
    returned = [up, side, corner]
    outs = join([inner, edge] + returned)
    return (*outs, *sum_terms(terms))


def solution(mesh):
    return jax.shard_map(
        per_device,
        mesh=mesh,
        in_specs=(
            P(BOTH, None),
            P("lat", "lon", None, None),
            P("lat", "lon", None),
            P(),
            P(),
            P(),
            P("lat", "lon", None, None),
        ),
        out_specs=(
            P("lat", "lon", None, None),
            P("lat", "lon", None, None),
            P(BOTH, None),
            P(BOTH, None),
        ),
        check_vma=False,
    )
```

```python
import functools
import jax
import jax.numpy as jnp
import numpy as np
from jax import lax
from jax.experimental import pallas as pl
from jax.experimental.pallas import tpu as pltpu
from jax.sharding import PartitionSpec as P

NN = (((1,), (0,)), ((), ()))
NT = (((1,), (1,)), ((), ()))
TN = (((0,), (0,)), ((), ()))
F32 = jnp.float32
BF16 = jnp.bfloat16
I32 = jnp.int32
D = 512
BANDS, SECTORS = 16, 8
DEVICES = BANDS * SECTORS
LAT, LON, LEV = 12, 48, 4
TOKENS = LAT * LON * LEV
STRIP = LON * LEV
ROWS = 1152
CAP = 288
WIN = 144
HALF = 72
SMALL = 80
BLOCK = 2 * WIN
QUAD = 256
SCALE = 0.125
LOG2E = 1.4426950408889634
FAR = -1e30
BOTH = ("lat", "lon")

UP, SIDE, CORNER = 3 * WIN + SMALL, WIN + SMALL, SMALL
INNER, EDGE = 6 * WIN, 4 * WIN + SMALL


def split_matrix(places, rows):
    matrix = np.zeros((rows, places * 4), np.float32)
    for place in range(places):
        for level in range(4):
            matrix[(level // 2) * places * 2 + place * 2 + level % 2, place * 4 + level] = 1
    return matrix


SPLIT = split_matrix(36, WIN)
SPLIT_SMALL = split_matrix(18, SMALL)


def corner_matrix():
    matrix = np.zeros((BLOCK, 4 * SMALL), np.float32)
    for r in range(2):
        for part in range(4):
            for at in range(36):
                matrix[r * WIN + part * 36 + at, part * SMALL + r * 36 + at] = 1
    return matrix


CORNER_JOIN = corner_matrix()


def corner_back():
    matrix = np.zeros((4 * SMALL, BLOCK), np.float32)
    for part in range(4):
        split = CORNER_JOIN[:, part * SMALL : part * SMALL + HALF]
        matrix[part * SMALL : part * SMALL + HALF] = SPLIT_SMALL[:HALF].T @ split.T
    return matrix


CORNER_BACK = corner_back()


def back_matrices():
    back = np.zeros((2, WIN + 3 * SMALL, BLOCK), np.float32)
    rows = np.arange(WIN)
    first = rows + np.where(rows < HALF, 0, HALF)
    for part in range(2):
        back[0, part * WIN : part * WIN + WIN, first + part * HALF] = SPLIT
    edge, side, up, corner = CORNER_BACK.reshape(4, SMALL, BLOCK)
    back[1, :SMALL] = edge
    for at, part in enumerate((up, side, corner)):
        back[1, WIN + at * SMALL : WIN + at * SMALL + SMALL] = part
    return back


BACK = back_matrices()


def product(left, right, form=NN):
    return lax.dot_general(left, right, form, preferred_element_type=F32)


def normalise(values):
    centred = values - jnp.mean(values, -1, keepdims=True)
    inverse = lax.rsqrt(jnp.mean(centred * centred, -1, keepdims=True) + 1e-5)
    return centred * inverse, inverse


def whole(*shape):
    return pl.BlockSpec(shape, lambda *i: (0,) * len(shape))


def blocks(rows, width):
    return pl.BlockSpec((rows, width), lambda i: (i, 0))


def shapes(*dims, dtype=BF16):
    return [jax.ShapeDtypeStruct(dim, dtype) for dim in dims]


def call(kernel, name, grid, ins, outs, out_shapes, scratch, cost, vmem, aliases={}):
    flops, moved, exps = cost
    return pl.pallas_call(
        kernel,
        grid=grid,
        in_specs=ins,
        out_specs=outs,
        out_shape=out_shapes,
        scratch_shapes=scratch,
        input_output_aliases=aliases,
        compiler_params=pltpu.CompilerParams(vmem_limit_bytes=vmem * 2**20),
        cost_estimate=pl.CostEstimate(flops=flops, bytes_accessed=moved, transcendentals=exps),
        name=name,
    )


ZONES = (0, 3, 9, 12)
GROUP = 16
COMPACT = [(b - a) * STRIP + BANDS * 2 * (GROUP - 1) for a, b in zip(ZONES, ZONES[1:])]


def request_kernel(owner_ref, slot_ref, lists_ref, place_ref, table_ref, hits, ranks):
    owner = owner_ref[...]
    slot = slot_ref[...]
    hit = owner == lax.broadcasted_iota(I32, (BANDS, TOKENS), 0)
    hits[...] = hit.astype(F32)
    step = STRIP
    row = lax.broadcasted_iota(I32, (step, step), 0)
    triangle = (row <= lax.broadcasted_iota(I32, (step, step), 1)).astype(F32).astype(BF16)
    row = lax.broadcasted_iota(I32, (BANDS, BANDS), 0)
    earlier = (lax.broadcasted_iota(I32, (BANDS, BANDS), 1) < row).astype(F32).astype(BF16)
    before = jnp.zeros((BANDS, 1), F32)
    columns = []
    for zone in range(3):
        first = before
        strips = range(ZONES[zone], ZONES[zone + 1])
        for strip in strips:
            spot = slice(strip * step, strip * step + step)
            part = hits[:, spot]
            count = product(part.astype(BF16), triangle) + before
            ranks[:, spot] = jnp.sum(part * count, 0, keepdims=True) - 1.0
            before = before + jnp.sum(part, 1, keepdims=True)
        start = jnp.floor(first * (1.0 / GROUP))
        groups = jnp.floor((before + (GROUP - 1)) * (1.0 / GROUP)) - start
        groups = jnp.where(before > first, groups, 0.0)
        base = product(earlier, jnp.broadcast_to(groups, (BANDS, 128)).astype(BF16))[:, :1]
        shift = (base - start) * GROUP
        for strip in strips:
            spot = slice(strip * step, strip * step + step)
            moved = jnp.sum(hits[:, spot] * shift, 0, keepdims=True)
            place_ref[:, spot] = (ranks[:, spot] + moved).astype(I32)
        columns += [start, groups]
    columns += [jnp.zeros((BANDS, 2), F32)]
    table_ref[...] = jnp.concatenate(columns, 1).astype(I32)
    rank = ranks[...]
    high = jnp.where(hit, lax.shift_right_logical(slot, 5), 0).astype(F32).astype(BF16)
    low = jnp.where(hit, slot & 31, 0).astype(F32).astype(BF16)
    chosen = rank == lax.broadcasted_iota(I32, (CAP, TOKENS), 0).astype(F32)
    chosen = jnp.where(chosen, 1.0, 0.0).astype(BF16)
    found = product(high, chosen, NT) * 32.0 + product(low, chosen, NT)
    lists_ref[...] = found.astype(I32).reshape(BANDS, 1, CAP)


def make_requests(owners, slots):
    return call(
        request_kernel, "requests", (),
        [whole(1, TOKENS)] * 2,
        [whole(BANDS, 1, CAP), whole(1, TOKENS), whole(BANDS, 8)],
        shapes((BANDS, 1, CAP), (1, TOKENS), (BANDS, 8), dtype=I32),
        [pltpu.VMEM((BANDS, TOKENS), F32), pltpu.VMEM((1, TOKENS), F32)],
        (100000000, 100000, 0), 62,
    )(owners, slots)


ASKERS = 4


def serve_kernel(lists_ref, buffer_ref, out_ref):
    for at in range(ASKERS):
        row = jnp.broadcast_to(lists_ref[at].astype(F32), (8, CAP))
        wanted = row.T[:, :1].astype(I32)
        for half in range(2):
            chosen = wanted[half * 144 : half * 144 + 144] == lax.broadcasted_iota(I32, (144, ROWS), 1)
            chosen = jnp.where(chosen, 1.0, 0.0).astype(BF16)
            rows = slice(at * CAP + half * 144, at * CAP + half * 144 + 144)
            out_ref[rows, :] = product(chosen, buffer_ref[...]).astype(BF16)


def serve(lists, buffer):
    return call(
        serve_kernel, "serve", (BANDS // ASKERS,),
        [pl.BlockSpec((ASKERS, 1, CAP), lambda i: (i, 0, 0)), whole(ROWS, D)],
        blocks(ASKERS * CAP, D),
        shapes((BANDS * CAP, D))[0],
        [], (5400000000, 6000000, 0), 60,
    )(lists, buffer)


def pick_kernel(table_ref, place_ref, replies_ref, up_ref, side_ref, corner_ref, inner_ref, edge_ref, compact):
    compact[...] = jnp.zeros_like(compact)
    firsts = (0, UP + CORNER, UP + CORNER + 2 * WIN + INNER)
    for zone, size in enumerate(COMPACT):
        filled = 0
        for owner in range(BANDS):
            start = owner * CAP + table_ref[owner, 2 * zone] * GROUP
            groups = table_ref[owner, 2 * zone + 1]

            def move(at, filled, start=start):
                source = pl.multiple_of(start + at * GROUP, GROUP)
                target = pl.multiple_of(filled, GROUP)
                compact[pl.ds(target, GROUP), :] = replies_ref[pl.ds(source, GROUP), :]
                return filled + GROUP

            filled = lax.fori_loop(0, groups, move, filled)

        def find(first, count, size=size):
            place = place_ref[first : first + count, :]
            chosen = place == lax.broadcasted_iota(I32, (count, size), 1)
            chosen = jnp.where(chosen, 1.0, 0.0).astype(BF16)
            return product(chosen, compact[:size, :]).astype(BF16)

        first = firsts[zone]
        if zone == 0:
            found = find(first, UP + CORNER)
            up_ref[...] = found[:UP]
            corner_ref[...] = found[UP:]
        elif zone == 1:
            found = find(first, 2 * WIN + INNER)
            side_ref[:WIN, :] = found[:WIN]
            edge_ref[:WIN, :] = found[WIN : 2 * WIN]
            inner_ref[...] = found[2 * WIN :]
        else:
            found = find(first, SMALL + EDGE - WIN)
            side_ref[WIN:, :] = found[:SMALL]
            edge_ref[WIN:, :] = found[SMALL:]


def pick(table, place, replies):
    return call(
        pick_kernel, "pick", (),
        [pl.BlockSpec(memory_space=pltpu.SMEM), whole(PLACES, 1), whole(BANDS * CAP, D)],
        [whole(n, D) for n in (UP, SIDE, CORNER, INNER, EDGE)],
        shapes(*[(n, D) for n in (UP, SIDE, CORNER, INNER, EDGE)]),
        [pltpu.VMEM((max(COMPACT), D), BF16)], (3600000000, 8000000, 0), 60,
    )(table, place, replies)


def sort_kernel(grid_ref, split_ref, small_ref, up_ref, side_ref, corner_ref, inner_ref, edge_ref):
    strips = [grid_ref[i * STRIP : i * STRIP + STRIP, :].astype(F32) for i in range(LAT)]

    def put(ref, at, lats, first, cols):
        part = jnp.concatenate([strips[i][first * 4 : (first + cols) * 4] for i in lats])
        matrix = split_ref if part.shape[0] == WIN else small_ref
        ref[at : at + matrix.shape[0], :] = product(matrix[...], part.astype(BF16)).astype(BF16)

    low, mid, high = range(3), range(3, 9), range(9, 12)
    for q in range(3):
        put(up_ref, q * WIN, low, 6 + 12 * q, 12)
        put(inner_ref, q * BLOCK, range(3, 6), 6 + 12 * q, 12)
        put(inner_ref, q * BLOCK + WIN, range(6, 9), 6 + 12 * q, 12)
        put(edge_ref, WIN + q * WIN, high, 6 + 12 * q, 12)
    put(up_ref, 3 * WIN, low, 42, 6)
    put(side_ref, 0, mid, 0, 6)
    put(side_ref, WIN, high, 0, 6)
    put(corner_ref, 0, low, 0, 6)
    put(edge_ref, 0, mid, 42, 6)
    put(edge_ref, 4 * WIN, high, 42, 6)


def sort_pieces(values):
    return call(
        sort_kernel, "sort_pieces", (),
        [whole(TOKENS, D), whole(WIN, WIN), whole(SMALL, HALF)],
        [whole(n, D) for n in (UP, SIDE, CORNER, INNER, EDGE)],
        shapes(*[(n, D) for n in (UP, SIDE, CORNER, INNER, EDGE)]),
        [], (400000000, 5000000, 0), 24,
    )(values, jnp.asarray(SPLIT, BF16), jnp.asarray(SPLIT_SMALL, BF16))


def order_ids():
    ids = np.arange(TOKENS).reshape(LAT, LON, 2, 2)

    def piece(lats, first, cols):
        part = ids[lats[0] : lats[-1] + 1, first : first + cols].transpose(2, 0, 1, 3).reshape(-1)
        return np.pad(part, (0, WIN - 64 - HALF if part.size == HALF else 0))

    low, mid, high = range(3), range(3, 9), range(9, 12)
    order = [piece(low, 6 + 12 * q, 12) for q in range(3)] + [piece(low, 42, 6), piece(low, 0, 6)]
    order += [piece(mid, 0, 6), piece(mid, 42, 6)]
    for q in range(3):
        first, second = piece(range(3, 6), 6 + 12 * q, 12), piece(range(6, 9), 6 + 12 * q, 12)
        order += [first[:HALF], second[:HALF], first[HALF:], second[HALF:]]
    order += [piece(high, 0, 6)]
    order += [piece(high, 6 + 12 * q, 12) for q in range(3)] + [piece(high, 42, 6)]
    return np.concatenate(order)


ORDER = order_ids()
PLACES = UP + SIDE + CORNER + INNER + EDGE


EDGE_BLOCKS = (
    (WIN, lambda i: i),
    (WIN, lambda i: jnp.maximum(i - 1, 0)),
    (WIN, lambda i: i // 4),
    (SMALL, lambda i: 0),
)
EDGE_SPECS = [pl.BlockSpec((n, D), lambda i, at=at: (at(i), 0)) for n, at in EDGE_BLOCKS]
EDGE_PAIRS = [pl.BlockSpec((2, n, D), lambda i, at=at: (0, at(i), 0)) for n, at in EDGE_BLOCKS]


def join_halves(first, second):
    first, second = first.astype(F32), second.astype(F32)
    return jnp.concatenate([first[:HALF], second[:HALF], first[HALF:], second[HALF:]])


def attend(x_all, bias, ga_ref, w_ref, gain_ref, x_out, ha_ref, dp_ref, packed):
    x_out[...] = x_all.astype(BF16)
    normed, _ = normalise(x_all)
    hidden = (normed * gain_ref[...]).astype(BF16)
    ha_ref[:, :D] = hidden
    for part in range(3):
        cols = slice(part * D, part * D + D)
        packed[:, cols] = product(hidden, w_ref[:, cols]).astype(BF16)
    lane = lax.broadcasted_iota(I32, (1, QUAD), 1)
    sides = [jnp.where((lane >= 64 * n) & (lane < 64 * n + 64), 1.0, 0.0) for n in range(4)]
    low_sides = [side.astype(BF16) for side in sides]

    def spread(values):
        return jnp.concatenate([values * side for side in low_sides])

    def gather(matrix, values):
        parts = product(matrix, values, TN)
        return sum(parts[n * WIN : n * WIN + WIN] * side for n, side in enumerate(sides))

    for window in range(2):
        rows = slice(window * WIN, window * WIN + WIN)
        for quad in range(2):
            spot = [slice(part * D + quad * QUAD, part * D + quad * QUAD + QUAD) for part in range(3)]
            queries, keys, values = (packed[rows, cols] for cols in spot)
            queries, grads = spread(queries), spread(ga_ref[rows, spot[0]])
            scores = product(keys, queries, NT) * (SCALE * LOG2E)
            if bias is not None:
                scores = scores + bias()
            grown = jnp.exp2(scores - jnp.max(scores, 0, keepdims=True))
            probs = grown * (1.0 / jnp.sum(grown, 0, keepdims=True))
            low = probs.astype(BF16)
            weighted = probs * product(values, grads, NT)
            slope = weighted - probs * jnp.sum(weighted, 0, keepdims=True)
            slope = slope.astype(BF16)
            ha_ref[rows, slice(D + quad * QUAD, D + quad * QUAD + QUAD)] = gather(low, values).astype(BF16)
            dp_ref[rows, spot[0]] = (gather(slope, keys) * SCALE).astype(BF16)
            dp_ref[rows, spot[1]] = (product(slope, queries) * SCALE).astype(BF16)
            dp_ref[rows, spot[2]] = product(low, grads).astype(BF16)


def join_corner(join_ref, edge, side, up, corner):
    parts = [edge[:SMALL, :], side[:SMALL, :], up[:SMALL, :], corner[...]]
    return product(join_ref[...], jnp.concatenate(parts))


def slopes(c_all, ow_ref, cot_ref, ga_ref):
    cot = c_all.astype(BF16)
    cot_ref[...] = cot
    ga_ref[...] = product(cot, ow_ref[...], NT).astype(BF16)


def prepare_inner_kernel(inner, ow_ref, cot_ref, ga_ref):
    slopes(join_halves(inner[:WIN, :], inner[WIN:, :]), ow_ref, cot_ref, ga_ref)


def prepare_edge_kernel(edge, up, side, corner, join_ref, ow_ref, _, cot_ref, ga_ref, c_all):
    step = pl.program_id(0)

    @pl.when(step == 0)
    def _():
        c_all[...] = join_halves(edge[...], side[...])

    @pl.when((step > 0) & (step < 4))
    def _():
        c_all[...] = join_halves(edge[...], up[...])

    @pl.when(step == 4)
    def _():
        c_all[...] = join_corner(join_ref, edge, side, up, corner)

    slopes(c_all[...], ow_ref, cot_ref, ga_ref)


def prepare_inner(inner, ow):
    return call(
        prepare_inner_kernel, "prepare_inner", (3,),
        [blocks(BLOCK, D), whole(D, D)],
        [blocks(BLOCK, D)] * 2, shapes((TOKENS, D), (INNER, D)),
        [], (500000000, 3000000, 0), 10,
    )(inner, ow)


def prepare_edge(parts, ow, cot):
    return call(
        prepare_edge_kernel, "prepare_edge", (5,),
        EDGE_SPECS + [whole(BLOCK, 4 * SMALL), whole(D, D), pl.BlockSpec(memory_space=pl.ANY)],
        [pl.BlockSpec((BLOCK, D), lambda i: (i + 3, 0)), blocks(BLOCK, D)],
        shapes((TOKENS, D), (5 * BLOCK, D)),
        [pltpu.VMEM((BLOCK, D), F32)], (800000000, 5000000, 0), 12,
        aliases={6: 0},
    )(*parts, jnp.asarray(CORNER_JOIN, BF16), ow, cot)


def inner_kernel(x_ref, *refs):
    attend(x_ref[...].astype(F32), None, *refs)


def edge_kernel(flag_ref, xe, xu, xs, xc, join_ref, apart_ref, *refs):
    sources, (*refs, x_all, mask) = refs[:3], refs[6:]
    step = pl.program_id(0)

    @pl.when(step == 0)
    def _():
        x_all[...] = join_halves(xe[...], xs[...])

    @pl.when((step > 0) & (step < 4))
    def _():
        x_all[...] = join_halves(xe[...], xu[...])

    @pl.when(step == 4)
    def _():
        x_all[...] = join_corner(join_ref, xe, xs, xu, xc)

    seam = jnp.where(step > 0, flag_ref[0], 0).astype(F32)
    mask[...] = apart_ref[...] * seam
    attend(x_all[...], lambda: mask[...], *sources, *refs)


def attend_specs(rows, skip):
    widths = (D, 2 * D, 3 * D)
    row = lambda n: pl.BlockSpec((BLOCK, n), lambda i: (i + skip, 0))
    sources = [blocks(BLOCK, D), whole(D, 3 * D), whole(1, D)]
    out_shapes = shapes(*[(TOKENS, n) for n in widths])
    scratch = [pltpu.VMEM((BLOCK, 3 * D), BF16)]
    cost = (rows * 6000000, rows * 10000, rows * 1200)
    return sources, [row(n) for n in widths], out_shapes, scratch, cost


WEIGHTS = [(D, 3 * D), (1, D), (D, D)]


def attend_inner(x, ga, weights):
    sources, outs, out_shapes, scratch, cost = attend_specs(INNER, 0)
    return call(
        inner_kernel, "attend_inner", (3,),
        [blocks(BLOCK, D)] + sources,
        outs, out_shapes, scratch, cost, 14,
    )(x, ga, *weights[:2])


def apart_matrix():
    late = np.arange(WIN) >= HALF
    return np.tile(np.where(late[:, None] != late[None, :], FAR, 0.0).astype(np.float32), (1, 4))


def attend_edge(parts, ga, flag, weights, carried):
    sources, outs, out_shapes, scratch, cost = attend_specs(5 * BLOCK, 3)
    return call(
        edge_kernel, "attend_edge", (5,),
        [pl.BlockSpec(memory_space=pltpu.SMEM)]
        + EDGE_SPECS
        + [whole(BLOCK, 4 * SMALL), whole(WIN, 4 * WIN)]
        + sources
        + [pl.BlockSpec(memory_space=pl.ANY)] * 3,
        outs, out_shapes, scratch + [pltpu.VMEM((BLOCK, D), F32), pltpu.VMEM((WIN, 4 * WIN), F32)], cost, 16,
        aliases={10 + n: n for n in range(3)},
    )(flag, *parts, jnp.asarray(CORNER_JOIN, BF16), jnp.asarray(apart_matrix()), ga, *weights[:2], *carried)


def weight_kernel(core_ref, left_ref, dp_ref, cot_ref, own_ref, away_ref, turned):
    for c in range(4):
        right = dp_ref[:, c * D : c * D + D] if c < 3 else cot_ref[...]
        chunk = product(left_ref[:, c // 3 * D : c // 3 * D + D], right, TN).reshape(64, 8, D)
        half = c % 2 * 4
        turned[:, 0, c // 2, half : half + 4] = chunk[:, :4]
        turned[:, 1, c // 2, half : half + 4] = chunk[:, 4:]
    core = core_ref[0]
    for at in range(BANDS // 2):
        for ref, which in ((own_ref, core), (away_ref, 1 - core)):
            part = turned[pl.ds(at * 8 + which * 4, 4)].reshape(128, D)
            ref[at * 128 : at * 128 + 128, :] = part.astype(ref.dtype)


def weight_terms(core, left, dp, cot):
    return call(
        weight_kernel, "weight_terms", (),
        [pl.BlockSpec(memory_space=pltpu.SMEM), whole(TOKENS, 2 * D), whole(TOKENS, 3 * D), whole(TOKENS, D)],
        [whole(1024, D)] * 2,
        [jax.ShapeDtypeStruct((1024, D), F32), jax.ShapeDtypeStruct((1024, D), BF16)],
        [pltpu.VMEM((64, 2, 2, 8, D), F32)],
        (1000, 1000, 0), 14,
    )(core, left, dp, cot)


def add_kernel(own_ref, got_ref, out_ref):
    out_ref[...] = (own_ref[...] + got_ref[...].astype(F32)).astype(BF16)


def add_halves(own, got):
    return call(
        add_kernel, "add_halves", (4,),
        [blocks(256, D)] * 2, blocks(256, D), shapes((1024, D))[0], [],
        (1000000, 4000000, 0), 6,
    )(own, got)


def finished(x_ref, att_ref, dp_ref, c_ref, w_ref, gain_ref, ow_ref):
    x = x_ref[...].astype(F32)
    out = x + product(att_ref[...], ow_ref[...])
    normed, inverse = normalise(x)
    hidden = product(dp_ref[...], w_ref[...], NT) * gain_ref[...]
    hidden = (
        hidden
        - jnp.mean(hidden, -1, keepdims=True)
        - normed * jnp.mean(hidden * normed, -1, keepdims=True)
    )
    grad = c_ref[...].astype(F32) + inverse * hidden
    return out, grad


def grid_pieces(split_ref, values):
    first = jnp.concatenate([values[:HALF], values[WIN : WIN + HALF]]).astype(BF16)
    second = jnp.concatenate([values[HALF:WIN], values[WIN + HALF :]]).astype(BF16)
    return [product(split_ref[...], part, TN).astype(BF16) for part in (first, second)]


def finish_inner_kernel(split_ref, *refs):
    *refs, inner = refs
    for n, values in enumerate(finished(*refs)):
        first, second = grid_pieces(split_ref, values)
        inner[n, :WIN, :] = first
        inner[n, WIN:, :] = second


def finish_edge_kernel(back_ref, *refs):
    refs, (edge, up, side, corner) = refs[:7], refs[7:]
    step = pl.program_id(0)
    for n, values in enumerate(finished(*refs)):
        parts = product(back_ref[...], values.astype(BF16)).astype(BF16)
        edge[n] = parts[:WIN]
        up[n] = parts[WIN:BLOCK]

        @pl.when(step == 0)
        def _(n=n, parts=parts):
            side[n] = parts[WIN:BLOCK]

        @pl.when(step == 4)
        def _(n=n, parts=parts):
            side[n, :SMALL, :] = parts[WIN + SMALL : WIN + 2 * SMALL]
            corner[n] = parts[WIN + 2 * SMALL :]


PIECES = (INNER, EDGE, UP, SIDE, CORNER)


def finish_specs(skip):
    row = lambda width, col: pl.BlockSpec((BLOCK, width), lambda i: (i + skip, col))
    return [row(D, 0), row(D, 1), row(3 * D, 0), row(D, 0)] + [whole(*dim) for dim in WEIGHTS]


def finish_cost(rows):
    return rows * 2200000, rows * 9000, rows


def finish_inner(values, weights):
    return call(
        finish_inner_kernel, "finish_inner", (3,),
        [whole(WIN, WIN)] + finish_specs(0),
        pl.BlockSpec((2, BLOCK, D), lambda i: (0, i, 0)), shapes((2, INNER, D))[0], [],
        (1000, 1000, 0), 14,
    )(jnp.asarray(SPLIT, BF16), *values, *weights)


def finish_edge(values, weights):
    return call(
        finish_edge_kernel, "finish_edge", (5,),
        [pl.BlockSpec((None,) + BACK.shape[1:], lambda i: (i // 4, 0, 0))] + finish_specs(3),
        EDGE_PAIRS, shapes(*[(2, n, D) for n in PIECES[1:]]), [],
        finish_cost(5 * BLOCK), 16,
    )(jnp.asarray(BACK, BF16), *values, *weights)


def join_kernel(inner, edge, up, side, corner, *outs):
    run, stub = 48, 24

    def load(ref, n, at, count):
        return ref[n, at : at + count, :].astype(F32)

    for zone in range(3):

        @pl.when((pl.program_id(0) + 1) // 2 == zone)
        def _(zone=zone):
            for n, out_ref in enumerate(outs):
                if zone == 1:
                    half = pl.program_id(0) - 1
                    left = load(side, n, 0, WIN)
                    right = load(edge, n, 0, WIN)
                    left, right = (jnp.where(half == 0, v[:HALF], v[HALF:]) for v in (left, right))
                    full = []
                    for q in range(3):
                        at = pl.multiple_of(q * BLOCK + half * WIN, 16)
                        full.append(inner[n, pl.ds(at, WIN), :].astype(F32))
                elif zone == 0:
                    left, right = load(corner, n, 0, SMALL), load(up, n, 3 * WIN, SMALL)
                    full = [load(up, n, q * WIN, WIN) for q in range(3)]
                else:
                    left, right = load(side, n, WIN, SMALL), load(edge, n, 4 * WIN, SMALL)
                    full = [load(edge, n, WIN + q * WIN, WIN) for q in range(3)]
                for i in range(3):
                    parts = [left[i * stub : i * stub + stub]]
                    parts += [part[i * run : i * run + run] for part in full]
                    parts.append(right[i * stub : i * stub + stub])
                    strip = jnp.concatenate(parts)
                    out_ref[i] = strip.reshape(LON, LEV, D).astype(BF16)


def join(parts):
    spec = pl.BlockSpec((3, LON, LEV, D), lambda i: (i, 0, 0, 0))
    dim = (LAT, LON, LEV, D)
    return call(
        join_kernel, "join", (4,),
        [whole(2, n, D) for n in PIECES],
        [spec] * 2, shapes(*[dim] * 2), [],
        (60000000000, 9000000, 0), 16,
    )(*parts)


def sum_kernel(terms_ref, qkv_ref, out_ref):
    total = jnp.sum(terms_ref[...].astype(F32).reshape(DEVICES // 2, 16, D), 0)
    for c in range(3):
        qkv_ref[:, c * D : c * D + D] = total[4 * c : 4 * c + 4]
    out_ref[...] = total[12:]


def sum_terms(terms):
    return call(
        sum_kernel, "sum_terms", (),
        [whole(1024, D)], [whole(4, 3 * D), whole(4, D)],
        shapes((4, 3 * D), (4, D), dtype=F32), [], (2000000, 2200000, 0), 20,
    )(terms)


def shift_pairs(lat_step, lon_step):
    return [
        (a * SECTORS + b, (a + lat_step) % BANDS * SECTORS + (b + lon_step) % SECTORS)
        for a in range(BANDS)
        for b in range(SECTORS)
    ]


def exchange(parts, sign):
    steps = ((sign, 0), (0, sign), (sign, sign))
    return [lax.ppermute(part, BOTH, shift_pairs(*step)) for part, step in zip(parts, steps)]


def swap_blocks(values, axis, groups=None):
    return lax.all_to_all(
        values, axis, split_axis=0, concat_axis=0, axis_index_groups=groups, tiled=True
    )


SAME_CORE = [
    [a * SECTORS + b for a in range(core, BANDS, 2) for b in range(SECTORS)] for core in range(2)
]
OTHER_CORE = [(d, d ^ SECTORS) for d in range(DEVICES)]


def per_device(buffer, fetch_owner, fetch_slot, norm_gain, qkv_weight, out_weight, out_grad):
    weights = (qkv_weight, norm_gain.reshape(1, D), out_weight)
    lists, place, table = make_requests(fetch_owner.reshape(1, TOKENS), fetch_slot.reshape(1, TOKENS))
    lists = swap_blocks(lists, "lat")
    replies = swap_blocks(serve(lists, buffer).reshape(BANDS, CAP, D), "lat")
    replies = replies.reshape(BANDS * CAP, D)

    c_up, c_side, c_corner, c_inner, c_edge = sort_pieces(out_grad.reshape(TOKENS, D))
    c_parts = [c_edge] + exchange([c_up, c_side, c_corner], -1)
    cot, ga_inner = prepare_inner(c_inner, out_weight)
    cot, ga_edge = prepare_edge(c_parts, out_weight, cot)
    place = place.reshape(TOKENS)[ORDER].reshape(-1, 1)

    replies, ga_inner = lax.optimization_barrier((replies, ga_inner))
    x_up, x_side, x_corner, x_inner, x_edge = pick(table, place, replies)
    x_parts = [x_edge] + exchange([x_up, x_side, x_corner], -1)

    band = lax.axis_index("lat")
    flag = (band == BANDS - 1).astype(I32).reshape(1)
    core = (band % 2).astype(I32).reshape(1)
    first = attend_inner(x_inner, ga_inner, weights)
    x, left, dp = attend_edge(x_parts, ga_edge, flag, weights, first)
    edge, *away = finish_edge((x, left, dp, cot), weights)
    up, side, corner = exchange(away, 1)
    left, dp, edge = lax.optimization_barrier((left, dp, edge))
    own, away = weight_terms(core, left, dp, cot)
    got = lax.ppermute(away, BOTH, OTHER_CORE)
    inner = finish_inner((x, left, dp, cot), weights)
    got, inner = lax.optimization_barrier((got, inner))
    terms = swap_blocks(add_halves(own, got), BOTH, SAME_CORE)
    returned = [up, side, corner]
    outs = join([inner, edge] + returned)
    return (*outs, *sum_terms(terms))


def solution(mesh):
    return jax.shard_map(
        per_device,
        mesh=mesh,
        in_specs=(
            P(BOTH, None),
            P("lat", "lon", None, None),
            P("lat", "lon", None),
            P(),
            P(),
            P(),
            P("lat", "lon", None, None),
        ),
        out_specs=(
            P("lat", "lon", None, None),
            P("lat", "lon", None, None),
            P(BOTH, None),
            P(BOTH, None),
        ),
        check_vma=False,
    )
```
